32 devices in a mesh: replica: 4 (over y, x), fsdp: 8 (over z, core).
Axes of the slice: x: 2, y: 2, z: 4, core: 2. Of those that a mesh axis runs over, the one named last changes fastest.
Arguments:
- tokens: bfloat16 [6144, 2048], P(('replica', 'fsdp')), may hold values from -6 to 6
- segment: int32 [6144], P('replica'), may hold values from 0 to 4, as said below
- position: int32 [6144], P('replica'), may hold values from 0 to 1023, as said below
- attn_gain: bfloat16 [2048], P('fsdp'), may hold values from 0.5 to 1.5
- w_query: bfloat16 [2048, 2048], P('fsdp'), may hold values from -0.125 to 0.125
- w_key: bfloat16 [2048, 512], P('fsdp'), may hold values from -0.125 to 0.125
- w_value: bfloat16 [2048, 512], P('fsdp'), may hold values from -0.125 to 0.125
- w_out: bfloat16 [2048, 2048], P('fsdp'), may hold values from -1 to 1
- mlp_gain: bfloat16 [2048], P('fsdp'), may hold values from 0.5 to 1.5
- w_gate: bfloat16 [2048, 8192], P('fsdp'), may hold values from -0.125 to 0.125
- w_up: bfloat16 [2048, 8192], P('fsdp'), may hold values from -0.125 to 0.125
- w_down: bfloat16 [8192, 2048], P('fsdp'), may hold values from -0.0625 to 0.0625
- cotangent: bfloat16 [6144, 2048], P(('replica', 'fsdp')), may hold values from -6 to 6
Outputs:
- output: bfloat16 [6144, 2048], P(('replica', 'fsdp'))
- grad_tokens: float32 [6144, 2048], P(('replica', 'fsdp'))
- grad_attn_gain: float32 [2048], P('fsdp')
- grad_w_query: float32 [2048, 2048], P('fsdp')
- grad_w_key: float32 [2048, 512], P('fsdp')
- grad_w_value: float32 [2048, 512], P('fsdp')
- grad_w_out: float32 [2048, 2048], P('fsdp')
- grad_mlp_gain: float32 [2048], P('fsdp')
- grad_w_gate: float32 [2048, 8192], P('fsdp')
- grad_w_up: float32 [2048, 8192], P('fsdp')
- grad_w_down: float32 [8192, 2048], P('fsdp')
The draws below stay inside these ranges and needn't reach their ends.
Inputs may be any that keep to these rules, and one draw needn't show every extreme that they name: Within each group of 1536 consecutive tokens the tokens with one segment number form one sequence; numbers of different groups are unrelated. Each group holds one sequence of exactly 1024 tokens and none longer. `position`: the positions of one sequence are 0 to its length minus 1, each once.
All inputs are finite; a program needn't handle non-finite values.
Results may differ from the reference program's by a relative error of at most 0.023.
Values may be sent and summed in bfloat16 or wider, within the bound.
A program may use at most 640 MiB of HBM per device.

```python
import math
import jax
import jax.numpy as jnp
from jax import lax

D = 2048
H = 32
KVH = 8
HD = 64
FF = 8192
TOK_DEV = 192
NCUT = 3
SHARE = 4
QW = 2048
KVW = 512
GROUP = 1536
TOKENS = 6144
MAXLEN = 1024
N_REPLICA = 4
N_FSDP = 8


def layout(key):
    long_slots = MAXLEN // N_FSDP
    rest_len = GROUP - MAXLEN

    def one_group(group_key):
        sub_keys = jax.random.split(group_key, N_FSDP + 1)
        slot_order = jax.vmap(lambda sub_key: jax.random.permutation(sub_key, TOK_DEV))(sub_keys[:N_FSDP]).astype(jnp.int32)
        cut_points = (jax.random.permutation(sub_keys[N_FSDP], rest_len - 1)[:NCUT] + 1).astype(jnp.int32)
        device_ids = jnp.arange(N_FSDP, dtype=jnp.int32)[:, None]
        long_pos = slot_order * N_FSDP + device_ids
        packed = jnp.maximum(device_ids * (TOK_DEV - long_slots) + slot_order - long_slots, 0)
        passed = cut_points[None, None, :] <= packed[:, :, None]
        cut_count = jnp.sum(passed.astype(jnp.int32), -1)
        last_cut = jnp.max(jnp.where(passed, cut_points[None, None, :], 0), -1)
        seq_start = jnp.maximum(last_cut, packed // MAXLEN * MAXLEN)
        is_long = slot_order < long_slots
        segment_ids = jnp.where(is_long, 0, 1 + cut_count + packed // MAXLEN)
        position_ids = jnp.where(is_long, long_pos, packed - seq_start)
        return (segment_ids.reshape(GROUP).astype(jnp.int32), position_ids.reshape(GROUP).astype(jnp.int32))
    segment_ids, position_ids = jax.vmap(one_group)(jax.random.split(key, N_REPLICA))
    return (segment_ids.reshape(TOKENS), position_ids.reshape(TOKENS))


def draw_segment(key, part=0):
    shared = layout(key)
    return shared[0]


def draw_position(key, part=0):
    shared = layout(key)
    return shared[1]


def steps_of(rng, shape, cuts, least, largest):
    gain, own = 1.0, jax.random.fold_in(rng, 6)
    for axis_at, shards_of in cuts:
        steps = jnp.exp(jax.random.uniform(jax.random.fold_in(own, axis_at), (shards_of,), jnp.float32, least / len(cuts), largest / len(cuts)))
        gain = gain * jnp.repeat(steps, shape[axis_at] // shards_of).reshape([-1 if axis == axis_at else 1 for axis in range(len(shape))])
    return gain


def gaussian(stream_key, extent, width, limit, cuts=(), kind=jnp.bfloat16):
    drawn = jax.random.normal(stream_key, extent, jnp.float32) * width
    if len(cuts) > 0:
        drawn = steps_of(stream_key, extent, cuts, -0.22, 0.18) * drawn
    return jnp.clip(drawn, min=-limit, max=limit).astype(kind)


def setup_inputs(seed: int = 0) -> dict:
    key_list = jax.random.split(jax.random.key(seed), 14)
    return {
        "tokens": gaussian(key_list[0], (TOKENS, D), 1.0, 6.0, ((0, 32),)),
        "segment": draw_segment(jax.random.fold_in(key_list[13], 71), 0),
        "position": draw_position(jax.random.fold_in(key_list[13], 71), 0),
        "attn_gain": jnp.clip(1.0 + 0.1 * jax.random.normal(key_list[3], (D,), jnp.float32), 0.5, 1.5).astype(jnp.bfloat16),
        "w_query": gaussian(key_list[4], (D, QW), D ** -0.5, 0.125, ((0, 8),)),
        "w_key": gaussian(key_list[5], (D, KVW), D ** -0.5, 0.125, ((0, 8),)),
        "w_value": gaussian(key_list[6], (D, KVW), D ** -0.5, 0.125, ((0, 8),)),
        "w_out": gaussian(key_list[7], (QW, D), (QW // 64) ** -0.5, 1.0, ((0, 8),)),
        "mlp_gain": jnp.clip(1.0 + 0.1 * jax.random.normal(key_list[8], (D,), jnp.float32), 0.5, 1.5).astype(jnp.bfloat16),
        "w_gate": gaussian(key_list[9], (D, FF), D ** -0.5, 0.125, ((0, 8),)),
        "w_up": gaussian(key_list[10], (D, FF), D ** -0.5, 0.125, ((0, 8),)),
        "w_down": gaussian(key_list[11], (FF, D), FF ** -0.5, 0.0625, ((0, 8),)),
        "cotangent": gaussian(key_list[12], (TOKENS, D), 1.0, 6.0, ((0, 32),)),
    }


@jax.custom_vjp
def low(v):
    return lax.optimization_barrier(v.astype(jnp.bfloat16)).astype(jnp.float32)

@jax.custom_vjp
def low_back(v):
    return v

def low_keep(v):
    return (low(v), None)

def low_pass(kept, grad):
    return (grad,)

def back_keep(v):
    return (v, None)

def back_low(kept, grad):
    return (low(grad),)
low.defvjp(low_keep, low_pass)
low_back.defvjp(back_keep, back_low)
EPSILON = 1e-05
ROPE_BASE = 500000.0
MASKED_VALUE = -1e+30
PRECISE = lax.Precision.HIGHEST

def matmul_hi(first_op, second_op):
    return jnp.dot(first_op, second_op, precision=PRECISE)

def rotate(values, cos_tab, sin_tab):
    half_dim = values.shape[-1] // 2
    front_half = values[..., :half_dim]
    back_half = values[..., half_dim:]
    return jnp.concatenate([front_half * cos_tab - back_half * sin_tab, back_half * cos_tab + front_half * sin_tab], -1)

def rms_scale(resid_in):
    return lax.rsqrt(lax.optimization_barrier(jnp.mean(resid_in * resid_in, -1, keepdims=True)) + EPSILON)

def group_layer(resid_in, seg_ids, pos_ids, weights):
    gain_attn, query_w, key_w, value_w, out_w, gain_mlp, gate_w, up_w, down_w = weights
    frequencies = jnp.exp(-math.log(ROPE_BASE) * jnp.arange(HD // 2, dtype=jnp.float32) * (2.0 / HD))
    angles = pos_ids.astype(jnp.float32)[:, None] * frequencies[None, :]
    cos_tab = jnp.cos(angles)[:, None, :]
    sin_tab = jnp.sin(angles)[:, None, :]
    normed_attn = low(resid_in * rms_scale(resid_in) * gain_attn)
    queries = low(rotate(low_back(matmul_hi(normed_attn, query_w)).reshape(GROUP, H, HD), cos_tab, sin_tab))
    queries = queries.reshape(GROUP, KVH, SHARE, HD)
    key_vals = low(rotate(low_back(matmul_hi(normed_attn, key_w)).reshape(GROUP, KVH, HD), cos_tab, sin_tab))
    value_vals = low_back(low(matmul_hi(normed_attn, value_w))).reshape(GROUP, KVH, HD)
    q_block = math.gcd(GROUP, 512)
    num_blocks = GROUP // q_block

    def attend(query_item):
        query_blk, seg_blk, pos_blk = query_item
        logits = jnp.einsum('qhgd,khd->hgqk', query_blk, key_vals, precision=PRECISE) * 0.125
        logits = low_back(logits)
        visible = (seg_blk[:, None] == seg_ids[None, :]) & (pos_ids[None, :] <= pos_blk[:, None])
        logits = jnp.where(visible, logits, MASKED_VALUE)
        row_max = lax.optimization_barrier(jnp.max(logits, -1, keepdims=True))
        exp_terms = jnp.where(visible, jnp.exp(logits - row_max), 0.0)
        probs_low = low(exp_terms / lax.optimization_barrier(jnp.sum(exp_terms, -1, keepdims=True)))
        return jnp.einsum('hgqk,khd->qhgd', probs_low, value_vals, precision=PRECISE).reshape(q_block, QW)
    attended = lax.map(jax.checkpoint(attend), (queries.reshape(num_blocks, q_block, KVH, SHARE, HD), seg_ids.reshape(num_blocks, q_block), pos_ids.reshape(num_blocks, q_block)))
    attended = low_back(low(attended.reshape(GROUP, QW)))
    middle = resid_in + low_back(matmul_hi(attended, out_w))
    normed_mlp = low(middle * rms_scale(middle) * gain_mlp)
    gate_act = low_back(matmul_hi(normed_mlp, gate_w))
    up_act = low_back(matmul_hi(normed_mlp, up_w))
    hidden = low(jax.nn.silu(gate_act) * up_act)
    return middle + low_back(matmul_hi(hidden, down_w))

def reference(tokens, segment, position, attn_gain, w_query, w_key, w_value, w_out, mlp_gain, w_gate, w_up, w_down, cotangent):
    seg_groups = segment.reshape(N_REPLICA, GROUP)
    pos_groups = position.reshape(N_REPLICA, GROUP)

    def forward(resid_all, gain_attn, query_w, key_w, value_w, out_w, gain_mlp, gate_w, up_w, down_w):
        weights = (gain_attn, query_w, key_w, value_w, out_w, gain_mlp, gate_w, up_w, down_w)

        def one_group(group_item):
            return group_layer(group_item[0], group_item[1], group_item[2], weights)
        layered = lax.map(jax.checkpoint(one_group), (resid_all.reshape(N_REPLICA, GROUP, D), seg_groups, pos_groups))
        return layered.reshape(TOKENS, D)
    result, pullback = jax.vjp(forward, tokens.astype(jnp.float32), attn_gain.astype(jnp.float32), w_query.astype(jnp.float32), w_key.astype(jnp.float32), w_value.astype(jnp.float32), w_out.astype(jnp.float32), mlp_gain.astype(jnp.float32), w_gate.astype(jnp.float32), w_up.astype(jnp.float32), w_down.astype(jnp.float32))
    gradients = pullback(cotangent.astype(jnp.float32))
    return (result.astype(jnp.bfloat16), gradients[0], gradients[1], gradients[2], gradients[3], gradients[4], gradients[5], gradients[6], gradients[7], gradients[8], gradients[9])
```

```python
import math

import jax
import jax.numpy as jnp
from jax import lax
from jax.sharding import PartitionSpec as P

H = 32
KVH = 8
HD = 64
EPSILON = 1e-05
ROPE_BASE = 500000.0
MASKED = -1e30
F32 = jnp.float32
BF16 = jnp.bfloat16


def rotate(values, cos_tab, sin_tab):
    half = values.shape[-1] // 2
    front, back = values[..., :half], values[..., half:]
    return jnp.concatenate([front * cos_tab - back * sin_tab, back * cos_tab + front * sin_tab], -1)


def dot(a, b):
    return jnp.dot(a, b, preferred_element_type=F32)


def tdot(a, b):
    return lax.dot_general(a, b, (((0,), (0,)), ((), ())), preferred_element_type=F32)


def dot_t(a, b):
    return lax.dot_general(a, b, (((1,), (1,)), ((), ())), preferred_element_type=F32)


def norm_back(grad_normed, unit, inverse, gain):
    scaled = grad_normed * gain
    return inverse * (scaled - unit * jnp.mean(scaled * unit, -1, keepdims=True))


def attention_plan(group_len, long_len):
    block = 256
    plan = [(i, block, 0, i + block) for i in range(0, long_len, block)]
    plan += [(i, block, long_len, i + block - long_len) for i in range(long_len, group_len, block)]
    return plan


def block_mask(item, seg_sorted, long_len):
    q0, qn, k0, kn = item
    rows = q0 + lax.broadcasted_iota(jnp.int32, (qn, kn), 0)
    cols = k0 + lax.broadcasted_iota(jnp.int32, (qn, kn), 1)
    visible = cols <= rows
    if q0 >= long_len:
        visible &= seg_sorted[q0 : q0 + qn, None] == seg_sorted[None, k0 : k0 + kn]
    return visible


def attention_forward(q, k, v, seg_sorted, long_len):
    outs, maxes, totals = [], [], []
    for item in attention_plan(q.shape[0], long_len):
        q0, qn, k0, kn = item
        visible = block_mask(item, seg_sorted, long_len)
        logits = jnp.einsum("qhd,kd->hqk", q[q0 : q0 + qn], k[k0 : k0 + kn], preferred_element_type=F32) * 0.125
        logits = jnp.where(visible, logits, MASKED)
        top = jnp.max(logits, -1, keepdims=True)
        terms = jnp.exp(logits - top)
        total = jnp.sum(terms, -1, keepdims=True)
        probs = (terms / total).astype(BF16)
        outs.append(jnp.einsum("hqk,kd->qhd", probs, v[k0 : k0 + kn], preferred_element_type=F32))
        maxes.append(top)
        totals.append(total)
    return jnp.concatenate(outs, 0), maxes, totals


def attention_backward(q, k, v, grad_out, attended, maxes, totals, seg_sorted, long_len):
    group_len = q.shape[0]
    grad_k = jnp.zeros((group_len, HD), F32)
    grad_v = jnp.zeros((group_len, HD), F32)
    grad_q = []
    for item, top, total in zip(attention_plan(group_len, long_len), maxes, totals):
        q0, qn, k0, kn = item
        visible = block_mask(item, seg_sorted, long_len)
        qb, kb, vb, gb = q[q0 : q0 + qn], k[k0 : k0 + kn], v[k0 : k0 + kn], grad_out[q0 : q0 + qn]
        centre = jnp.sum(gb.astype(F32) * attended[q0 : q0 + qn], -1).T[..., None]
        logits = jnp.einsum("qhd,kd->hqk", qb, kb, preferred_element_type=F32) * 0.125
        probs = jnp.exp(jnp.where(visible, logits, MASKED) - top) / total
        grad_probs = jnp.einsum("qhd,kd->hqk", gb, vb, preferred_element_type=F32)
        grad_logits = (probs * (grad_probs - centre)).astype(BF16)
        grad_q.append(jnp.einsum("hqk,kd->qhd", grad_logits, kb, preferred_element_type=F32) * 0.125)
        part_k = jnp.einsum("hqk,qhd->kd", grad_logits, qb, preferred_element_type=F32) * 0.125
        part_v = jnp.einsum("hqk,qhd->kd", probs.astype(BF16), gb, preferred_element_type=F32)
        grad_k = grad_k.at[k0 : k0 + kn].add(part_k)
        grad_v = grad_v.at[k0 : k0 + kn].add(part_v)
    return jnp.concatenate(grad_q, 0), grad_k, grad_v


def body(
    tokens, segment, position, attn_gain, w_query, w_key, w_value, w_out, mlp_gain, w_gate, w_up, w_down, cotangent
):
    rows, width = tokens.shape
    group_len = segment.shape[0]
    long_len = group_len * 2 // 3
    n = lax.axis_size("fsdp")
    reps = lax.axis_size("replica")
    replica = lax.axis_index("replica")
    shard = lax.axis_index("fsdp")
    w_rows = w_query.shape[0]
    ff = w_gate.shape[1]
    ff_own = ff // n
    ff_blk = ff_own // reps
    q_heads = H // n
    q_cols = q_heads * HD
    dup = n // KVH

    def gather(x):
        return lax.all_gather(x, "fsdp", axis=0, tiled=True)

    def swap(x):
        return lax.all_to_all(x, "fsdp", 0, 0, tiled=True)

    def by_dest(x):
        return x.reshape(x.shape[0], n, -1).transpose(1, 0, 2)

    tokens_all = gather(tokens)
    gains = gather(jnp.stack([attn_gain, mlp_gain], 1)).astype(F32)
    gain_a, gain_m = gains[:, 0], gains[:, 1]

    kv_w = jnp.concatenate([w_key.reshape(w_rows, KVH, HD), w_value.reshape(w_rows, KVH, HD)], -1)
    kv_w = jnp.repeat(kv_w, dup, axis=1)
    qkv_w = swap(jnp.concatenate([w_query.reshape(w_rows, n, q_cols), kv_w], -1).transpose(1, 0, 2))
    qkv_w = qkv_w.reshape(width, q_cols + 2 * HD)
    gate_up = jnp.stack([w_gate.reshape(w_rows, n, reps, ff_blk), w_up.reshape(w_rows, n, reps, ff_blk)])
    gate_up = lax.dynamic_index_in_dim(gate_up, replica, 3, keepdims=False)
    gate_up = swap(gate_up.transpose(2, 0, 1, 3)).transpose(1, 0, 2, 3).reshape(2, width, ff_blk)
    gate_up = lax.all_gather(gate_up, "replica", axis=0, tiled=False)
    gate_w, up_w = gate_up[:, 0], gate_up[:, 1]
    cot_all = gather(cotangent)

    same = jnp.sum((segment[:, None] == segment[None, :]).astype(jnp.int32), 1)
    key = jnp.where(same == long_len, -1, segment) * group_len + position
    rank = jnp.sum((key[None, :] < key[:, None]).astype(jnp.int32), 1)
    places = lax.iota(jnp.int32, group_len)
    onehot = rank[None, :] == places[:, None]
    sorter = onehot.astype(BF16)
    seg_sorted = jnp.sum(jnp.where(onehot, segment[None, :], 0), 1)
    pos_sorted = jnp.sum(jnp.where(onehot, position[None, :], 0), 1)

    freqs = jnp.exp(-math.log(ROPE_BASE) * jnp.arange(HD // 2, dtype=F32) * (2.0 / HD))

    def tables(pos):
        angles = pos.astype(F32)[:, None] * freqs[None, :]
        return jnp.cos(angles)[:, None, :], jnp.sin(angles)[:, None, :]

    def normed(resid, gain):
        inverse = lax.rsqrt(jnp.mean(resid * resid, -1, keepdims=True) + EPSILON)
        unit = resid * inverse
        return inverse, unit, (unit * gain).astype(BF16)

    normed_all = normed(tokens_all.astype(F32), gain_a)[2]
    resid = tokens.astype(F32)
    inv_attn, unit_attn, _ = normed(resid, gain_a)
    cos_tab, sin_tab = tables(position)
    qkv = dot(normed_all, qkv_w)
    queries = rotate(qkv[:, :q_cols].reshape(group_len, q_heads, HD), cos_tab, sin_tab)
    keys = rotate(qkv[:, None, q_cols : q_cols + HD], cos_tab, sin_tab)
    qkv = jnp.concatenate(
        [queries.reshape(group_len, q_cols), keys.reshape(group_len, HD), qkv[:, q_cols + HD :]], 1
    ).astype(BF16)
    qkv = dot(sorter, qkv).astype(BF16)
    queries = qkv[:, :q_cols].reshape(group_len, q_heads, HD)
    keys = qkv[:, q_cols : q_cols + HD]
    values = qkv[:, q_cols + HD :]
    attended, maxes, totals = attention_forward(queries, keys, values, seg_sorted, long_len)
    attended_tp = tdot(sorter, attended.reshape(group_len, q_cols).astype(BF16)).astype(BF16)

    own = jnp.concatenate([w_out, w_query, w_key, w_value], 1)
    own_cols = own.shape[1]
    part = lax.dynamic_slice_in_dim(own, replica * (own_cols // reps), own_cols // reps, 1)
    whole_w = lax.all_gather(gather(part), "replica", axis=1, tiled=True)
    out_w, query_w = whole_w[:, :width], whole_w[:, width:]

    attended_low = swap(attended_tp.reshape(n, rows, q_cols)).transpose(1, 0, 2).reshape(rows, H * HD)
    middle = resid + dot(attended_low, out_w)
    inv_mlp, unit_mlp, normed_mlp = normed(middle, gain_m)
    normed_mlp_all = gather(normed_mlp)

    def blocks(x, w):
        return jnp.einsum("sd,bdc->bsc", x, w, preferred_element_type=F32)

    gate_act = blocks(normed_mlp_all, gate_w)
    up_act = blocks(normed_mlp_all, up_w)
    down_w = w_down.reshape(reps, ff_blk, width)
    grad_hidden = jnp.einsum("sd,bcd->bsc", cot_all, down_w, preferred_element_type=F32)
    sig = jax.nn.sigmoid(gate_act)
    hidden = (gate_act * sig * up_act).astype(BF16)
    grad_gate = (grad_hidden * up_act * sig * (1.0 + gate_act * (1.0 - sig))).astype(BF16)
    grad_up = (grad_hidden * gate_act * sig).astype(BF16)

    grad_normed = jnp.einsum("bsc,bdc->sd", grad_gate, gate_w, preferred_element_type=F32) + jnp.einsum(
        "bsc,bdc->sd", grad_up, up_w, preferred_element_type=F32
    )
    grad_normed_mlp = lax.psum_scatter(
        grad_normed.astype(BF16), "fsdp", scatter_dimension=0, tiled=True
    ).astype(F32)
    down = jnp.einsum("bsc,bcd->sd", hidden, down_w, preferred_element_type=F32)
    down = lax.psum_scatter(down.astype(BF16), "fsdp", scatter_dimension=0, tiled=True)
    output = (middle + down.astype(F32)).astype(BF16)

    grad_down = jnp.einsum("bsc,sd->bcd", hidden, cot_all, preferred_element_type=F32)
    grad_down = lax.psum(grad_down.astype(BF16).reshape(ff_own, width), "replica").astype(F32)

    def by_rows(grad):
        grad = lax.psum_scatter(grad.astype(BF16), "replica", scatter_dimension=0, tiled=True)
        grad = swap(grad.reshape(n, w_rows, -1))
        grad = lax.all_gather(grad, "replica", axis=0, tiled=False)
        return grad.transpose(2, 1, 0, 3).reshape(w_rows, -1).astype(F32)

    grad_w_gate = by_rows(jnp.einsum("sd,bsc->bdc", normed_mlp_all, grad_gate, preferred_element_type=F32))
    grad_w_up = by_rows(jnp.einsum("sd,bsc->bdc", normed_mlp_all, grad_up, preferred_element_type=F32))

    gain_term_mlp = jnp.sum(grad_normed_mlp * unit_mlp, 0)
    grad_middle = cotangent.astype(F32) + norm_back(grad_normed_mlp, unit_mlp, inv_mlp, gain_m)
    grad_middle_low = grad_middle.astype(BF16)
    grad_att = dot_t(grad_middle_low, out_w).astype(BF16)
    grad_att = swap(by_dest(grad_att)).reshape(group_len, q_cols)
    grad_middle_all = gather(grad_middle_low)
    grad_w_out = lax.psum(tdot(attended_tp, grad_middle_all).astype(BF16), "replica").astype(F32)
    grad_att = dot(sorter, grad_att).astype(BF16).reshape(group_len, q_heads, HD)
    grad_q, grad_k, grad_v = attention_backward(
        queries, keys, values, grad_att, attended, maxes, totals, seg_sorted, long_len
    )
    cos_tab, sin_tab = tables(pos_sorted)
    grad_q = rotate(grad_q, cos_tab, -sin_tab).reshape(group_len, q_cols)
    grad_k = rotate(grad_k[:, None, :], cos_tab, -sin_tab).reshape(group_len, HD)
    grad_qkv = jnp.concatenate([grad_q, grad_k, grad_v], 1).astype(BF16)
    grad_qkv = tdot(sorter, grad_qkv).astype(BF16)

    def split_qkv(x):
        lead = x.shape[0]
        kv = x[:, :, q_cols:].astype(F32).reshape(lead, KVH, dup, 2 * HD).sum(2).astype(x.dtype)
        return x[:, :, :q_cols].reshape(lead, H * HD), kv[:, :, :HD].reshape(lead, -1), kv[:, :, HD:].reshape(lead, -1)

    own_grads = swap(grad_qkv.reshape(n, rows, -1)).transpose(1, 0, 2)
    own_grads = jnp.concatenate(split_qkv(own_grads), 1)
    grad_normed_attn = dot_t(own_grads, query_w)
    gain_term_attn = jnp.sum(grad_normed_attn * unit_attn, 0)
    grad_tokens = grad_middle + norm_back(grad_normed_attn, unit_attn, inv_attn, gain_a)

    grad_w = tdot(normed_all, grad_qkv).astype(BF16)
    grad_w = grad_w.reshape(n, reps, w_rows // reps, -1).transpose(1, 0, 2, 3)
    grad_w = lax.psum_scatter(grad_w, "replica", scatter_dimension=0, tiled=True)[0]
    grad_w = lax.all_gather(swap(grad_w), "replica", axis=0, tiled=False)
    grad_w = grad_w.transpose(0, 2, 1, 3).reshape(w_rows, n, -1).astype(F32)
    grad_w_query, grad_w_key, grad_w_value = split_qkv(grad_w)

    gain_sums = lax.psum(jnp.stack([gain_term_attn, gain_term_mlp]), ("replica", "fsdp"))
    gain_own = lax.dynamic_slice_in_dim(gain_sums, shard * w_rows, w_rows, 1)
    return (
        output,
        grad_tokens,
        gain_own[0],
        grad_w_query,
        grad_w_key,
        grad_w_value,
        grad_w_out,
        gain_own[1],
        grad_w_gate,
        grad_w_up,
        grad_down,
    )


def solution(mesh):
    both = P(("replica", "fsdp"), None)
    mat = P("fsdp", None)
    vec = P("fsdp")
    return jax.shard_map(
        body,
        mesh=mesh,
        in_specs=(both, P("replica"), P("replica"), vec, mat, mat, mat, mat, vec, mat, mat, mat, both),
        out_specs=(both, both, vec, mat, mat, mat, mat, vec, mat, mat, mat),
        check_vma=False,
    )
```

```python
import functools
import math

import jax
import jax.numpy as jnp
from jax import lax
from jax.experimental import pallas as pl
from jax.experimental.pallas import tpu as pltpu
from jax.sharding import PartitionSpec as P

H = 32
KVH = 8
HD = 64
EPSILON = 1e-05
ROPE_BASE = 500000.0
MASKED = -1e30
QBLK = 256
F32 = jnp.float32
BF16 = jnp.bfloat16
MESH = pl.DeviceIdType.MESH
VMEM = pl.BlockSpec(memory_space=pltpu.VMEM)
ANY = pl.BlockSpec(memory_space=pl.ANY)
DMA = pltpu.SemaphoreType.DMA
VMEM_BYTES = 60 * 2**20


def dot(a, b):
    return jnp.dot(a, b, preferred_element_type=F32)


def tdot(a, b):
    return lax.dot_general(a, b, (((0,), (0,)), ((), ())), preferred_element_type=F32)


def dot_t(a, b):
    return lax.dot_general(a, b, (((1,), (1,)), ((), ())), preferred_element_type=F32)


class Line:
    def __init__(self, n):
        f = lax.axis_index("fsdp")
        self.n = n
        self.replica = lax.axis_index("replica")
        self.chips = n // 2
        self.z = lax.div(f, 2)
        self.c = lax.rem(f, 2)
        self.me = f
        x, y = lax.rem(self.replica, 2), lax.div(self.replica, 2)
        self.xn, self.yn = self.replica + 1 - 2 * x, self.replica + 2 - 4 * y
        self.diag = 3 - self.replica

    def dev(self, z, c):
        return (self.replica, 2 * z + c)

    def other(self, i):
        return lax.rem(self.me + i, self.n)

    def enter(self, square=False):
        barrier = pltpu.get_barrier_semaphore()
        z, c = self.z, self.c

        def greet(device):
            pl.semaphore_signal(barrier, inc=1, device_id=device, device_id_type=MESH)

        greet(self.dev(z, 1 - c))

        @pl.when(z > 0)
        def _():
            greet(self.dev(z - 1, c))

        @pl.when(z < self.chips - 1)
        def _():
            greet(self.dev(z + 1, c))

        count = 1 + (z > 0).astype(jnp.int32) + (z < self.chips - 1).astype(jnp.int32)
        if square:
            greet((self.xn, self.me))
            greet((self.yn, self.me))
            count = count + 2
        pl.semaphore_wait(barrier, count)

    def enter_all(self, reps, square=False):
        barrier = pltpu.get_barrier_semaphore()

        def greet(device):
            pl.semaphore_signal(barrier, inc=1, device_id=device, device_id_type=MESH)

        for i in range(1, self.n):
            greet((self.replica, self.other(i)))
        if square:
            greet((self.xn, self.me))
            greet((self.yn, self.me))
        else:
            for i in range(1, reps):
                greet((lax.rem(self.replica + i, reps), self.me))
        pl.semaphore_wait(barrier, self.n - 1 + (2 if square else reps - 1))

    def far_first(self, s):
        z, last = self.z, self.chips - 1
        right = last - z
        low = jnp.where(s < right, last - s, s - right)
        high = jnp.where(s < z, s, last - (s - z))
        return jnp.where(2 * z < self.chips, low, high)

    def near_first(self, j):
        z, last = self.z, self.chips - 1
        short = jnp.minimum(z, last - z)
        half = lax.div(j + 1, 2)
        both = jnp.where(lax.rem(j, 2) == 1, z - half, z + half)
        rest = jnp.where(2 * z < self.chips, j, last - j)
        return jnp.where(j <= 2 * short, both, rest)


def remote(src, dst, send, recv, device):
    return pltpu.make_async_remote_copy(
        src_ref=src, dst_ref=dst, send_sem=send, recv_sem=recv, device_id=device, device_id_type=MESH
    )


def row_step(rows):
    return 32 if rows % 32 == 0 else 16


def row_chunks(rows, fn):
    step = row_step(rows)

    @pl.loop(0, rows // step)
    def _(i):
        fn(pl.ds(pl.multiple_of(i * step, step), step))


PARTS = 2


class Scatter:
    @staticmethod
    def scratch(n, rows, width):
        chips = n // 2
        return [
            pltpu.VMEM((chips, 2, rows, width), BF16),
            pltpu.VMEM((chips, rows, width), BF16),
            pltpu.VMEM((chips + 1, rows, width), BF16),
            pltpu.VMEM((rows, width), F32),
            DMA((chips,)),
            DMA((chips,)),
            DMA((chips, PARTS)),
            DMA((chips + 1, PARTS)),
        ]

    def __init__(self, line, scratch):
        self.line = line
        self.part, self.sib, self.rx, self.total = scratch[:4]
        self.sib_send, self.sib_recv, self.line_send, self.line_recv = scratch[4:]
        self.rows, self.width = self.total.shape
        self.rows_q = self.rows // PARTS

    def to_sibling(self, d):
        line = self.line
        return remote(
            self.part.at[d, 1 - line.c], self.sib.at[d], self.sib_send.at[d], self.sib_recv.at[d], line.dev(line.z, 1 - line.c)
        )

    def along(self, d, slot, q, z):
        c = self.line.c
        at = pl.ds(q * self.rows_q, self.rows_q)
        return remote(
            self.part.at[d, c, at], self.rx.at[slot, at], self.line_send.at[d, q], self.line_recv.at[slot, q], self.line.dev(z, c)
        )

    def to_right(self, d, q):
        return self.along(d, d, q, self.line.z + 1)

    def to_left(self, d, q):
        z = self.line.z
        return self.along(d, jnp.where(d == z - 1, self.line.chips, d), q, z - 1)

    def wait_line(self, slot, q):
        line = self.line
        at = pl.ds(q * self.rows_q, self.rows_q)
        here = self.rx.at[slot, at]
        remote(here, here, self.line_send.at[0, q], self.line_recv.at[slot, q], line.dev(line.z, 1 - line.c)).wait_recv()

    def add(self, d, q, with_line):
        step = row_step(self.rows_q)
        c = self.line.c

        @pl.loop(0, self.rows_q // step)
        def _(i):
            at = pl.ds(pl.multiple_of(q * self.rows_q + i * step, step), step)
            value = self.part[d, c, at, :].astype(F32) + self.sib[d, at, :].astype(F32)
            if with_line:
                value = value + self.rx[d, at, :].astype(F32)
            self.part[d, c, at, :] = value.astype(BF16)

    def produce(self, compute):
        line = self.line
        chips, z = line.chips, line.z

        @pl.loop(0, chips)
        def _(s):
            d = line.far_first(s)
            compute(d)
            self.to_sibling(d).start()

            @pl.when(((z == 0) | (z == chips - 1)) & (s > 0))
            def _():
                before = line.far_first(s - 1)
                self.to_sibling(before).wait_recv()
                for q in range(PARTS):
                    self.add(before, q, False)

                    @pl.when(z == 0)
                    def _():
                        self.to_right(before, q).start()

                    @pl.when(z > 0)
                    def _():
                        self.to_left(before, q).start()

    def duty(self, s):
        chips, z, c = self.line.chips, self.line.z, self.line.c
        for near in (True, False):
            right = (2 * z < chips) if near else (2 * z >= chips)
            d = jnp.where(right, chips - 1 - s, s)
            active = jnp.where(right, (z > 0) & (d > z), (z < chips - 1) & (d < z))

            @pl.when(active)
            def _():
                self.to_sibling(d).wait_recv()
                for q in range(PARTS):
                    self.wait_line(d, q)
                    self.add(d, q, True)
                    slot = jnp.where(~right & (d == z - 1), chips, d)
                    self.along(d, slot, q, jnp.where(right, z + 1, z - 1)).start()

    def own_sum(self):
        chips, z, c = self.line.chips, self.line.z, self.line.c
        total, rx = self.total, self.rx
        self.to_sibling(z).wait_recv()
        for q in range(PARTS):

            @pl.when(z > 0)
            def _():
                self.wait_line(z, q)

            @pl.when(z < chips - 1)
            def _():
                self.wait_line(chips, q)

        def add_up(at):
            total[at, :] = self.part[z, c, at, :].astype(F32) + self.sib[z, at, :].astype(F32)

            @pl.when(z > 0)
            def _():
                total[at, :] += rx[z, at, :].astype(F32)

            @pl.when(z < chips - 1)
            def _():
                total[at, :] += rx[chips, at, :].astype(F32)

        row_chunks(self.rows, add_up)

    def finish(self):
        z = self.line.z

        @pl.loop(0, self.line.chips)
        def _(d):
            self.to_sibling(d).wait_send()
            for q in range(PARTS):

                @pl.when(d > z)
                def _():
                    self.to_right(d, q).wait_send()

                @pl.when(d < z)
                def _():
                    self.to_left(d, q).wait_send()


class Gather:
    @staticmethod
    def scratch(n):
        return [DMA((3, n)), DMA((n,)), DMA(())]

    def __init__(self, line, own, buf, scratch):
        self.line, self.own, self.buf = line, own, buf
        self.send, self.recv, self.local_sem = scratch

    def copy(self, way, slot, mine=False):
        line, z, c = self.line, self.line.z, self.line.c
        src = self.own if mine else self.buf.at[slot]
        device = (line.dev(z, 1 - c), line.dev(z + 1, c), line.dev(z - 1, c))[way]
        return remote(src, self.buf.at[slot], self.send.at[way, slot], self.recv.at[slot], device)

    def local(self):
        return pltpu.make_async_copy(self.own, self.buf.at[self.line.me], self.local_sem)

    def pass_on(self, at, mine=False):
        z, slot = self.line.z, 2 * at + self.line.c

        @pl.when((z < self.line.chips - 1) & (at <= z))
        def _():
            self.copy(1, slot, mine).start()

        @pl.when((z > 0) & (at >= z))
        def _():
            self.copy(2, slot, mine).start()

        self.copy(0, slot, mine).start()

    def start(self):
        self.pass_on(self.line.z, True)
        self.local().start()

    def arrive(self, t):
        z = self.line.z
        for at, there in ((z - t, z - t >= 0), (z + t, z + t < self.line.chips)):

            @pl.when(there)
            def _():
                self.copy(0, 2 * at + self.line.c).wait_recv()
                self.pass_on(at)

    def ready(self, j):
        at = self.line.near_first(j)
        if isinstance(j, int):
            if j == 0:
                self.local().wait()
        else:

            @pl.when(j == 0)
            def _():
                self.local().wait()

        self.copy(0, 2 * at + 1 - self.line.c).wait_recv()
        return at

    def finish(self):
        z = self.line.z

        @pl.loop(0, self.line.chips)
        def _(at):
            slot = 2 * at + self.line.c
            self.copy(0, slot).wait_send()

            @pl.when((z < self.line.chips - 1) & (at <= z))
            def _():
                self.copy(1, slot).wait_send()

            @pl.when((z > 0) & (at >= z))
            def _():
                self.copy(2, slot).wait_send()


def load(src, dst, sem):
    copy = pltpu.make_async_copy(src, dst, sem)
    copy.start()
    copy.wait()


def rows_of(z, rows):
    return pl.ds(pl.multiple_of(z * 2 * rows, 2 * rows), 2 * rows)


class Square:
    @staticmethod
    def scratch(units, tiles):
        return [DMA((units, 2, tiles)), DMA((units, 2, tiles)), DMA((units,)), DMA((units,)), DMA(())]

    def __init__(self, line, units, scratch):
        self.line, self.units = line, units
        self.send1, self.recv1, self.send2, self.recv2, self.sem = scratch
        self.tiles = self.send1.shape[2]

    def ways(self, u):
        line = self.line
        return (line.xn, line.yn) if self.units[u]["x_first"] else (line.yn, line.xn)

    def whole(self, u, block):
        unit = self.units[u]
        return unit["parts"].at[block, pl.ds(unit["row"], unit["rows"])]

    def first(self, u, slot, t):
        unit = self.units[u]
        one, _ = self.ways(u)
        block = one if slot == 0 else self.line.diag
        src, dst = self.whole(u, block), unit["land1"].at[slot]
        if self.tiles > 1:
            axis = unit["axis"]
            step = dst.shape[axis] // self.tiles
            at = (pl.ds(t * step, step),) if axis == 0 else (slice(None), pl.ds(t * step, step))
            src, dst = src.at[at], dst.at[at]
        return remote(src, dst, self.send1.at[u, slot, t], self.recv1.at[u, slot, t], (one, self.line.me))

    def start(self, u, t=0):
        for slot in range(2):
            self.first(u, slot, t).start()

    def add(self, u, slot, block, also=None):
        unit = self.units[u]
        for t in range(self.tiles):
            self.first(u, slot, t).wait_recv()
        land, tmp = unit["land1"], unit["tmp"].at[pl.ds(0, unit["rows"])]
        load(self.whole(u, block), tmp, self.sem)

        def one(at):
            value = land[slot, at, :].astype(F32) + tmp[at, :].astype(F32)
            if also is not None:
                value = value + also[at, :].astype(F32)
            land[slot, at, :] = value.astype(BF16)

        row_chunks(unit["rows"], one)

    def second(self, u):
        unit = self.units[u]
        _, two = self.ways(u)
        return remote(unit["land1"].at[1], unit["land2"], self.send2.at[u], self.recv2.at[u], (two, self.line.me))

    def fold(self, u):
        self.add(u, 1, self.ways(u)[1])
        self.second(u).start()

    def result(self, u):
        self.second(u).wait_recv()
        self.add(u, 0, self.line.replica, self.units[u]["land2"])

    def finish(self):
        for u in range(len(self.units)):
            self.second(u).wait_send()
            for slot in range(2):
                for t in range(self.tiles):
                    self.first(u, slot, t).wait_send()


def start_kernel(
    n, reps, spread, tok, gains, wqkv, wg, wu, cos, sin, normed, qkv, w_all, gu_own, gain_a, gain_m, gains_buf, own, wv, blk,
    g_send, g_recv, a_send, a_recv, r_send, r_recv, u_send, u_recv, local_sem, load_sem, *ag_scratch,
):
    line = Line(n)
    me, rep = line.me, line.replica
    rows, width = tok.shape
    w_rows = gains.shape[1]
    fb = gu_own.shape[-1]
    own_cols = fb * reps
    line.enter_all(reps)

    def gain_copy(i, to, slot):
        return remote(gains, gains_buf.at[slot], g_send.at[i], g_recv.at[slot], (rep, to))

    def qkv_copy(i, to, slot):
        piece = wqkv.at[to, pl.ds(rep * (w_rows // reps), w_rows // reps)]
        return remote(piece, w_all.at[slot, rep], a_send.at[i], a_recv.at[slot], (rep, to))

    def gu_copy(k, i, to, slot):
        piece = (wg, wu)[k].at[:, pl.ds(pl.multiple_of(to * own_cols + rep * fb, 128), fb)]
        at = pl.ds(pl.multiple_of(slot * w_rows, 16), w_rows)
        return remote(piece, gu_own.at[k, at], u_send.at[k, i], u_recv.at[k, slot], (rep, to))

    for i in range(1, n):
        gain_copy(i, line.other(i), me).start()
    for i in range(1, n):
        qkv_copy(i, line.other(i), me).start()
    mine = [
        pltpu.make_async_copy(
            wqkv.at[me, pl.ds(rep * (w_rows // reps), w_rows // reps)], w_all.at[me, rep], local_sem.at[0]
        )
    ]
    if spread:
        for i in range(1, n):
            for k in range(2):
                gu_copy(k, i, line.other(i), me).start()
        for k in range(2):
            piece = (wg, wu)[k].at[:, pl.ds(pl.multiple_of(me * own_cols + rep * fb, 128), fb)]
            at = pl.ds(pl.multiple_of(me * w_rows, 16), w_rows)
            mine.append(pltpu.make_async_copy(piece, gu_own.at[k, at], local_sem.at[1 + k]))
    for copy in mine:
        copy.start()
    gains_buf[me] = gains[...]
    for i in range(1, n):
        gain_copy(i, me, line.other(i)).wait_recv()
    gain_a[...] = jnp.concatenate([gains_buf[i, 0:1, :].astype(F32) for i in range(n)], 1)
    gain_m[...] = jnp.concatenate([gains_buf[i, 1:2, :].astype(F32) for i in range(n)], 1)

    def norm(at):
        resid = tok[at, :].astype(F32)
        inverse = lax.rsqrt(jnp.mean(resid * resid, -1, keepdims=True) + EPSILON)
        own[at, :] = (resid * inverse * gain_a[...]).astype(BF16)

    row_chunks(rows, norm)
    gather = Gather(line, own, normed, ag_scratch)
    gather.start()

    for i in range(1, n):
        qkv_copy(i, me, line.other(i)).wait_recv()
    mine[0].wait()

    def share(i, to, slot):
        return remote(w_all.at[:, slot], w_all.at[:, slot], r_send.at[i], r_recv.at[slot], (to, me))

    for i in range(1, reps):
        share(i, lax.rem(rep + i, reps), rep).start()
    gather.arrive(1)
    for i in range(1, reps):
        share(i, rep, lax.rem(rep + i, reps)).wait_recv()
    load(w_all, wv, load_sem)
    cols = wv.shape[-1]
    lane = lax.broadcasted_iota(jnp.int32, (2 * rows, 128), 1)
    front = lax.rem(lane, HD) < HD // 2

    @pl.loop(0, line.chips)
    def _(j):
        @pl.when((j > 0) & (j < line.chips - 1))
        def _():
            gather.arrive(j + 1)

        z = gather.ready(j)
        load(normed.at[pl.ds(2 * z, 2)], blk, load_sem)
        at = rows_of(z, rows)
        raw = dot(blk[...].reshape(2 * rows, width), wv[...].reshape(width, cols))
        for t in range(0, cols, 128):
            part = raw[:, t : t + 128]
            cos_t, sin_t = cos[at, :], sin[at, :]
            if t == cols - 128:
                cos_t, sin_t = jnp.where(lane < HD, cos_t, 1.0), jnp.where(lane < HD, sin_t, 0.0)
            partner = jnp.where(front, pltpu.roll(part, 128 - HD // 2, 1), pltpu.roll(part, HD // 2, 1))
            qkv[at, t : t + 128] = (part * cos_t + partner * sin_t).astype(BF16)

    for i in range(1, n):
        gain_copy(i, line.other(i), me).wait_send()
        qkv_copy(i, line.other(i), me).wait_send()
    for i in range(1, reps):
        share(i, lax.rem(rep + i, reps), rep).wait_send()
    if spread:
        for k in range(2):
            mine[1 + k].wait()
            for i in range(1, n):
                gu_copy(k, i, line.other(i), me).wait_send()
                gu_copy(k, i, me, line.other(i)).wait_recv()
    gather.finish()


def start_layer(n, reps, spread, tok, gains, wqkv, wg, wu, cos, sin):
    rows, width = tok.shape
    w_rows = gains.shape[1]
    cols = wqkv.shape[-1]
    group = cos.shape[0]
    fb = wg.shape[1] // n // reps
    return pl.pallas_call(
        functools.partial(start_kernel, n, reps, spread),
        name="start_layer",
        out_shape=(
            jax.ShapeDtypeStruct((n, rows, width), BF16),
            jax.ShapeDtypeStruct((group, cols), BF16),
            jax.ShapeDtypeStruct((n, reps, w_rows // reps, cols), BF16),
            jax.ShapeDtypeStruct((2, width, fb), BF16),
            jax.ShapeDtypeStruct((1, width), F32),
            jax.ShapeDtypeStruct((1, width), F32),
        ),
        in_specs=[VMEM, VMEM, ANY, ANY, ANY, VMEM, VMEM],
        out_specs=(ANY, VMEM, ANY, ANY, VMEM, VMEM),
        scratch_shapes=[
            pltpu.VMEM((n, 16, w_rows), BF16),
            pltpu.VMEM((rows, width), BF16),
            pltpu.VMEM((n, reps, w_rows // reps, cols), BF16),
            pltpu.VMEM((2, rows, width), BF16),
            DMA((n,)),
            DMA((n,)),
            DMA((n,)),
            DMA((n,)),
            DMA((reps,)),
            DMA((reps,)),
            DMA((2, n)),
            DMA((2, n)),
            DMA((3,)),
            DMA(()),
        ]
        + Gather.scratch(n),
        compiler_params=pltpu.CompilerParams(collective_id=4, has_side_effects=True, vmem_limit_bytes=VMEM_BYTES),
        cost_estimate=pl.CostEstimate(flops=2 * group * width * cols, bytes_accessed=300 * 2**20, transcendentals=0),
    )(tok, gains, wqkv, wg, wu, cos, sin)


def weight_copies(gu, wbuf, w_sem):
    blocks, _, _, fb = gu.shape
    own = blocks * fb

    def copy(b, k):
        at = k * own + b * fb
        if not isinstance(at, int):
            at = pl.multiple_of(at, 128)
        return pltpu.make_async_copy(gu.at[b, k], wbuf.at[:, pl.ds(at, fb)], w_sem.at[k, b])

    return copy


def mlp_kernel(
    n, blocks, spread, att, wo, tok, gain, gu_in, cot, wd, normed, middle, hidden, grads, gu_out, cot_all, *scratch
):
    scatter_scratch, scratch = scratch[:8], scratch[8:]
    ag_scratch, cot_scratch, scratch = scratch[:3], scratch[3:6], scratch[6:]
    own_normed, blk, wbuf, wd_buf, grad_hid, hid_stage, grad_stage, w_sem, out_sem, load_sem, x_send, x_recv = scratch
    line = Line(n)
    rows, width = tok.shape
    fb = gu_in.shape[-1]
    own = blocks * fb
    rep = line.replica
    scatter = Scatter(line, scatter_scratch)
    cots = Gather(line, cot, cot_all, cot_scratch)
    gather = Gather(line, own_normed, normed, ag_scratch)
    wd_copy = pltpu.make_async_copy(wd, wd_buf, load_sem.at[1])
    wd_copy.start()
    line.enter(spread)
    cots.start()
    if spread:
        gu = gu_out

        def gu_copy(way, k, src, slot, device):
            return remote(src, gu.at[slot, k], x_send.at[way, k], x_recv.at[way, k], (device, line.me))

        firsts = [(0, 0, line.xn), (1, 1, line.yn), (0, 1, line.xn), (1, 0, line.yn)]
        for way, k, device in firsts:
            gu_copy(way, k, gu_in.at[k], rep, device).start()
        for k in range(2):
            pltpu.make_async_copy(gu_in.at[k], wbuf.at[:, pl.ds(pl.multiple_of(k * own + rep * fb, 128), fb)], w_sem.at[k, rep]).start()
            pltpu.make_async_copy(gu_in.at[k], gu.at[rep, k], load_sem.at[2 + k]).start()
    else:
        gu = gu_in
    weight_copy = weight_copies(gu, wbuf, w_sem)
    if not spread:
        for b in range(blocks):
            for k in range(2):
                weight_copy(b, k).start()

    def out_part(d):
        x = att[rows_of(d, rows), :]
        for t in range(0, width, 512):
            part = dot(x, wo[:, t : t + 512]).astype(BF16)
            scatter.part[d, :, :, t : t + 512] = part.reshape(2, rows, 512)

    scatter.produce(out_part)
    wd_copy.wait()

    def grad_hidden(j):
        z = cots.ready(j)
        load(cot_all.at[pl.ds(2 * z, 2)], blk, load_sem.at[0])
        x = blk[...].reshape(2 * rows, width)
        tile = min(256, own)
        for t in range(0, own, tile):
            grad_hid[rows_of(z, rows), t : t + tile] = dot_t(x, wd_buf[t : t + tile, :]).astype(BF16)

    @pl.loop(0, line.chips - 1)
    def _(s):
        cots.arrive(s + 1)
        scatter.duty(s)
        grad_hidden(s)

    grad_hidden(line.chips - 1)
    if spread:
        for way, k, slot, device in ((0, 0, line.xn, line.yn), (1, 1, line.yn, line.xn)):
            gu_copy(way, k, gu.at[slot, k], slot, device).wait_recv()
            gu_copy(2 + way, k, gu.at[slot, k], slot, device).start()
            weight_copy(slot, k).start()
    scatter.own_sum()

    def norm(at):
        mid = tok[at, :].astype(F32) + scatter.total[at, :]
        middle[at, :] = mid
        inverse = lax.rsqrt(jnp.mean(mid * mid, -1, keepdims=True) + EPSILON)
        own_normed[at, :] = (mid * inverse * gain[...]).astype(BF16)

    row_chunks(rows, norm)
    gather.start()
    if spread:
        for way, k, slot in ((0, 1, line.xn), (1, 0, line.yn)):
            gu_copy(way, k, gu.at[slot, k], slot, line.xn).wait_recv()
            weight_copy(slot, k).start()
        for way, k, device in ((2, 0, line.yn), (3, 1, line.xn)):
            gu_copy(way, k, gu.at[line.diag, k], line.diag, device).wait_recv()
            weight_copy(line.diag, k).start()
        for k in range(2):
            pltpu.make_async_copy(gu_in.at[k], gu.at[rep, k], load_sem.at[2 + k]).wait()
    for b in range(blocks):
        for k in range(2):
            weight_copy(b, k).wait()

    def out_copies(z):
        at = rows_of(z, rows)
        return (
            pltpu.make_async_copy(hid_stage, hidden.at[at], out_sem.at[0]),
            pltpu.make_async_copy(grad_stage, grads.at[at], out_sem.at[1]),
        )

    @pl.loop(0, line.chips)
    def _(j):
        @pl.when(j > 0)
        def _():
            gather.arrive(j)

        z = gather.ready(j)
        load(normed.at[pl.ds(2 * z, 2)], blk, load_sem.at[0])

        @pl.when(j > 0)
        def _():
            for copy in out_copies(line.near_first(j - 1)):
                copy.wait()

        at = rows_of(z, rows)
        x = blk[...].reshape(2 * rows, width)
        tile = min(256, own)
        for t in range(0, own, tile):
            gate = dot(x, wbuf[:, t : t + tile])
            up = dot(x, wbuf[:, own + t : own + t + tile])
            sig = 1.0 / (1.0 + jnp.exp(-gate))
            gated = gate * sig
            gh = grad_hid[at, t : t + tile].astype(F32)
            hid_stage[:, t : t + tile] = (gated * up).astype(BF16)
            grad_stage[:, t : t + tile] = (gh * up * sig * (1.0 + gate * (1.0 - sig))).astype(BF16)
            grad_stage[:, own + t : own + t + tile] = (gh * gated).astype(BF16)
        for copy in out_copies(z):
            copy.start()

    for copy in out_copies(line.near_first(line.chips - 1)):
        copy.wait()
    if spread:
        for way, k, device in firsts:
            gu_copy(way, k, gu_in.at[k], rep, device).wait_send()
        for way, k, slot, device in ((2, 0, line.xn, line.yn), (3, 1, line.yn, line.xn)):
            gu_copy(way, k, gu.at[slot, k], slot, device).wait_send()
    scatter.finish()
    cots.finish()
    gather.finish()


def mlp_forward(n, reps, spread, att, wo, tok, gain, gu, cot, wd):
    rows, width = tok.shape
    group = att.shape[0]
    fb = gu.shape[-1]
    blocks = reps if spread else gu.shape[0]
    own = blocks * fb
    kept = (blocks, 2, width, fb) if spread else (1, 16, 128)
    return pl.pallas_call(
        functools.partial(mlp_kernel, n, blocks, spread),
        name="mlp_forward",
        out_shape=(
            jax.ShapeDtypeStruct((n, rows, width), BF16),
            jax.ShapeDtypeStruct((rows, width), F32),
            jax.ShapeDtypeStruct((group, own), BF16),
            jax.ShapeDtypeStruct((group, 2 * own), BF16),
            jax.ShapeDtypeStruct(kept, BF16),
            jax.ShapeDtypeStruct((n, rows, width), BF16),
        ),
        in_specs=[VMEM, VMEM, VMEM, VMEM, ANY, ANY, ANY],
        out_specs=(ANY, VMEM, ANY, ANY, ANY, ANY),
        scratch_shapes=Scatter.scratch(n, rows, width)
        + Gather.scratch(n)
        + Gather.scratch(n)
        + [
            pltpu.VMEM((rows, width), BF16),
            pltpu.VMEM((2, rows, width), BF16),
            pltpu.VMEM((width, 2 * own), BF16),
            pltpu.VMEM((own, width), BF16),
            pltpu.VMEM((group, own), BF16),
            pltpu.VMEM((2 * rows, own), BF16),
            pltpu.VMEM((2 * rows, 2 * own), BF16),
            DMA((2, blocks)),
            DMA((2,)),
            DMA((4,)),
            DMA((4, 2)),
            DMA((4, 2)),
        ],
        compiler_params=pltpu.CompilerParams(collective_id=1, has_side_effects=True, vmem_limit_bytes=VMEM_BYTES),
        cost_estimate=pl.CostEstimate(flops=2 * group * width * own * 3, bytes_accessed=400 * 2**20, transcendentals=0),
    )(att, wo, tok, gain, gu, cot, wd)


def norm_back(grad_normed, resid, gain):
    inverse = lax.rsqrt(jnp.mean(resid * resid, -1, keepdims=True) + EPSILON)
    unit = resid * inverse
    scaled = grad_normed * gain
    return inverse * (scaled - unit * jnp.mean(scaled * unit, -1, keepdims=True)), grad_normed * unit


def middle_kernel(
    n, blocks, spread, grads, gu, mid, cot, gain, wo, normed, hidden, cot_all, grad_mid, gml, grad_att, gain_sum,
    gate_parts, up_parts, down_parts, gate_q, up_q, down_q, *scratch,
):
    scatter_scratch, ag_scratch, scratch = scratch[:8], scratch[8:11], scratch[11:]
    own_low, blk, wbuf, w_sem, load_sem = scratch[:5]
    line = Line(n)
    rows, width = mid.shape
    group = grads.shape[0]
    fb = gu.shape[-1]
    own = blocks * fb
    scatter = Scatter(line, scatter_scratch)
    gather = Gather(line, own_low, gml, ag_scratch)
    weight_copy = weight_copies(gu, wbuf, w_sem)
    for b in range(blocks):
        for k in range(2):
            weight_copy(b, k).start()
    line.enter(spread)
    for b in range(blocks):
        for k in range(2):
            weight_copy(b, k).wait()

    def normed_part(d):
        x = grads[rows_of(d, rows), :]
        for t in range(0, width, 512):
            part = dot_t(x, wbuf[t : t + 512, :]).astype(BF16)
            scatter.part[d, :, :, t : t + 512] = part.reshape(2, rows, 512)

    scatter.produce(normed_part)
    tiles = 4
    tile = width // tiles
    if spread:
        gate_land, up_land, down_land, gate_in, up_in, down_in, tmp, tmp_down, stage, part_sem, out_sem = scratch[5:16]
        half = fb // 2
        units = [
            dict(parts=gate_parts, row=0, rows=width, x_first=True, axis=0, land1=gate_land, land2=gate_in, tmp=tmp),
            dict(parts=up_parts, row=0, rows=width, x_first=False, axis=0, land1=up_land, land2=up_in, tmp=tmp),
        ]
        for i in range(2):
            units.append(
                dict(
                    parts=down_parts, row=i * half, rows=half, x_first=i == 0, axis=1,
                    land1=down_land.at[i], land2=down_in.at[i], tmp=tmp_down,
                )
            )
        square = Square(line, units, scratch[16:])
        slots = [wbuf.at[pl.ds(0, group), pl.ds(i * tile, tile)] for i in range(2)]
        hid = wbuf.at[pl.ds(0, group), pl.ds(2 * tile, own)]

        def column_copy(i):
            src = normed if i < tiles else cot_all
            return pltpu.make_async_copy(src.at[:, pl.ds(i % tiles * tile, tile)], slots[i % 2], w_sem.at[0, i % 2])

        hid_copy = pltpu.make_async_copy(hidden, hid, w_sem.at[1, 0])
        hid_copy.start()
        column_copy(0).start()

        def weight_tile(i):
            t = i % tiles
            column_copy(i).wait()
            if i + 1 < 2 * tiles:
                column_copy(i + 1).start()
            if i < tiles:
                x = slots[i % 2][...]
                for k in range(2):
                    for b in range(blocks):
                        at = k * own + b * fb
                        stage[k, b] = tdot(x, grads[:, at : at + fb]).astype(BF16)
                copies = [
                    pltpu.make_async_copy(stage.at[k, b], parts.at[b, pl.ds(t * tile, tile)], part_sem.at[k, b])
                    for k, parts in enumerate((gate_parts, up_parts))
                    for b in range(blocks)
                ]
            else:
                if i == tiles:
                    hid_copy.wait()
                x = slots[i % 2][...]
                for b in range(blocks):
                    part = tdot(hid[:, b * fb : (b + 1) * fb], x).astype(BF16)
                    for k in range(2):
                        stage[k, b, :fb, :] = part[:, k * fb : (k + 1) * fb]
                copies = [
                    pltpu.make_async_copy(
                        stage.at[k, b, pl.ds(0, fb)], down_parts.at[b, :, pl.ds(t * tile + k * fb, fb)], part_sem.at[k, b]
                    )
                    for k in range(2)
                    for b in range(blocks)
                ]
            for copy in copies:
                copy.start()
            for copy in copies:
                copy.wait()
            for u in (0, 1) if i < tiles else (2, 3):
                square.start(u, t)

    for s in range(line.chips - 1):
        if spread:
            for i in range(s * 2 * tiles // 3, (s + 1) * 2 * tiles // 3):
                weight_tile(i)
        scatter.duty(s)
    scatter.own_sum()
    gain_sum[...] = jnp.zeros_like(gain_sum)

    def back(at):
        through, gain_term = norm_back(scatter.total[at, :], mid[at, :], gain[...])
        value = cot[at, :].astype(F32) + through
        grad_mid[at, :] = value
        own_low[at, :] = value.astype(BF16)
        gain_sum[...] += jnp.sum(gain_term, 0, keepdims=True)

    row_chunks(rows, back)
    gather.start()

    def attended_part(j):
        z = gather.ready(j)
        load(gml.at[pl.ds(2 * z, 2)], blk, load_sem)
        grad_att[rows_of(z, rows), :] = dot_t(blk[...].reshape(2 * rows, width), wo[...]).astype(BF16)

    if spread:
        square.fold(0)
        square.fold(1)
        gather.arrive(1)
        square.fold(2)
        square.fold(3)
        attended_part(0)
        gather.arrive(2)
        attended_part(1)
        gather.arrive(3)
        attended_part(2)
        attended_part(3)
        copies = []
        for u, out in ((0, gate_q), (1, up_q), (2, down_q.at[pl.ds(0, half)]), (3, down_q.at[pl.ds(half, half)])):
            square.result(u)
            copies.append(pltpu.make_async_copy(units[u]["land1"].at[0], out, out_sem.at[u]))
            copies[-1].start()
        for copy in copies:
            copy.wait()
        square.finish()
    else:

        @pl.loop(0, line.chips)
        def _(j):
            @pl.when(j > 0)
            def _():
                gather.arrive(j)

            attended_part(j)

    scatter.finish()
    gather.finish()


def middle_backward(n, spread, grads, gu, mid, cot, gain, wo, normed, hidden, cot_all):
    rows, width = mid.shape
    group = grads.shape[0]
    blocks, _, _, fb = gu.shape
    own = blocks * fb
    parts = [(4, width, fb), (4, width, fb), (4, fb, width), (width, fb), (width, fb), (fb, width)]
    if not spread:
        parts = [(16, 128)] * 6
    scratch = []
    if spread:
        scratch = [
            pltpu.VMEM((2, width, fb), BF16),
            pltpu.VMEM((2, width, fb), BF16),
            pltpu.VMEM((2, 2, fb // 2, width), BF16),
            pltpu.VMEM((width, fb), BF16),
            pltpu.VMEM((width, fb), BF16),
            pltpu.VMEM((2, fb // 2, width), BF16),
            pltpu.VMEM((width, fb), BF16),
            pltpu.VMEM((fb // 2, width), BF16),
            pltpu.VMEM((2, blocks, width // 4, fb), BF16),
            DMA((2, blocks)),
            DMA((4,)),
        ] + Square.scratch(4, 4)
    return pl.pallas_call(
        functools.partial(middle_kernel, n, blocks, spread),
        name="middle_backward",
        out_shape=(
            jax.ShapeDtypeStruct((rows, width), F32),
            jax.ShapeDtypeStruct((n, rows, width), BF16),
            jax.ShapeDtypeStruct((group, wo.shape[0]), BF16),
            jax.ShapeDtypeStruct((1, width), F32),
            *[jax.ShapeDtypeStruct(shape, BF16) for shape in parts],
        ),
        in_specs=[VMEM, ANY, VMEM, VMEM, VMEM, VMEM, ANY, ANY, ANY],
        out_specs=(VMEM, ANY, VMEM, VMEM) + (ANY,) * 6,
        scratch_shapes=Scatter.scratch(n, rows, width)
        + Gather.scratch(n)
        + [
            pltpu.VMEM((rows, width), BF16),
            pltpu.VMEM((2, rows, width), BF16),
            pltpu.VMEM((width, 2 * own), BF16),
            DMA((2, blocks)),
            DMA(()),
        ]
        + scratch,
        compiler_params=pltpu.CompilerParams(collective_id=2, has_side_effects=True, vmem_limit_bytes=VMEM_BYTES),
        cost_estimate=pl.CostEstimate(flops=2 * group * width * own * 3, bytes_accessed=400 * 2**20, transcendentals=0),
    )(grads, gu, mid, cot, gain, wo, normed, hidden, cot_all)


def end_kernel(
    n, reps, spread, grads, w, tok, grad_mid, gain, gain_m_sum, gate_q, up_q, down_q, qkv_parts, out_parts,
    grad_tok, gain_grads, gate_out, up_out, down_out, qkv_out, out_out, *scratch,
):
    scatter_scratch, scratch = scratch[:8], scratch[8:]
    gain_sum, gain_src, gain_land, gain_all, g_send, g_recv = scratch[:6]
    line = Line(n)
    rows, width = tok.shape
    me, rep = line.me, line.replica
    scatter = Scatter(line, scatter_scratch)
    line.enter_all(reps)
    if spread:
        a_send, a_recv, x_send, x_recv, local_sem, qkv_land, qkv_in, out_land, out_in, qkv_tmp, out_tmp = scratch[6:17]
        fb = gate_q.shape[-1]
        own = 4 * fb
        quarters, outs = (gate_q, up_q), (gate_out, up_out)
        w_rows = gate_out.shape[0]
        down_rows = fb // n
        qkv_rows = w_rows // 4
        out_rows = out_parts.shape[1] // 2
        counts = (n, n, n, n, 2)
        units = [
            dict(
                parts=qkv_parts, row=i * 4 * qkv_rows, rows=4 * qkv_rows, x_first=i == 0,
                land1=qkv_land.at[i], land2=qkv_in.at[i], tmp=qkv_tmp,
            )
            for i in range(2)
        ] + [
            dict(
                parts=out_parts, row=i * out_rows, rows=out_rows, x_first=i == 0,
                land1=out_land.at[i], land2=out_in.at[i], tmp=out_tmp,
            )
            for i in range(2)
        ]
        square = Square(line, units, scratch[17:])

        def place(k, f, replica):
            if k == 2:
                return down_out.at[pl.ds(pl.multiple_of(replica * fb + f * down_rows, 16), down_rows)]
            if k == 3:
                return qkv_out.at[f, replica]
            if k == 4:
                return out_out.at[pl.ds(pl.multiple_of(replica * 2 * out_rows + f * out_rows, 16), out_rows)]
            return outs[k].at[:, pl.ds(pl.multiple_of(f * own + replica * fb, 128), fb)]

        def block(k, f):
            if k == 3:
                half, inner = lax.div(f, 4), lax.rem(f, 4)
                return qkv_land.at[half, 0, pl.ds(pl.multiple_of(inner * qkv_rows, 16), qkv_rows)]
            return quarters[k].at[pl.ds(pl.multiple_of(f * w_rows, 16), w_rows)]

        def exchange(k, i, to, at):
            return remote(block(k, to), place(k, at, rep), a_send.at[k, i], a_recv.at[k, at], (rep, to))

        def send(way, k, f, src, replica, device):
            return remote(src, place(k, f, replica), x_send.at[way, k, f], x_recv.at[way, k, f], (device, me))

        def share(k, f, src):
            send(0, k, f, src, rep, line.xn).start()
            send(1, k, f, src, rep, line.yn).start()

        def corner(f):
            return (0, line.xn, line.yn) if f % 2 == 0 else (1, line.yn, line.xn)

        def forward(k, f):
            way, replica, device = corner(f)
            src = place(k, f, replica)
            send(way, k, f, src, replica, replica).wait_recv()
            send(2 + way, k, f, src, replica, device).start()

        def down_piece(f):
            return down_q.at[pl.ds(pl.multiple_of(f * down_rows, 16), down_rows)]

        def local(i, src, dst):
            return pltpu.make_async_copy(src, dst, local_sem.at[i])

        def mine(k):
            if k == 2:
                return local(2, down_q, down_out.at[pl.ds(pl.multiple_of(rep * fb, 16), fb)])
            return local(k, block(k, me), place(k, me, rep))

        def mine_out(i):
            return local(4 + i, out_land.at[i, 0], place(4, i, rep))

        for u in range(4):
            square.start(u)
        for i in range(1, n):
            for k in range(2):
                exchange(k, i, line.other(i), me).start()
        for k in range(2):
            share(k, me, block(k, me))
            mine(k).start()
        for f in range(n):
            share(2, f, down_piece(f))
        mine(2).start()

    def normed_part(d):
        x = grads[rows_of(d, rows), :]
        for t in range(0, width, 512):
            part = dot_t(x, w[t : t + 512, :]).astype(BF16)
            scatter.part[d, :, :, t : t + 512] = part.reshape(2, rows, 512)

    scatter.produce(normed_part)

    def pass_on(z, kinds):
        for core in range(2):
            f = 2 * z + core

            @pl.when(f != me)
            def _():
                for k in kinds:
                    exchange(k, 1, me, f).wait_recv()
                    share(k, f, place(k, f, rep))

    for s in range(line.chips - 1):
        scatter.duty(s)
        if spread:
            pass_on(line.near_first(s), (0, 1))
            if s == 0:
                for u in range(4):
                    square.fold(u)
            if s == 1:
                for u in range(4):
                    square.result(u)
                for i in range(1, n):
                    exchange(3, i, line.other(i), me).start()
                share(3, me, block(3, me))
                mine(3).start()
                for i in range(2):
                    share(4, i, out_land.at[i, 0])
                    mine_out(i).start()
    scatter.own_sum()
    gain_sum[...] = jnp.zeros_like(gain_sum)

    def back(at):
        through, gain_term = norm_back(scatter.total[at, :], tok[at, :].astype(F32), gain[...])
        grad_tok[at, :] = grad_mid[at, :] + through
        gain_sum[...] += jnp.sum(gain_term, 0, keepdims=True)

    row_chunks(rows, back)

    g_rows = gain_grads.shape[1]
    gain_src[...] = jnp.zeros_like(gain_src)
    for f in range(n):
        gain_src[f, 0:1, :] = gain_sum[:, f * g_rows : (f + 1) * g_rows]
        gain_src[f, 1:2, :] = gain_m_sum[:, f * g_rows : (f + 1) * g_rows]

    def gain_copy(i, to, slot):
        return remote(gain_src.at[to], gain_land.at[slot], g_send.at[0, i], g_recv.at[0, slot], (rep, to))

    def gain_share(i, to, slot):
        return remote(gain_all.at[slot], gain_all.at[slot], g_send.at[1, i], g_recv.at[1, slot], (to, me))

    for i in range(1, n):
        gain_copy(i, line.other(i), me).start()
    gain_land[me] = gain_src[me]
    if spread:
        pass_on(line.near_first(line.chips - 1), (0, 1))
        for f in range(n):
            forward(2, f)
        for j in range(line.chips):
            pass_on(line.near_first(j), (3,))
    for i in range(1, n):
        gain_copy(i, me, line.other(i)).wait_recv()
    gain_all[rep] = functools.reduce(lambda a, b: a + b, [gain_land[i] for i in range(n)])
    for i in range(1, reps):
        gain_share(i, lax.rem(rep + i, reps), rep).start()
    if spread:
        for f in range(n):
            for k in range(2):
                forward(k, f)
        for f in range(n):
            forward(3, f)
        for f in range(2):
            forward(4, f)
    for i in range(1, reps):
        gain_share(i, rep, lax.rem(rep + i, reps)).wait_recv()
    gain_grads[...] = functools.reduce(lambda a, b: a + b, [gain_all[i] for i in range(reps)])
    for i in range(1, n):
        gain_copy(i, line.other(i), me).wait_send()
    for i in range(1, reps):
        gain_share(i, lax.rem(rep + i, reps), rep).wait_send()
    if spread:
        for k in range(4):
            mine(k).wait()
        for i in range(2):
            mine_out(i).wait()
        for k in (0, 1, 3):
            for i in range(1, n):
                exchange(k, i, line.other(i), me).wait_send()
        for k in range(5):
            for f in range(counts[k]):
                src = place(k, f, rep)
                send(0, k, f, src, rep, line.xn).wait_send()
                send(1, k, f, src, rep, line.yn).wait_send()
                way, replica, device = corner(f)
                send(2 + way, k, f, src, replica, device).wait_send()
                send(2 + way, k, f, src, line.diag, replica).wait_recv()
                far = (line.yn, line.xn)[way]
                send(1 - way, k, f, src, far, far).wait_recv()
        square.finish()
    scatter.finish()


def end_layer(n, reps, spread, grads, w, tok, grad_mid, gain, gain_m_sum, gate_q, up_q, down_q, qkv_parts, out_parts):
    rows, width = tok.shape
    group, cols = grads.shape
    w_rows = width // n
    shapes, scratch = [(16, 128)] * 5, []
    if spread:
        fb = gate_q.shape[-1]
        own = 4 * fb
        heads_rows = out_parts.shape[1]
        q_rows = w_rows // 4
        shapes = [(w_rows, n * own)] * 2 + [(own, width), (n, 4, q_rows, cols), (4 * heads_rows, width)]
        scratch = [
            DMA((4, n)),
            DMA((4, n)),
            DMA((4, 5, n)),
            DMA((4, 5, n)),
            DMA((6,)),
            pltpu.VMEM((2, 2, 4 * q_rows, cols), BF16),
            pltpu.VMEM((2, 4 * q_rows, cols), BF16),
            pltpu.VMEM((2, 2, heads_rows // 2, width), BF16),
            pltpu.VMEM((2, heads_rows // 2, width), BF16),
            pltpu.VMEM((4 * q_rows, cols), BF16),
            pltpu.VMEM((heads_rows // 2, width), BF16),
        ] + Square.scratch(4, 1)
    return pl.pallas_call(
        functools.partial(end_kernel, n, reps, spread),
        name="end_layer",
        out_shape=(
            jax.ShapeDtypeStruct((rows, width), F32),
            jax.ShapeDtypeStruct((8, w_rows), F32),
            *[jax.ShapeDtypeStruct(shape, BF16) for shape in shapes],
        ),
        in_specs=[VMEM] * 6 + [ANY] * 5,
        out_specs=(VMEM, VMEM) + (ANY,) * 5,
        scratch_shapes=Scatter.scratch(n, rows, width)
        + [
            pltpu.VMEM((1, width), F32),
            pltpu.VMEM((n, 8, w_rows), F32),
            pltpu.VMEM((n, 8, w_rows), F32),
            pltpu.VMEM((reps, 8, w_rows), F32),
            DMA((2, max(n, reps))),
            DMA((2, max(n, reps))),
        ]
        + scratch,
        compiler_params=pltpu.CompilerParams(collective_id=3, has_side_effects=True, vmem_limit_bytes=VMEM_BYTES),
        cost_estimate=pl.CostEstimate(flops=2 * group * width * cols, bytes_accessed=400 * 2**20, transcendentals=0),
    )(grads, w, tok, grad_mid, gain, gain_m_sum, gate_q, up_q, down_q, qkv_parts, out_parts)


def key_range(block, long_len):
    longs = long_len // QBLK
    return (0, block + 1, False) if block < longs else (longs, block + 1 - longs, True)


def score_mask(q_block, k_block, seg_row, seg_col, heads, compare):
    visible = None
    shape = (QBLK, QBLK)
    if q_block == k_block:
        visible = lax.broadcasted_iota(jnp.int32, shape, 0) <= lax.broadcasted_iota(jnp.int32, shape, 1)
    if compare:
        k_at, q_at = k_block * QBLK, q_block * QBLK
        same = seg_col[k_at : k_at + QBLK, :] == seg_row[:, q_at : q_at + QBLK]
        visible = same if visible is None else visible & same
    if visible is None:
        return None
    bias = jnp.where(visible, 0.0, MASKED)
    return jnp.concatenate([bias] * heads, 1)


def one_hot_rows(rank_row, start):
    group = rank_row.shape[1]
    places = start + lax.broadcasted_iota(jnp.int32, (QBLK, group), 0)
    return jnp.where(rank_row[...] == places, 1.0, 0.0).astype(BF16)


def one_hot_back(rank_col, start):
    group = rank_col.shape[0]
    places = lax.broadcasted_iota(jnp.int32, (QBLK, group), 1)
    return jnp.where(rank_col[pl.ds(start, QBLK), :] == places, 1.0, 0.0).astype(BF16)


def attention_kernel(heads, long_len, qkv, rank_row, rank_col, seg_row, seg_col, q_out, kv_out, lse, att_t, att, s_buf, v_t):
    group = qkv.shape[0]
    q_cols = heads * HD
    n_blocks = group // QBLK
    for b in range(n_blocks):
        ordered = dot(one_hot_rows(rank_row, b * QBLK), qkv[...])
        for h in range(heads):
            q_out[b, h * QBLK : (h + 1) * QBLK, :] = (ordered[:, h * HD : (h + 1) * HD] * 0.125).astype(BF16)
        kv_out[0, b * QBLK : (b + 1) * QBLK, :] = ordered[:, q_cols : q_cols + HD].astype(BF16)
        values = ordered[:, q_cols + HD :]
        kv_out[1, b * QBLK : (b + 1) * QBLK, :] = values.astype(BF16)
        v_t[:, b * QBLK : (b + 1) * QBLK] = values.T.astype(BF16)
    for b in range(n_blocks):
        first, count, compare = key_range(b, long_len)
        queries = q_out[b]
        top = None
        for i in range(count):
            k_at = (first + i) * QBLK
            scores = dot_t(kv_out[0, k_at : k_at + QBLK, :], queries)
            bias = score_mask(b, first + i, seg_row, seg_col, heads, compare)
            if bias is not None:
                scores = scores + bias
            s_buf[i] = scores
            high = jnp.max(scores, 0, keepdims=True)
            top = high if top is None else jnp.maximum(top, high)
        total, out = 0.0, 0.0
        for i in range(count):
            k_at = (first + i) * QBLK
            terms = jnp.exp(s_buf[i] - top)
            total = total + jnp.sum(terms, 0, keepdims=True)
            out = out + dot(v_t[:, k_at : k_at + QBLK], terms.astype(BF16))
        lse[b] = top + jnp.log(total)
        out = out / total
        for h in range(heads):
            att_t[h * HD : (h + 1) * HD, b * QBLK : (b + 1) * QBLK] = out[:, h * QBLK : (h + 1) * QBLK]
    low = att_t[...].astype(BF16)

    @pl.loop(0, n_blocks)
    def _(b):
        at = pl.multiple_of(b * QBLK, QBLK)
        att[pl.ds(at, QBLK), :] = dot_t(one_hot_back(rank_col, at), low).astype(BF16)


def attention_forward(heads, long_len, qkv, rank_row, rank_col, seg_row, seg_col):
    group = qkv.shape[0]
    n_blocks = group // QBLK
    return pl.pallas_call(
        functools.partial(attention_kernel, heads, long_len),
        name="attention_forward",
        out_shape=(
            jax.ShapeDtypeStruct((n_blocks, heads * QBLK, HD), BF16),
            jax.ShapeDtypeStruct((2, group, HD), BF16),
            jax.ShapeDtypeStruct((n_blocks, 1, heads * QBLK), F32),
            jax.ShapeDtypeStruct((heads * HD, group), F32),
            jax.ShapeDtypeStruct((group, heads * HD), BF16),
        ),
        in_specs=[VMEM] * 5,
        out_specs=(VMEM,) * 5,
        scratch_shapes=[
            pltpu.VMEM((long_len // QBLK, QBLK, heads * QBLK), F32),
            pltpu.VMEM((HD, group), BF16),
        ],
        compiler_params=pltpu.CompilerParams(vmem_limit_bytes=VMEM_BYTES),
        cost_estimate=pl.CostEstimate(flops=10**10, bytes_accessed=10 * 2**20, transcendentals=0),
    )(qkv, rank_row, rank_col, seg_row, seg_col)


def attention_back_kernel(
    heads, long_len, q_in, kv, lse, att_t, grad_att, rank_row, rank_col, seg_row, seg_col, cos_t, sin_t, out,
    grad_kv, grad_t, k_t, go_rows, go_t,
):
    group = kv.shape[1]
    n_blocks = group // QBLK
    half = HD // 2
    q_cols = heads * HD
    for b in range(n_blocks):
        at = b * QBLK
        ordered = dot(one_hot_rows(rank_row, at), grad_att[...])
        for h in range(heads):
            go_rows[b, h * QBLK : (h + 1) * QBLK, :] = ordered[:, h * HD : (h + 1) * HD].astype(BF16)
        go_t[:, at : at + QBLK] = ordered.T
        k_t[:, at : at + QBLK] = kv[0, at : at + QBLK, :].astype(F32).T.astype(BF16)
    grad_kv[...] = jnp.zeros_like(grad_kv)
    for b in range(n_blocks):
        first, count, compare = key_range(b, long_len)
        q_at = b * QBLK
        queries, grad_rows = q_in[b], go_rows[b]
        centre = jnp.concatenate(
            [
                jnp.sum(
                    go_t[h * HD : (h + 1) * HD, q_at : q_at + QBLK] * att_t[h * HD : (h + 1) * HD, q_at : q_at + QBLK],
                    0,
                    keepdims=True,
                )
                for h in range(heads)
            ],
            1,
        )
        grad_q = 0.0
        for i in range(count):
            k_at = (first + i) * QBLK
            scores = dot_t(kv[0, k_at : k_at + QBLK, :], queries)
            bias = score_mask(b, first + i, seg_row, seg_col, heads, compare)
            if bias is not None:
                scores = scores + bias
            probs = jnp.exp(scores - lse[b])
            grad_probs = dot_t(kv[1, k_at : k_at + QBLK, :], grad_rows)
            grad_scores = (probs * (grad_probs - centre)).astype(BF16)
            grad_kv[0, k_at : k_at + QBLK, :] += dot(grad_scores, queries)
            grad_kv[1, k_at : k_at + QBLK, :] += dot(probs.astype(BF16), grad_rows)
            grad_q = grad_q + dot(k_t[:, k_at : k_at + QBLK], grad_scores)
        cos_b, sin_b = cos_t[:, q_at : q_at + QBLK], sin_t[:, q_at : q_at + QBLK]

        def turned(value):
            front, back = value[:half], value[half:]
            return jnp.concatenate([front * cos_b + back * sin_b, back * cos_b - front * sin_b], 0).astype(BF16)

        for h in range(heads):
            grad_t[h * HD : (h + 1) * HD, q_at : q_at + QBLK] = turned(grad_q[:, h * QBLK : (h + 1) * QBLK] * 0.125)
    for b in range(n_blocks):
        at = b * QBLK
        cos_b, sin_b = cos_t[:, at : at + QBLK], sin_t[:, at : at + QBLK]
        value = grad_kv[0, at : at + QBLK, :].T
        front, back = value[:half], value[half:]
        grad_t[q_cols : q_cols + half, at : at + QBLK] = (front * cos_b + back * sin_b).astype(BF16)
        grad_t[q_cols + half : q_cols + HD, at : at + QBLK] = (back * cos_b - front * sin_b).astype(BF16)
        grad_t[q_cols + HD :, at : at + QBLK] = grad_kv[1, at : at + QBLK, :].T.astype(BF16)

    @pl.loop(0, n_blocks)
    def _(b):
        at = pl.multiple_of(b * QBLK, QBLK)
        out[pl.ds(at, QBLK), :] = dot_t(one_hot_back(rank_col, at), grad_t[...]).astype(BF16)


def attention_backward(heads, long_len, q_in, kv, lse, att_t, grad_att, rank_row, rank_col, seg_row, seg_col, cos_t, sin_t):
    group = kv.shape[1]
    n_blocks = group // QBLK
    cols = heads * HD + 2 * HD
    return pl.pallas_call(
        functools.partial(attention_back_kernel, heads, long_len),
        name="attention_backward",
        out_shape=jax.ShapeDtypeStruct((group, cols), BF16),
        in_specs=[VMEM] * 11,
        out_specs=VMEM,
        scratch_shapes=[
            pltpu.VMEM((2, group, HD), F32),
            pltpu.VMEM((cols, group), BF16),
            pltpu.VMEM((HD, group), BF16),
            pltpu.VMEM((n_blocks, heads * QBLK, HD), BF16),
            pltpu.VMEM((heads * HD, group), F32),
        ],
        compiler_params=pltpu.CompilerParams(vmem_limit_bytes=VMEM_BYTES),
        cost_estimate=pl.CostEstimate(flops=2 * 10**10, bytes_accessed=10 * 2**20, transcendentals=0),
    )(q_in, kv, lse, att_t, grad_att, rank_row, rank_col, seg_row, seg_col, cos_t, sin_t)


def body(
    tokens, segment, position, attn_gain, w_query, w_key, w_value, w_out, mlp_gain, w_gate, w_up, w_down, cotangent
):
    rows, width = tokens.shape
    group = segment.shape[0]
    long_len = group * 2 // 3
    n = lax.axis_size("fsdp")
    reps = lax.axis_size("replica")
    w_rows = w_query.shape[0]
    ff_own = w_gate.shape[1] // n
    ff_blk = ff_own // reps
    heads = H // n
    q_cols = heads * HD
    dup = n // KVH
    spread = reps == 4 and ff_blk % 128 == 0

    def swap(x):
        return lax.all_to_all(x, "fsdp", 0, 0, tiled=True)

    same = jnp.sum((segment[:, None] == segment[None, :]).astype(jnp.int32), 1)
    key = jnp.where(same == long_len, -1, segment) * group + position
    rank = jnp.sum((key[None, :] < key[:, None]).astype(jnp.int32), 1)
    onehot = rank[None, :] == lax.iota(jnp.int32, group)[:, None]
    seg_sorted = jnp.sum(jnp.where(onehot, segment[None, :], 0), 1)
    pos_sorted = jnp.sum(jnp.where(onehot, position[None, :], 0), 1)
    ranks = (rank[None, :], rank[:, None], seg_sorted[None, :], seg_sorted[:, None])
    freqs = jnp.exp(-math.log(ROPE_BASE) * jnp.arange(HD // 2, dtype=F32) * (2.0 / HD))
    angles = position.astype(F32)[:, None] * freqs[None, :]
    cos_tab, sin_tab = jnp.cos(angles), jnp.sin(angles)
    cos_tab = jnp.concatenate([cos_tab] * 4, 1)
    sin_tab = jnp.concatenate([-sin_tab, sin_tab] * 2, 1)

    gains = jnp.concatenate([attn_gain[None], mlp_gain[None], jnp.zeros((14, w_rows), BF16)])
    kv_w = jnp.concatenate([w_key.reshape(w_rows, KVH, HD), w_value.reshape(w_rows, KVH, HD)], -1)
    kv_w = jnp.repeat(kv_w, dup, axis=1)
    qkv_w = jnp.concatenate([w_query.reshape(w_rows, n, q_cols), kv_w], -1).transpose(1, 0, 2)
    normed_all, qkv, qkv_w, gu_own, gain_a, gain_m = start_layer(
        n, reps, spread, tokens, gains, qkv_w, w_gate, w_up, cos_tab, sin_tab
    )
    normed_all = normed_all.reshape(group, width)
    qkv_w = qkv_w.reshape(width, q_cols + 2 * HD)
    if not spread:
        gate_up = jnp.stack([w.reshape(w_rows, n, ff_own).transpose(1, 0, 2) for w in (w_gate, w_up)], 1)
        gu_own = swap(gate_up).transpose(1, 0, 2, 3).reshape(1, 2, width, ff_own)
    q_in, kv, lse, att_t, attended = attention_forward(heads, long_len, qkv, *ranks)
    normed_mlp, middle, hidden, grads, gate_up, cot_all = mlp_forward(
        n, reps, spread, attended, w_out, tokens, gain_m, gu_own, cotangent, w_down
    )
    normed_mlp, cot_all = normed_mlp.reshape(group, width), cot_all.reshape(group, width)
    if not spread:
        gate_up = gu_own

    def over_replicas(x):
        return lax.psum_scatter(x, "replica", scatter_dimension=0, tiled=True)

    grad_mid, gml, grad_att, gain_m_sum, _, _, _, gate_q, up_q, down_q = middle_backward(
        n, spread, grads, gate_up, middle, cotangent, gain_m, w_out, normed_mlp, hidden, cot_all
    )
    down = dot(hidden, w_down).astype(BF16)
    grad_w_out = tdot(attended, gml.reshape(group, width)).astype(BF16)
    angles = pos_sorted.astype(F32)[None, :] * freqs[:, None]
    grad_qkv = attention_backward(
        heads, long_len, q_in, kv, lse, att_t, grad_att, *ranks, jnp.cos(angles), jnp.sin(angles)
    )
    down, grad_qkv, grad_w_out = lax.optimization_barrier((down, grad_qkv, grad_w_out))
    down = lax.psum_scatter(down, "fsdp", scatter_dimension=0, tiled=True)
    output = (middle + down.astype(F32)).astype(BF16)
    grad_w = tdot(normed_all, grad_qkv).astype(BF16)
    grad_w = grad_w.reshape(n, reps, w_rows // reps, -1).transpose(1, 0, 2, 3).reshape(reps, width // reps, -1)
    if not spread:

        def column_blocks(first):
            grad = tdot(normed_mlp, grads[:, first : first + ff_own]).astype(BF16)
            return grad.reshape(width, reps, ff_blk).transpose(1, 0, 2).reshape(reps * width, ff_blk)

        gate_q, up_q = over_replicas(column_blocks(0)), over_replicas(column_blocks(ff_own))
        down_q = over_replicas(tdot(hidden, cot_all).astype(BF16))
    grad_tokens, gain_grads, grad_gate, grad_up, grad_down, grad_qkv_w, grad_out_w = end_layer(
        n, reps, spread, grad_qkv, qkv_w, tokens, grad_mid, gain_a, gain_m_sum, gate_q, up_q, down_q, grad_w,
        grad_w_out.reshape(reps, q_cols // reps, width),
    )
    if not spread:

        def by_rows(grad):
            grad = swap(grad.reshape(n, w_rows, -1))
            grad = lax.all_gather(grad, "replica", axis=0, tiled=False)
            return grad.transpose(2, 1, 0, 3).reshape(w_rows, -1)

        grad_gate, grad_up = by_rows(gate_q), by_rows(up_q)
        grad_down = lax.all_gather(down_q, "replica", axis=0, tiled=True)
        grad_w = over_replicas(grad_w)[0].reshape(n, w_rows // reps, -1)
        grad_qkv_w = lax.all_gather(swap(grad_w), "replica", axis=0, tiled=False).transpose(1, 0, 2, 3)
        grad_out_w = lax.psum(grad_w_out, "replica")
    grad_w = grad_qkv_w.transpose(1, 2, 0, 3).reshape(w_rows, n, -1).astype(F32)
    grad_w_query = grad_w[:, :, :q_cols].reshape(w_rows, H * HD)
    grad_kv = grad_w[:, :, q_cols:].reshape(w_rows, KVH, dup, 2 * HD).sum(2)
    grad_w_key = grad_kv[:, :, :HD].reshape(w_rows, KVH * HD)
    grad_w_value = grad_kv[:, :, HD:].reshape(w_rows, KVH * HD)
    return (
        output,
        grad_tokens,
        gain_grads[0],
        grad_w_query,
        grad_w_key,
        grad_w_value,
        grad_out_w.astype(F32),
        gain_grads[1],
        grad_gate.astype(F32),
        grad_up.astype(F32),
        grad_down.astype(F32),
    )


def solution(mesh):
    both = P(("replica", "fsdp"), None)
    mat = P("fsdp", None)
    vec = P("fsdp")
    return jax.shard_map(
        body,
        mesh=mesh,
        in_specs=(both, P("replica"), P("replica"), vec, mat, mat, mat, mat, vec, mat, mat, mat, both),
        out_specs=(both, both, vec, mat, mat, mat, mat, vec, mat, mat, mat),
        check_vma=False,
    )
```

```python
import functools
import math

import jax
import jax.numpy as jnp
from jax import lax
from jax.experimental import pallas as pl
from jax.experimental.pallas import tpu as pltpu
from jax.sharding import PartitionSpec as P

H = 32
KVH = 8
HD = 64
EPSILON = 1e-05
ROPE_BASE = 500000.0
MASKED = -1e30
QBLK = 256
F32 = jnp.float32
BF16 = jnp.bfloat16
MESH = pl.DeviceIdType.MESH
VMEM = pl.BlockSpec(memory_space=pltpu.VMEM)
ANY = pl.BlockSpec(memory_space=pl.ANY)
DMA = pltpu.SemaphoreType.DMA
VMEM_BYTES = 60 * 2**20


def dot(a, b):
    return jnp.dot(a, b, preferred_element_type=F32)


def tdot(a, b):
    return lax.dot_general(a, b, (((0,), (0,)), ((), ())), preferred_element_type=F32)


def dot_t(a, b):
    return lax.dot_general(a, b, (((1,), (1,)), ((), ())), preferred_element_type=F32)


class Line:
    def __init__(self, n):
        f = lax.axis_index("fsdp")
        self.n = n
        self.replica = lax.axis_index("replica")
        self.chips = n // 2
        self.z = lax.div(f, 2)
        self.c = lax.rem(f, 2)
        self.me = f
        x, y = lax.rem(self.replica, 2), lax.div(self.replica, 2)
        self.xn, self.yn = self.replica + 1 - 2 * x, self.replica + 2 - 4 * y
        self.diag = 3 - self.replica

    def dev(self, z, c):
        return (self.replica, 2 * z + c)

    def other(self, i):
        return lax.rem(self.me + i, self.n)

    def enter(self, square=False):
        barrier = pltpu.get_barrier_semaphore()
        z, c = self.z, self.c

        def greet(device):
            pl.semaphore_signal(barrier, inc=1, device_id=device, device_id_type=MESH)

        greet(self.dev(z, 1 - c))

        @pl.when(z > 0)
        def _():
            greet(self.dev(z - 1, c))

        @pl.when(z < self.chips - 1)
        def _():
            greet(self.dev(z + 1, c))

        count = 1 + (z > 0).astype(jnp.int32) + (z < self.chips - 1).astype(jnp.int32)
        if square:
            greet((self.xn, self.me))
            greet((self.yn, self.me))
            count = count + 2
        pl.semaphore_wait(barrier, count)

    def enter_all(self, reps, square=False):
        barrier = pltpu.get_barrier_semaphore()

        def greet(device):
            pl.semaphore_signal(barrier, inc=1, device_id=device, device_id_type=MESH)

        for i in range(1, self.n):
            greet((self.replica, self.other(i)))
        if square:
            greet((self.xn, self.me))
            greet((self.yn, self.me))
        else:
            for i in range(1, reps):
                greet((lax.rem(self.replica + i, reps), self.me))
        pl.semaphore_wait(barrier, self.n - 1 + (2 if square else reps - 1))

    def far_first(self, s):
        z, last = self.z, self.chips - 1
        right = last - z
        low = jnp.where(s < right, last - s, s - right)
        high = jnp.where(s < z, s, last - (s - z))
        return jnp.where(2 * z < self.chips, low, high)

    def near_first(self, j):
        z, last = self.z, self.chips - 1
        short = jnp.minimum(z, last - z)
        half = lax.div(j + 1, 2)
        both = jnp.where(lax.rem(j, 2) == 1, z - half, z + half)
        rest = jnp.where(2 * z < self.chips, j, last - j)
        return jnp.where(j <= 2 * short, both, rest)


def remote(src, dst, send, recv, device):
    return pltpu.make_async_remote_copy(
        src_ref=src, dst_ref=dst, send_sem=send, recv_sem=recv, device_id=device, device_id_type=MESH
    )


def row_step(rows):
    return 32 if rows % 32 == 0 else 16


def row_chunks(rows, fn):
    step = row_step(rows)

    @pl.loop(0, rows // step)
    def _(i):
        fn(pl.ds(pl.multiple_of(i * step, step), step))


PARTS = 2


class Scatter:
    @staticmethod
    def scratch(n, rows, width):
        chips = n // 2
        return [
            pltpu.VMEM((n * rows, width), BF16),
            pltpu.VMEM((chips, rows, width), BF16),
            pltpu.VMEM((chips + 1, rows, width), BF16),
            pltpu.VMEM((rows, width), F32),
            DMA((chips,)),
            DMA((chips,)),
            DMA((chips, PARTS)),
            DMA((chips + 1, PARTS)),
        ]

    def __init__(self, line, scratch):
        self.line = line
        self.part, self.sib, self.rx, self.total = scratch[:4]
        self.sib_send, self.sib_recv, self.line_send, self.line_recv = scratch[4:]
        self.rows, self.width = self.total.shape
        self.rows_q = self.rows // PARTS

    def rows_at(self, d, c, first=0, count=None):
        at = (2 * d + c) * self.rows + first
        return pl.ds(pl.multiple_of(at, 16), self.rows if count is None else count)

    def to_sibling(self, d):
        line = self.line
        return remote(
            self.part.at[self.rows_at(d, 1 - line.c)], self.sib.at[d], self.sib_send.at[d], self.sib_recv.at[d], line.dev(line.z, 1 - line.c)
        )

    def along(self, d, slot, q, z):
        c = self.line.c
        at = pl.ds(q * self.rows_q, self.rows_q)
        return remote(
            self.part.at[self.rows_at(d, c, q * self.rows_q, self.rows_q)], self.rx.at[slot, at], self.line_send.at[d, q], self.line_recv.at[slot, q], self.line.dev(z, c)
        )

    def to_right(self, d, q):
        return self.along(d, d, q, self.line.z + 1)

    def to_left(self, d, q):
        z = self.line.z
        return self.along(d, jnp.where(d == z - 1, self.line.chips, d), q, z - 1)

    def wait_line(self, slot, q):
        line = self.line
        at = pl.ds(q * self.rows_q, self.rows_q)
        here = self.rx.at[slot, at]
        remote(here, here, self.line_send.at[0, q], self.line_recv.at[slot, q], line.dev(line.z, 1 - line.c)).wait_recv()

    def add(self, d, q, with_line):
        step = row_step(self.rows_q)
        c = self.line.c

        @pl.loop(0, self.rows_q // step)
        def _(i):
            at = pl.ds(pl.multiple_of(q * self.rows_q + i * step, step), step)
            here = self.rows_at(d, c, q * self.rows_q + i * step, step)
            value = self.part[here, :].astype(F32) + self.sib[d, at, :].astype(F32)
            if with_line:
                value = value + self.rx[d, at, :].astype(F32)
            self.part[here, :] = value.astype(BF16)

    def produce(self, compute, after_first=None, between=None):
        line = self.line
        chips, z = line.chips, line.z

        def step(s):
            d = line.far_first(s)
            compute(d)
            self.to_sibling(d).start()

            @pl.when(((z == 0) | (z == chips - 1)) & (s > 0))
            def _():
                before = line.far_first(s - 1)
                self.to_sibling(before).wait_recv()
                for q in range(PARTS):
                    self.add(before, q, False)

                    @pl.when(z == 0)
                    def _():
                        self.to_right(before, q).start()

                    @pl.when(z > 0)
                    def _():
                        self.to_left(before, q).start()

                if after_first is not None:

                    @pl.when(s == 1)
                    def _():
                        after_first()

        if between is None:
            pl.loop(0, chips)(step)
        else:
            for s in range(chips):
                step(s)
                between(s)

    def duty(self, s):
        chips, z, c = self.line.chips, self.line.z, self.line.c
        for near in (True, False):
            right = (2 * z < chips) if near else (2 * z >= chips)
            d = jnp.where(right, chips - 1 - s, s)
            active = jnp.where(right, (z > 0) & (d > z), (z < chips - 1) & (d < z))

            @pl.when(active)
            def _():
                self.to_sibling(d).wait_recv()
                for q in range(PARTS):
                    self.wait_line(d, q)
                    self.add(d, q, True)
                    slot = jnp.where(~right & (d == z - 1), chips, d)
                    self.along(d, slot, q, jnp.where(right, z + 1, z - 1)).start()

    def own_sum(self):
        chips, z, c = self.line.chips, self.line.z, self.line.c
        total, rx = self.total, self.rx
        self.to_sibling(z).wait_recv()
        for q in range(PARTS):

            @pl.when(z > 0)
            def _():
                self.wait_line(z, q)

            @pl.when(z < chips - 1)
            def _():
                self.wait_line(chips, q)

        def add_up(at):
            total[at, :] = self.part[self.rows_at(z, c, at.start, at.size), :].astype(F32) + self.sib[z, at, :].astype(F32)

            @pl.when(z > 0)
            def _():
                total[at, :] += rx[z, at, :].astype(F32)

            @pl.when(z < chips - 1)
            def _():
                total[at, :] += rx[chips, at, :].astype(F32)

        row_chunks(self.rows, add_up)

    def finish(self):
        z = self.line.z

        @pl.loop(0, self.line.chips)
        def _(d):
            self.to_sibling(d).wait_send()
            for q in range(PARTS):

                @pl.when(d > z)
                def _():
                    self.to_right(d, q).wait_send()

                @pl.when(d < z)
                def _():
                    self.to_left(d, q).wait_send()


class Gather:
    @staticmethod
    def scratch(n):
        return [DMA((3, n)), DMA((n,)), DMA(())]

    def __init__(self, line, own, buf, scratch):
        self.line, self.own, self.buf = line, own, buf
        self.send, self.recv, self.local_sem = scratch

    def copy(self, way, slot, mine=False):
        line, z, c = self.line, self.line.z, self.line.c
        src = self.own if mine else self.buf.at[slot]
        device = (line.dev(z, 1 - c), line.dev(z + 1, c), line.dev(z - 1, c))[way]
        return remote(src, self.buf.at[slot], self.send.at[way, slot], self.recv.at[slot], device)

    def local(self):
        return pltpu.make_async_copy(self.own, self.buf.at[self.line.me], self.local_sem)

    def along(self, at, mine=False):
        z, slot = self.line.z, 2 * at + self.line.c

        @pl.when((z < self.line.chips - 1) & (at <= z))
        def _():
            self.copy(1, slot, mine).start()

        @pl.when((z > 0) & (at >= z))
        def _():
            self.copy(2, slot, mine).start()

    def pass_on(self, at, mine=False):
        self.along(at, mine)
        self.copy(0, 2 * at + self.line.c, mine).start()

    def start(self, ends_later=False):
        line = self.line
        if ends_later:

            @pl.when((line.z > 0) & (line.z < line.chips - 1))
            def _():
                self.along(line.z, True)

            self.copy(0, line.me, True).start()
        else:
            self.pass_on(line.z, True)
        self.local().start()

    def start_ends(self):
        self.along(self.line.z, True)

    def arrive(self, t, sides=(True, False)):
        z, chips = self.line.z, self.line.chips
        for far in sides:
            at = jnp.where((2 * z < chips) == far, z + t, z - t)
            there = (at >= 0) & (at < chips)

            @pl.when(there)
            def _():
                self.copy(0, 2 * at + self.line.c).wait_recv()
                self.pass_on(at)

    def ready(self, j):
        at = self.line.near_first(j)
        if isinstance(j, int):
            if j == 0:
                self.local().wait()
        else:

            @pl.when(j == 0)
            def _():
                self.local().wait()

        self.copy(0, 2 * at + 1 - self.line.c).wait_recv()
        return at

    def finish(self):
        z = self.line.z

        @pl.loop(0, self.line.chips)
        def _(at):
            slot = 2 * at + self.line.c
            self.copy(0, slot).wait_send()

            @pl.when((z < self.line.chips - 1) & (at <= z))
            def _():
                self.copy(1, slot).wait_send()

            @pl.when((z > 0) & (at >= z))
            def _():
                self.copy(2, slot).wait_send()


def load(src, dst, sem):
    copy = pltpu.make_async_copy(src, dst, sem)
    copy.start()
    copy.wait()


def rows_of(z, rows):
    return pl.ds(pl.multiple_of(z * 2 * rows, 2 * rows), 2 * rows)


class Square:
    @staticmethod
    def scratch(units, tiles):
        return [DMA((units, 2, tiles)), DMA((units, 2, tiles)), DMA((units,)), DMA((units,)), DMA(())]

    def __init__(self, line, units, scratch):
        self.line, self.units = line, units
        self.send1, self.recv1, self.send2, self.recv2, self.sem = scratch
        self.tiles = self.send1.shape[2]

    def ways(self, u):
        line = self.line
        return (line.xn, line.yn) if self.units[u]["x_first"] else (line.yn, line.xn)

    def whole(self, u, block):
        unit = self.units[u]
        return unit["parts"].at[block, pl.ds(unit["row"], unit["rows"])]

    def first(self, u, slot, t):
        unit = self.units[u]
        one, _ = self.ways(u)
        block = one if slot == 0 else self.line.diag
        src, dst = self.whole(u, block), unit["land1"].at[slot]
        if self.tiles > 1:
            axis = unit["axis"]
            step = dst.shape[axis] // self.tiles
            at = (pl.ds(t * step, step),) if axis == 0 else (slice(None), pl.ds(t * step, step))
            src, dst = src.at[at], dst.at[at]
        return remote(src, dst, self.send1.at[u, slot, t], self.recv1.at[u, slot, t], (one, self.line.me))

    def start(self, u, t=0):
        for slot in range(2):
            self.first(u, slot, t).start()

    def add(self, u, slot, block, also=None):
        unit = self.units[u]
        for t in range(self.tiles):
            self.first(u, slot, t).wait_recv()
        land, tmp = unit["land1"], unit["tmp"].at[pl.ds(0, unit["rows"])]
        load(self.whole(u, block), tmp, self.sem)

        def one(at):
            value = land[slot, at, :].astype(F32) + tmp[at, :].astype(F32)
            if also is not None:
                value = value + also[at, :].astype(F32)
            land[slot, at, :] = value.astype(BF16)

        row_chunks(unit["rows"], one)

    def second(self, u):
        unit = self.units[u]
        _, two = self.ways(u)
        return remote(unit["land1"].at[1], unit["land2"], self.send2.at[u], self.recv2.at[u], (two, self.line.me))

    def fold(self, u):
        self.add(u, 1, self.ways(u)[1])
        self.second(u).start()

    def result(self, u):
        self.second(u).wait_recv()
        self.add(u, 0, self.line.replica, self.units[u]["land2"])

    def finish(self):
        for u in range(len(self.units)):
            self.second(u).wait_send()
            for slot in range(2):
                for t in range(self.tiles):
                    self.first(u, slot, t).wait_send()


def key_range(block, long_len):
    longs = long_len // QBLK
    return (0, block + 1, False) if block < longs else (longs, block + 1 - longs, True)


def score_mask(q_block, k_block, seg_row, seg_col, heads, compare):
    visible = None
    shape = (QBLK, QBLK)
    if q_block == k_block:
        visible = lax.broadcasted_iota(jnp.int32, shape, 0) <= lax.broadcasted_iota(jnp.int32, shape, 1)
    if compare:
        k_at, q_at = k_block * QBLK, q_block * QBLK
        same = seg_col[k_at : k_at + QBLK, :] == seg_row[:, q_at : q_at + QBLK]
        visible = same if visible is None else visible & same
    if visible is None:
        return None
    bias = jnp.where(visible, 0.0, MASKED)
    return jnp.concatenate([bias] * heads, 1)


def one_hot_rows(rank_row, start):
    group = rank_row.shape[1]
    places = start + lax.broadcasted_iota(jnp.int32, (QBLK, group), 0)
    return jnp.where(rank_row[...] == places, 1.0, 0.0).astype(BF16)


def one_hot_back(rank_col, start):
    group = rank_col.shape[0]
    places = lax.broadcasted_iota(jnp.int32, (QBLK, group), 1)
    return jnp.where(rank_col[pl.ds(start, QBLK), :] == places, 1.0, 0.0).astype(BF16)


def attention_kernel(heads, long_len, qkv, rank_row, rank_col, seg_row, seg_col, q_out, kv_out, lse, att_t, att, s_buf, v_t):
    group = qkv.shape[0]
    q_cols = heads * HD
    n_blocks = group // QBLK
    for b in range(n_blocks):
        ordered = dot(one_hot_rows(rank_row, b * QBLK), qkv[...])
        for h in range(heads):
            q_out[b, h * QBLK : (h + 1) * QBLK, :] = (ordered[:, h * HD : (h + 1) * HD] * 0.125).astype(BF16)
        kv_out[0, b * QBLK : (b + 1) * QBLK, :] = ordered[:, q_cols : q_cols + HD].astype(BF16)
        values = ordered[:, q_cols + HD :]
        kv_out[1, b * QBLK : (b + 1) * QBLK, :] = values.astype(BF16)
        v_t[:, b * QBLK : (b + 1) * QBLK] = values.T.astype(BF16)
    for b in range(n_blocks):
        first, count, compare = key_range(b, long_len)
        queries = q_out[b]
        top = None
        for i in range(count):
            k_at = (first + i) * QBLK
            scores = dot_t(kv_out[0, k_at : k_at + QBLK, :], queries)
            bias = score_mask(b, first + i, seg_row, seg_col, heads, compare)
            if bias is not None:
                scores = scores + bias
            s_buf[i] = scores
            high = jnp.max(scores, 0, keepdims=True)
            top = high if top is None else jnp.maximum(top, high)
        total, out = 0.0, 0.0
        for i in range(count):
            k_at = (first + i) * QBLK
            terms = jnp.exp(s_buf[i] - top)
            total = total + jnp.sum(terms, 0, keepdims=True)
            out = out + dot(v_t[:, k_at : k_at + QBLK], terms.astype(BF16))
        lse[b] = top + jnp.log(total)
        out = out / total
        for h in range(heads):
            att_t[h * HD : (h + 1) * HD, b * QBLK : (b + 1) * QBLK] = out[:, h * QBLK : (h + 1) * QBLK]
    low = att_t[...].astype(BF16)

    @pl.loop(0, n_blocks)
    def _(b):
        at = pl.multiple_of(b * QBLK, QBLK)
        att[pl.ds(at, QBLK), :] = dot_t(one_hot_back(rank_col, at), low).astype(BF16)


def attention_back_kernel(
    heads, long_len, q_in, kv, lse, att_t, grad_att, rank_row, rank_col, seg_row, seg_col, cos_t, sin_t, out,
    grad_kv, grad_t, k_t, go_rows, go_t, after_block,
):
    group = kv.shape[1]
    n_blocks = group // QBLK
    half = HD // 2
    q_cols = heads * HD
    for b in range(n_blocks):
        at = b * QBLK
        ordered = dot(one_hot_rows(rank_row, at), grad_att[...])
        for h in range(heads):
            go_rows[b, h * QBLK : (h + 1) * QBLK, :] = ordered[:, h * HD : (h + 1) * HD].astype(BF16)
        go_t[:, at : at + QBLK] = ordered.T
        k_t[:, at : at + QBLK] = kv[0, at : at + QBLK, :].astype(F32).T.astype(BF16)
    grad_kv[...] = jnp.zeros_like(grad_kv)
    for b in range(n_blocks):
        first, count, compare = key_range(b, long_len)
        q_at = b * QBLK
        queries, grad_rows = q_in[b], go_rows[b]
        centre = jnp.concatenate(
            [
                jnp.sum(
                    go_t[h * HD : (h + 1) * HD, q_at : q_at + QBLK] * att_t[h * HD : (h + 1) * HD, q_at : q_at + QBLK],
                    0,
                    keepdims=True,
                )
                for h in range(heads)
            ],
            1,
        )
        grad_q = 0.0
        for i in range(count):
            k_at = (first + i) * QBLK
            scores = dot_t(kv[0, k_at : k_at + QBLK, :], queries)
            bias = score_mask(b, first + i, seg_row, seg_col, heads, compare)
            if bias is not None:
                scores = scores + bias
            probs = jnp.exp(scores - lse[b])
            grad_probs = dot_t(kv[1, k_at : k_at + QBLK, :], grad_rows)
            grad_scores = (probs * (grad_probs - centre)).astype(BF16)
            grad_kv[0, k_at : k_at + QBLK, :] += dot(grad_scores, queries)
            grad_kv[1, k_at : k_at + QBLK, :] += dot(probs.astype(BF16), grad_rows)
            grad_q = grad_q + dot(k_t[:, k_at : k_at + QBLK], grad_scores)
        cos_b, sin_b = cos_t[:, q_at : q_at + QBLK], sin_t[:, q_at : q_at + QBLK]

        def turned(value):
            front, back = value[:half], value[half:]
            return jnp.concatenate([front * cos_b + back * sin_b, back * cos_b - front * sin_b], 0).astype(BF16)

        for h in range(heads):
            grad_t[h * HD : (h + 1) * HD, q_at : q_at + QBLK] = turned(grad_q[:, h * QBLK : (h + 1) * QBLK] * 0.125)
        after_block(b)
    for b in range(n_blocks):
        at = b * QBLK
        cos_b, sin_b = cos_t[:, at : at + QBLK], sin_t[:, at : at + QBLK]
        value = grad_kv[0, at : at + QBLK, :].T
        front, back = value[:half], value[half:]
        grad_t[q_cols : q_cols + half, at : at + QBLK] = (front * cos_b + back * sin_b).astype(BF16)
        grad_t[q_cols + half : q_cols + HD, at : at + QBLK] = (back * cos_b - front * sin_b).astype(BF16)
        grad_t[q_cols + HD :, at : at + QBLK] = grad_kv[1, at : at + QBLK, :].T.astype(BF16)

    @pl.loop(0, n_blocks)
    def _(b):
        at = pl.multiple_of(b * QBLK, QBLK)
        out[pl.ds(at, QBLK), :] = dot_t(one_hot_back(rank_col, at), grad_t[...]).astype(BF16)


def order_group(long_len, ids, ids_col, rank_row, rank_col, seg_row_out, seg_col_out, pos_out, key_col, acc):
    group = ids.shape[1]
    seg_row, pos_row = ids.at[0:1, :], ids.at[1:2, :]

    def chunks(fn):
        @pl.loop(0, group // QBLK)
        def _(i):
            fn(pl.multiple_of(i * QBLK, QBLK))

    def ones(mask):
        return jnp.where(mask, 1.0, 0.0)

    acc[...] = jnp.zeros_like(acc)

    def lengths(at):
        here = pl.ds(at, QBLK)
        same = ones(ids_col[here, 0:1] == seg_row[...])
        acc[0:1, :] += jnp.sum(same, 0, keepdims=True)
        first = jnp.sum(same, 1, keepdims=True) == float(long_len)
        key_col[here, :] = jnp.where(first, -1.0, ids_col[here, 0:1]) * float(group) + ids_col[here, 1:2]

    chunks(lengths)
    key_row = jnp.where(acc[0:1, :] == float(long_len), -1.0, seg_row[...]) * float(group)
    acc[1:2, :] = key_row + pos_row[...]

    def ranks(at):
        here = pl.ds(at, QBLK)
        mine, others = key_col[here, :], acc[1:2, :]
        rank_col[here, :] = jnp.sum(ones(others < mine), 1, keepdims=True).astype(jnp.int32)
        acc[2:3, :] += jnp.sum(ones(mine < others), 0, keepdims=True)

    chunks(ranks)
    rank_row[...] = acc[2:3, :].astype(jnp.int32)

    def ordered(at):
        here = pl.ds(at, QBLK)
        places = at + lax.broadcasted_iota(jnp.int32, (QBLK, group), 0)
        seg = jnp.sum(jnp.where(rank_row[...] == places, seg_row[...], 0.0), 1, keepdims=True)
        seg_col_out[here, :] = seg.astype(jnp.int32)
        moved = rank_col[here, :] == lax.broadcasted_iota(jnp.int32, (QBLK, group), 1)
        acc[3:4, :] += jnp.sum(jnp.where(moved, ids_col[here, 0:1], 0.0), 0, keepdims=True)
        acc[4:5, :] += jnp.sum(jnp.where(moved, ids_col[here, 1:2], 0.0), 0, keepdims=True)

    chunks(ordered)
    seg_row_out[...] = acc[3:4, :].astype(jnp.int32)
    pos_out[...] = acc[4:5, :]


def frequencies(index):
    return jnp.exp(-math.log(ROPE_BASE) * index.astype(F32) * (2.0 / HD))


def start_kernel(
    n, reps, spread, heads, long_len, tok, gains, ids, wqkv, wg, wu,
    q_out, kv_out, lse, att_t, att, rank_row, rank_col, seg_row_out, seg_col_out, cos_back, sin_back, gain_a, gain_m,
    normed, w_all, gu_own,
    gains_buf, own, wv, blk, qkv, cos, sin, ids_col, key_col, acc, pos_out, s_buf, v_t,
    g_send, g_recv, a_send, a_recv, r_send, r_recv, u_send, u_recv, local_sem, load_sem, *ag_scratch,
):
    line = Line(n)
    me, rep = line.me, line.replica
    rows, width = tok.shape
    w_rows = gains.shape[1]
    fb = gu_own.shape[-1]
    own_cols = fb * reps
    line.enter_all(reps)

    def gain_copy(i, to, slot):
        return remote(gains, gains_buf.at[slot], g_send.at[i], g_recv.at[slot], (rep, to))

    def qkv_copy(i, to, slot):
        piece = wqkv.at[to, pl.ds(rep * (w_rows // reps), w_rows // reps)]
        return remote(piece, w_all.at[slot, rep], a_send.at[i], a_recv.at[slot], (rep, to))

    def gu_copy(k, to, slot):
        piece = (wg, wu)[k].at[:, pl.ds(pl.multiple_of(to * own_cols + rep * fb, 128), fb)]
        at = pl.ds(pl.multiple_of(slot * w_rows, 16), w_rows)
        return remote(piece, gu_own.at[k, at], u_send.at[k, to], u_recv.at[k, slot], (rep, to))

    def spread_weights(stage):
        if not spread:
            return
        if stage == 0:
            for k in range(2):
                gu_copy(k, 2 * line.z + 1 - line.c, me).start()
            return
        last = line.chips - 1

        @pl.loop(1, line.chips)
        def _(d):
            for to in (line.z + d, line.z - d):
                to_end = (to == 0) | (to == last)
                next_to_end = ((line.z == 0) | (line.z == last)) & (d == 1)
                now = (to_end, (~to_end) & next_to_end, (~to_end) & (~next_to_end))[stage % 3]

                @pl.when((to >= 0) & (to <= last) & now)
                def _():
                    for core in range(2):
                        for k in range(2):
                            gu_copy(k, 2 * to + core, me).start()

    for i in range(1, n):
        gain_copy(i, line.other(i), me).start()
    for i in range(1, n):
        qkv_copy(i, line.other(i), me).start()
    mine = [
        pltpu.make_async_copy(
            wqkv.at[me, pl.ds(rep * (w_rows // reps), w_rows // reps)], w_all.at[me, rep], local_sem.at[0]
        )
    ]
    if spread:
        for k in range(2):
            piece = (wg, wu)[k].at[:, pl.ds(pl.multiple_of(me * own_cols + rep * fb, 128), fb)]
            at = pl.ds(pl.multiple_of(me * w_rows, 16), w_rows)
            mine.append(pltpu.make_async_copy(piece, gu_own.at[k, at], local_sem.at[1 + k]))
    for copy in mine:
        copy.start()
    gains_buf[me] = gains[...]
    for i in range(1, n):
        gain_copy(i, me, line.other(i)).wait_recv()
    gain_a[...] = jnp.concatenate([gains_buf[i, 0:1, :].astype(F32) for i in range(n)], 1)
    gain_m[...] = jnp.concatenate([gains_buf[i, 1:2, :].astype(F32) for i in range(n)], 1)

    def norm(at):
        resid = tok[at, :].astype(F32)
        inverse = lax.rsqrt(jnp.mean(resid * resid, -1, keepdims=True) + EPSILON)
        own[at, :] = (resid * inverse * gain_a[...]).astype(BF16)

    row_chunks(rows, norm)
    gather = Gather(line, own, normed, ag_scratch)
    gather.start()
    spread_weights(0)
    for at in range(0, ids.shape[1], QBLK):
        ids_col[at : at + QBLK, :] = ids[:, at : at + QBLK].T
    order_group(long_len, ids, ids_col, rank_row, rank_col, seg_row_out, seg_col_out, pos_out, key_col, acc)
    for i in range(1, n):
        qkv_copy(i, me, line.other(i)).wait_recv()
    mine[0].wait()

    def share(i, to, slot):
        return remote(w_all.at[:, slot], w_all.at[:, slot], r_send.at[i], r_recv.at[slot], (to, me))

    for i in range(1, reps):
        share(i, lax.rem(rep + i, reps), rep).start()
    lanes = lax.broadcasted_iota(jnp.int32, (1, 128), 1)
    freq = frequencies(lax.rem(lanes, HD // 2))
    sign = jnp.where(lax.rem(lanes, HD) < HD // 2, -1.0, 1.0)

    def table(at):
        angles = ids_col[at, 1:2] * freq
        cos[at, :] = jnp.cos(angles)
        sin[at, :] = jnp.sin(angles) * sign

    row_chunks(ids_col.shape[0], table)
    gather.arrive(1)
    spread_weights(1)
    angles = frequencies(lax.broadcasted_iota(jnp.int32, (HD // 2, 1), 0)) * pos_out[...]
    cos_back[...] = jnp.cos(angles)
    sin_back[...] = jnp.sin(angles)
    for i in range(1, reps):
        share(i, rep, lax.rem(rep + i, reps)).wait_recv()
    load(w_all, wv, load_sem)
    cols = wv.shape[-1]
    lane = lax.broadcasted_iota(jnp.int32, (2 * rows, 128), 1)
    front = lax.rem(lane, HD) < HD // 2

    def project(j):
        z = gather.ready(j)
        load(normed.at[pl.ds(2 * z, 2)], blk, load_sem)
        at = rows_of(z, rows)
        raw = dot(blk[...].reshape(2 * rows, width), wv[...].reshape(width, cols))
        for t in range(0, cols, 128):
            part = raw[:, t : t + 128]
            cos_t, sin_t = cos[at, :], sin[at, :]
            if t == cols - 128:
                cos_t, sin_t = jnp.where(lane < HD, cos_t, 1.0), jnp.where(lane < HD, sin_t, 0.0)
            partner = jnp.where(front, pltpu.roll(part, 128 - HD // 2, 1), pltpu.roll(part, HD // 2, 1))
            qkv[at, t : t + 128] = (part * cos_t + partner * sin_t).astype(BF16)

    project(0)
    gather.arrive(2)
    spread_weights(2)

    @pl.loop(1, line.chips)
    def _(j):
        @pl.when(j + 2 < line.chips)
        def _():
            gather.arrive(j + 2)

        project(j)

    spread_weights(3)
    attention_kernel(
        heads, long_len, qkv, rank_row, rank_col, seg_row_out, seg_col_out, q_out, kv_out, lse, att_t, att, s_buf, v_t
    )
    for i in range(1, n):
        gain_copy(i, line.other(i), me).wait_send()
        qkv_copy(i, line.other(i), me).wait_send()
    for i in range(1, reps):
        share(i, lax.rem(rep + i, reps), rep).wait_send()
    if spread:
        for k in range(2):
            mine[1 + k].wait()
            for i in range(1, n):
                gu_copy(k, line.other(i), me).wait_send()
                gu_copy(k, me, line.other(i)).wait_recv()
    gather.finish()


def start_layer(n, reps, spread, heads, long_len, tok, gains, ids, wqkv, wg, wu):
    rows, width = tok.shape
    w_rows = gains.shape[1]
    cols = wqkv.shape[-1]
    group = ids.shape[1]
    n_blocks = group // QBLK
    fb = wg.shape[1] // n // reps
    return pl.pallas_call(
        functools.partial(start_kernel, n, reps, spread, heads, long_len),
        name="start_layer",
        out_shape=(
            jax.ShapeDtypeStruct((n_blocks, heads * QBLK, HD), BF16),
            jax.ShapeDtypeStruct((2, group, HD), BF16),
            jax.ShapeDtypeStruct((n_blocks, 1, heads * QBLK), F32),
            jax.ShapeDtypeStruct((heads * HD, group), F32),
            jax.ShapeDtypeStruct((group, heads * HD), BF16),
            jax.ShapeDtypeStruct((1, group), jnp.int32),
            jax.ShapeDtypeStruct((group, 1), jnp.int32),
            jax.ShapeDtypeStruct((1, group), jnp.int32),
            jax.ShapeDtypeStruct((group, 1), jnp.int32),
            jax.ShapeDtypeStruct((HD // 2, group), F32),
            jax.ShapeDtypeStruct((HD // 2, group), F32),
            jax.ShapeDtypeStruct((1, width), F32),
            jax.ShapeDtypeStruct((1, width), F32),
            jax.ShapeDtypeStruct((n, rows, width), BF16),
            jax.ShapeDtypeStruct((n, reps, w_rows // reps, cols), BF16),
            jax.ShapeDtypeStruct((2, width, fb), BF16),
        ),
        in_specs=[VMEM] * 3 + [ANY] * 3,
        out_specs=(VMEM,) * 13 + (ANY,) * 3,
        scratch_shapes=[
            pltpu.VMEM((n, 16, w_rows), BF16),
            pltpu.VMEM((rows, width), BF16),
            pltpu.VMEM((n, reps, w_rows // reps, cols), BF16),
            pltpu.VMEM((2, rows, width), BF16),
            pltpu.VMEM((group, cols), BF16),
            pltpu.VMEM((group, 128), F32),
            pltpu.VMEM((group, 128), F32),
            pltpu.VMEM((group, 8), F32),
            pltpu.VMEM((group, 1), F32),
            pltpu.VMEM((8, group), F32),
            pltpu.VMEM((1, group), F32),
            pltpu.VMEM((long_len // QBLK, QBLK, heads * QBLK), F32),
            pltpu.VMEM((HD, group), BF16),
            DMA((n,)),
            DMA((n,)),
            DMA((n,)),
            DMA((n,)),
            DMA((reps,)),
            DMA((reps,)),
            DMA((2, n)),
            DMA((2, n)),
            DMA((3,)),
            DMA(()),
        ]
        + Gather.scratch(n),
        compiler_params=pltpu.CompilerParams(collective_id=4, has_side_effects=True, vmem_limit_bytes=VMEM_BYTES),
        cost_estimate=pl.CostEstimate(flops=2 * group * width * cols, bytes_accessed=300 * 2**20, transcendentals=0),
    )(tok, gains, ids, wqkv, wg, wu)


def weight_copies(gu, wbuf, w_sem):
    blocks, _, _, fb = gu.shape
    own = blocks * fb

    def copy(b, k):
        at = k * own + b * fb
        if not isinstance(at, int):
            at = pl.multiple_of(at, 128)
        return pltpu.make_async_copy(gu.at[b, k], wbuf.at[:, pl.ds(at, fb)], w_sem.at[k, b])

    return copy


def mlp_kernel(
    n, blocks, spread, att, wo, tok, gain, gu_in, cot, wd, normed, middle, hidden, grads, gu_out, cot_all, *scratch
):
    scatter_scratch, scratch = scratch[:8], scratch[8:]
    ag_scratch, cot_scratch, scratch = scratch[:3], scratch[3:6], scratch[6:]
    own_normed, blk, wbuf, wd_buf, grad_hid, hid_stage, grad_stage, w_sem, out_sem, load_sem, x_send, x_recv = scratch
    line = Line(n)
    rows, width = tok.shape
    fb = gu_in.shape[-1]
    own = blocks * fb
    rep = line.replica
    scatter = Scatter(line, scatter_scratch)
    cots = Gather(line, cot, cot_all, cot_scratch)
    gather = Gather(line, own_normed, normed, ag_scratch)
    wd_copy = pltpu.make_async_copy(wd, wd_buf, load_sem.at[1])
    wd_copy.start()
    line.enter(spread)
    cots.start(True)
    if spread:
        gu = gu_out

        def gu_copy(way, k, src, slot, device):
            return remote(src, gu.at[slot, k], x_send.at[way, k], x_recv.at[way, k], (device, line.me))

        firsts = [(0, 0, line.xn), (1, 1, line.yn), (0, 1, line.xn), (1, 0, line.yn)]
        for way, k, device in firsts[:2]:
            gu_copy(way, k, gu_in.at[k], rep, device).start()
        for k in range(2):
            pltpu.make_async_copy(gu_in.at[k], wbuf.at[:, pl.ds(pl.multiple_of(k * own + rep * fb, 128), fb)], w_sem.at[k, rep]).start()
            pltpu.make_async_copy(gu_in.at[k], gu.at[rep, k], load_sem.at[2 + k]).start()
    else:
        gu = gu_in
    weight_copy = weight_copies(gu, wbuf, w_sem)
    if not spread:
        for b in range(blocks):
            for k in range(2):
                weight_copy(b, k).start()

    def out_part(d):
        x = att[rows_of(d, rows), :]
        for t in range(0, width, 512):
            part = dot(x, wo[:, t : t + 512]).astype(BF16)
            scatter.part[rows_of(d, rows), t : t + 512] = part

    scatter.produce(out_part, cots.start_ends)
    wd_copy.wait()

    def grad_hidden(j):
        z = cots.ready(j)
        load(cot_all.at[pl.ds(2 * z, 2)], blk, load_sem.at[0])
        x = blk[...].reshape(2 * rows, width)
        tile = min(256, own)
        for t in range(0, own, tile):
            grad_hid[rows_of(z, rows), t : t + tile] = dot_t(x, wd_buf[t : t + tile, :]).astype(BF16)

    cots.arrive(1, (True,))
    if spread:
        for way, k, device in firsts[2:]:
            gu_copy(way, k, gu_in.at[k], rep, device).start()
    scatter.duty(0)
    cots.arrive(1, (False,))
    grad_hidden(0)
    if spread:
        for way, k, slot, device in ((0, 0, line.xn, line.yn), (1, 1, line.yn, line.xn)):
            gu_copy(way, k, gu.at[slot, k], slot, device).wait_recv()
            gu_copy(2 + way, k, gu.at[slot, k], slot, device).start()
            weight_copy(slot, k).start()

    @pl.loop(1, line.chips - 2)
    def _(s):
        scatter.duty(s)
        cots.arrive(s + 1)
        grad_hidden(s)

    scatter.duty(line.chips - 2)
    scatter.own_sum()

    def norm(at):
        mid = tok[at, :].astype(F32) + scatter.total[at, :]
        middle[at, :] = mid
        inverse = lax.rsqrt(jnp.mean(mid * mid, -1, keepdims=True) + EPSILON)
        own_normed[at, :] = (mid * inverse * gain[...]).astype(BF16)

    row_chunks(rows, norm)
    gather.start()
    cots.arrive(line.chips - 1)
    grad_hidden(line.chips - 2)
    grad_hidden(line.chips - 1)
    if spread:
        for way, k, slot in ((0, 1, line.xn), (1, 0, line.yn)):
            gu_copy(way, k, gu.at[slot, k], slot, line.xn).wait_recv()
            weight_copy(slot, k).start()
        for way, k, device in ((2, 0, line.yn), (3, 1, line.xn)):
            gu_copy(way, k, gu.at[line.diag, k], line.diag, device).wait_recv()
            weight_copy(line.diag, k).start()
    for b in range(blocks):
        for k in range(2):
            weight_copy(b, k).wait()

    def out_copies(z):
        at = rows_of(z, rows)
        return (
            pltpu.make_async_copy(hid_stage, hidden.at[at], out_sem.at[0]),
            pltpu.make_async_copy(grad_stage, grads.at[at], out_sem.at[1]),
        )

    @pl.loop(0, line.chips)
    def _(j):
        @pl.when(j > 0)
        def _():
            gather.arrive(j)

        z = gather.ready(j)
        load(normed.at[pl.ds(2 * z, 2)], blk, load_sem.at[0])

        @pl.when(j > 0)
        def _():
            for copy in out_copies(line.near_first(j - 1)):
                copy.wait()

        at = rows_of(z, rows)
        x = blk[...].reshape(2 * rows, width)
        tile = min(256, own)
        for t in range(0, own, tile):
            gate = dot(x, wbuf[:, t : t + tile])
            up = dot(x, wbuf[:, own + t : own + t + tile])
            sig = 1.0 / (1.0 + jnp.exp(-gate))
            gated = gate * sig
            gh = grad_hid[at, t : t + tile].astype(F32)
            hid_stage[:, t : t + tile] = (gated * up).astype(BF16)
            grad_stage[:, t : t + tile] = (gh * up * sig * (1.0 + gate * (1.0 - sig))).astype(BF16)
            grad_stage[:, own + t : own + t + tile] = (gh * gated).astype(BF16)
        for copy in out_copies(z):
            copy.start()

    for copy in out_copies(line.near_first(line.chips - 1)):
        copy.wait()
    if spread:
        for k in range(2):
            pltpu.make_async_copy(gu_in.at[k], gu.at[rep, k], load_sem.at[2 + k]).wait()
        for way, k, device in firsts:
            gu_copy(way, k, gu_in.at[k], rep, device).wait_send()
        for way, k, slot, device in ((2, 0, line.xn, line.yn), (3, 1, line.yn, line.xn)):
            gu_copy(way, k, gu.at[slot, k], slot, device).wait_send()
    scatter.finish()
    cots.finish()
    gather.finish()


def mlp_forward(n, reps, spread, att, wo, tok, gain, gu, cot, wd):
    rows, width = tok.shape
    group = att.shape[0]
    fb = gu.shape[-1]
    blocks = reps if spread else gu.shape[0]
    own = blocks * fb
    kept = (blocks, 2, width, fb) if spread else (1, 16, 128)
    return pl.pallas_call(
        functools.partial(mlp_kernel, n, blocks, spread),
        name="mlp_forward",
        out_shape=(
            jax.ShapeDtypeStruct((n, rows, width), BF16),
            jax.ShapeDtypeStruct((rows, width), F32),
            jax.ShapeDtypeStruct((group, own), BF16),
            jax.ShapeDtypeStruct((group, 2 * own), BF16),
            jax.ShapeDtypeStruct(kept, BF16),
            jax.ShapeDtypeStruct((n, rows, width), BF16),
        ),
        in_specs=[VMEM, VMEM, VMEM, VMEM, ANY, VMEM, ANY],
        out_specs=(ANY, VMEM, ANY, ANY, ANY, ANY),
        scratch_shapes=Scatter.scratch(n, rows, width)
        + Gather.scratch(n)
        + Gather.scratch(n)
        + [
            pltpu.VMEM((rows, width), BF16),
            pltpu.VMEM((2, rows, width), BF16),
            pltpu.VMEM((width, 2 * own), BF16),
            pltpu.VMEM((own, width), BF16),
            pltpu.VMEM((group, own), BF16),
            pltpu.VMEM((2 * rows, own), BF16),
            pltpu.VMEM((2 * rows, 2 * own), BF16),
            DMA((2, blocks)),
            DMA((2,)),
            DMA((4,)),
            DMA((4, 2)),
            DMA((4, 2)),
        ],
        compiler_params=pltpu.CompilerParams(collective_id=1, has_side_effects=True, vmem_limit_bytes=VMEM_BYTES),
        cost_estimate=pl.CostEstimate(flops=2 * group * width * own * 3, bytes_accessed=400 * 2**20, transcendentals=0),
    )(att, wo, tok, gain, gu, cot, wd)


def norm_back(grad_normed, resid, gain):
    inverse = lax.rsqrt(jnp.mean(resid * resid, -1, keepdims=True) + EPSILON)
    unit = resid * inverse
    scaled = grad_normed * gain
    return inverse * (scaled - unit * jnp.mean(scaled * unit, -1, keepdims=True)), grad_normed * unit


def middle_kernel(
    n, blocks, spread, grads_in, gu, mid, cot, gain, wo, normed, hidden, cot_all, wd, grad_mid, gml, grad_att, gain_sum, output,
    gate_parts, up_parts, down_parts, gate_q, up_q, down_out, *scratch,
):
    scatter_scratch, ag_scratch, scratch = scratch[:8], scratch[8:11], scratch[11:]
    grads, own_low, blk, wbuf, w_sem, load_sem = scratch[:6]
    line = Line(n)
    rows, width = mid.shape
    group = grads.shape[0]
    fb = gu.shape[-1]
    own = blocks * fb
    scatter = Scatter(line, scatter_scratch)
    gather = Gather(line, own_low, gml, ag_scratch)
    grads_copy = pltpu.make_async_copy(grads_in, grads, load_sem)
    grads_copy.start()
    weight_copy = weight_copies(gu, wbuf, w_sem)
    for b in range(blocks):
        for k in range(2):
            weight_copy(b, k).start()
    line.enter(spread)
    grads_copy.wait()
    for b in range(blocks):
        for k in range(2):
            weight_copy(b, k).wait()

    def normed_part(d):
        x = grads[rows_of(d, rows), :]
        for t in range(0, width, 512):
            part = dot_t(x, wbuf[t : t + 512, :]).astype(BF16)
            scatter.part[rows_of(d, rows), t : t + 512] = part

    if not spread:
        scatter.produce(normed_part)
    tiles = 4
    tile = width // tiles
    if spread:
        gate_land, up_land, down_land, gate_in, up_in, down_in, tmp, tmp_down, stage, part_sem, out_sem, hid_buf = scratch[6:18]
        half = fb // 2
        units = [
            dict(parts=gate_parts, row=0, rows=width, x_first=True, axis=0, land1=gate_land, land2=gate_in, tmp=tmp),
            dict(parts=up_parts, row=0, rows=width, x_first=False, axis=0, land1=up_land, land2=up_in, tmp=tmp),
        ]
        for i in range(2):
            units.append(
                dict(
                    parts=down_parts, row=i * half, rows=half, x_first=i == 0, axis=1,
                    land1=down_land.at[i], land2=down_in.at[i], tmp=tmp_down,
                )
            )
        square = Square(line, units, scratch[18:23])
        d_send, d_recv = scratch[23:25]
        rx, *sems = scratch[25:]
        output_sum = Scatter(line, (grads, scatter.sib, rx, scatter.total, *sems))
        slots = [hid_buf.at[:, pl.ds(own + i * tile, tile)] for i in range(2)]
        hid = hid_buf.at[:, pl.ds(0, own)]

        def column_copy(i):
            src = cot_all if i < tiles else normed
            return pltpu.make_async_copy(src.at[:, pl.ds(i % tiles * tile, tile)], slots[i % 2], w_sem.at[0, i % 2])

        hid_copy = pltpu.make_async_copy(hidden, hid, w_sem.at[1, 0])
        hid_copy.start()
        column_copy(0).start()

        def weight_tile(i):
            t = i % tiles
            column_copy(i).wait()
            if i + 1 < 2 * tiles:
                column_copy(i + 1).start()
            if i >= tiles:
                x = slots[i % 2][...]
                for k in range(2):
                    for b in range(blocks):
                        at = k * own + b * fb
                        stage[k, b] = tdot(x, grads[:, at : at + fb]).astype(BF16)
                copies = [
                    pltpu.make_async_copy(stage.at[k, b], parts.at[b, pl.ds(t * tile, tile)], part_sem.at[k, b])
                    for k, parts in enumerate((gate_parts, up_parts))
                    for b in range(blocks)
                ]
            else:
                if i == 0:
                    hid_copy.wait()
                x = slots[i % 2][...]
                for b in range(blocks):
                    part = tdot(hid[:, b * fb : (b + 1) * fb], x).astype(BF16)
                    for k in range(2):
                        stage[k, b, :fb, :] = part[:, k * fb : (k + 1) * fb]
                copies = [
                    pltpu.make_async_copy(
                        stage.at[k, b, pl.ds(0, fb)], down_parts.at[b, :, pl.ds(t * tile + k * fb, fb)], part_sem.at[k, b]
                    )
                    for k in range(2)
                    for b in range(blocks)
                ]
            for copy in copies:
                copy.start()
            for copy in copies:
                copy.wait()

        def place(i, replica):
            at = replica * fb + i * half
            return down_out.at[pl.ds(pl.multiple_of(at, 16), half)]

        def down_send(way, i, src, replica, device):
            return remote(src, place(i, replica), d_send.at[way, i], d_recv.at[way, i], (device, line.me))

        def down_firsts(i):
            src = units[2 + i]["land1"].at[0]
            return [down_send(way, i, src, line.replica, device) for way, device in enumerate((line.xn, line.yn))]

        def down_second(i):
            replica, device = ((line.xn, line.yn), (line.yn, line.xn))[i]
            return down_send(2 + i, i, place(i, replica), replica, device)

        def down_local(i):
            return pltpu.make_async_copy(units[2 + i]["land1"].at[0], place(i, line.replica), out_sem.at[2 + i])

        def down_tile(s):
            if s > 0:
                weight_tile(s - 1)
                square.start(2, s - 1)
                square.start(3, s - 1)

        scatter.produce(normed_part, None, down_tile)
        for i in range(line.chips - 1, tiles):
            weight_tile(i)
            square.start(2, i)
            square.start(3, i)
        scatter.duty(0)
        weight_tile(tiles)
        weight_tile(tiles + 1)
        square.fold(2)
        square.fold(3)
        for i in range(2):
            square.start(0, i)
            square.start(1, i)
        scatter.duty(1)
        for i in range(2, 4):
            weight_tile(tiles + i)
            square.start(0, i)
            square.start(1, i)
        scatter.duty(2)
    else:
        for s in range(line.chips - 1):
            scatter.duty(s)
    scatter.own_sum()
    gain_sum[...] = jnp.zeros_like(gain_sum)

    def back(at):
        through, gain_term = norm_back(scatter.total[at, :], mid[at, :], gain[...])
        value = cot[at, :].astype(F32) + through
        grad_mid[at, :] = value
        own_low[at, :] = value.astype(BF16)
        gain_sum[...] += jnp.sum(gain_term, 0, keepdims=True)

    row_chunks(rows, back)
    gather.start()

    def attended_part(j, z=None):
        if z is None:
            z = gather.ready(j)
        load(gml.at[pl.ds(2 * z, 2)], blk, load_sem)
        grad_att[rows_of(z, rows), :] = dot_t(blk[...].reshape(2 * rows, width), wo[...]).astype(BF16)

    if spread:

        def down_copy(i):
            place = wbuf.at[pl.ds(0, own), pl.ds(i % 2 * tile, tile)]
            return pltpu.make_async_copy(wd.at[:, pl.ds(i * tile, tile)], place, w_sem.at[0, i % 2])

        down_copy(0).start()
        for i in range(2):
            square.result(2 + i)
            for copy in down_firsts(i):
                copy.start()
            down_local(i).start()
        for i in range(tiles):
            down_copy(i).wait()
            if i + 1 < tiles:
                down_copy(i + 1).start()
            for d in range(line.chips):
                at = pl.ds(d * 2 * rows, 2 * rows)
                x = dot(hid[at, :], wbuf[:own, i % 2 * tile : (i % 2 + 1) * tile])
                grads[at, i * tile : (i + 1) * tile] = x.astype(BF16)
        here = gather.ready(0)
        output_sum.produce(lambda d: None)
        gather.arrive(1)
        attended_part(0, here)
        gather.arrive(2)
        attended_part(1)
        output_sum.duty(0)
        square.fold(0)
        square.fold(1)
        gather.arrive(3)
        attended_part(2)
        output_sum.duty(1)
        for i in range(2):
            replica = (line.xn, line.yn)[i]
            down_send(i, i, place(i, replica), replica, replica).wait_recv()
            down_second(i).start()
        attended_part(3)
        output_sum.duty(2)
        output_sum.own_sum()

        def put(at):
            output[at, :] = (mid[at, :] + scatter.total[at, :]).astype(BF16)

        row_chunks(rows, put)
        output_sum.finish()
        copies = []
        for u, out in ((0, gate_q), (1, up_q)):
            square.result(u)
            copies.append(pltpu.make_async_copy(units[u]["land1"].at[0], out, out_sem.at[u]))
            copies[-1].start()
        for i in range(2):
            for copy in down_firsts(i):
                copy.wait_send()
            down_second(i).wait_send()
            down_local(i).wait()
            replica, far = ((line.xn, line.yn), (line.yn, line.xn))[i]
            down_send(2 + i, i, place(i, line.diag), line.diag, replica).wait_recv()
            down_send(1 - i, i, place(i, far), far, far).wait_recv()
        for copy in copies:
            copy.wait()
        square.finish()
    else:

        @pl.loop(0, line.chips)
        def _(j):
            @pl.when(j > 0)
            def _():
                gather.arrive(j)

            attended_part(j)

    scatter.finish()
    gather.finish()


def middle_backward(n, spread, grads, gu, mid, cot, gain, wo, normed, hidden, cot_all, wd):
    rows, width = mid.shape
    group = grads.shape[0]
    blocks, _, _, fb = gu.shape
    own = blocks * fb
    parts = [(4, width, fb), (4, width, fb), (4, fb, width), (width, fb), (width, fb), (4 * fb, width)]
    if not spread:
        parts = [(16, 128)] * 6
    scratch = []
    if spread:
        scratch = [
            pltpu.VMEM((2, width, fb), BF16),
            pltpu.VMEM((2, width, fb), BF16),
            pltpu.VMEM((2, 2, fb // 2, width), BF16),
            pltpu.VMEM((width, fb), BF16),
            pltpu.VMEM((width, fb), BF16),
            pltpu.VMEM((2, fb // 2, width), BF16),
            pltpu.VMEM((width, fb), BF16),
            pltpu.VMEM((fb // 2, width), BF16),
            pltpu.VMEM((2, blocks, width // 4, fb), BF16),
            DMA((2, blocks)),
            DMA((4,)),
            pltpu.VMEM((group, own + width // 2), BF16),
        ] + Square.scratch(4, 4) + [DMA((4, 2)), DMA((4, 2))]
        again = Scatter.scratch(n, rows, width)
        scratch += again[2:3] + again[4:]
    return pl.pallas_call(
        functools.partial(middle_kernel, n, blocks, spread),
        name="middle_backward",
        out_shape=(
            jax.ShapeDtypeStruct((rows, width), F32),
            jax.ShapeDtypeStruct((n, rows, width), BF16),
            jax.ShapeDtypeStruct((group, wo.shape[0]), BF16),
            jax.ShapeDtypeStruct((1, width), F32),
            jax.ShapeDtypeStruct((rows, width) if spread else (16, 128), BF16),
            *[jax.ShapeDtypeStruct(shape, BF16) for shape in parts],
        ),
        in_specs=[ANY, ANY, VMEM, VMEM, VMEM, VMEM, ANY, ANY, ANY, ANY],
        out_specs=(VMEM, ANY, VMEM, VMEM, VMEM) + (ANY,) * 6,
        scratch_shapes=Scatter.scratch(n, rows, width)
        + Gather.scratch(n)
        + [
            pltpu.VMEM((group, 2 * own), BF16),
            pltpu.VMEM((rows, width), BF16),
            pltpu.VMEM((2, rows, width), BF16),
            pltpu.VMEM((width, 2 * own), BF16),
            DMA((2, blocks)),
            DMA(()),
        ]
        + scratch,
        compiler_params=pltpu.CompilerParams(collective_id=2, has_side_effects=True, vmem_limit_bytes=62 * 2**20),
        cost_estimate=pl.CostEstimate(flops=2 * group * width * own * 3, bytes_accessed=400 * 2**20, transcendentals=0),
    )(grads, gu, mid, cot, gain, wo, normed, hidden, cot_all, wd)


def end_kernel(
    n, reps, spread, heads, long_len, q_in, kv, lse, att_t, grad_att, rank_row, rank_col, seg_row, seg_col, cos_t, sin_t,
    w, tok, grad_mid, gain, gain_m_sum, attended, gate_q, up_q, normed, gml,
    grad_tok, gain_grads, grads, gate_out, up_out, q_out, kv_out, out_out, *scratch,
):
    scatter_scratch, att_scratch, scratch = scratch[:8], scratch[8:13], scratch[13:]
    gain_sum, gain_src, gain_land, gain_all, g_send, g_recv = scratch[:6]
    line = Line(n)
    rows, width = tok.shape
    me, rep = line.me, line.replica
    scatter = Scatter(line, scatter_scratch)
    line.enter_all(reps)
    if spread:
        (
            a_send, a_recv, x_send, x_recv, local_sem, qkv_land, qkv_in, out_land, out_in, qkv_tmp, out_tmp,
            qkv_parts, out_parts, slots, slot_sem,
        ) = scratch[6:21]
        fb = gate_q.shape[-1]
        own = 4 * fb
        quarters, outs = (gate_q, up_q), (gate_out, up_out)
        w_rows = gate_out.shape[0]
        q_cols = heads * HD
        qkv_rows = w_rows // 4
        out_rows = out_parts.shape[1] // 2
        counts = (n, n, 0, n, 2, n)
        units = [
            dict(
                parts=qkv_parts, row=i * 4 * qkv_rows, rows=4 * qkv_rows, x_first=i == 0,
                land1=qkv_land.at[i], land2=qkv_in.at[i], tmp=qkv_tmp,
            )
            for i in range(2)
        ] + [
            dict(
                parts=out_parts, row=i * out_rows, rows=out_rows, x_first=i == 0,
                land1=out_land.at[i], land2=out_in.at[i], tmp=out_tmp,
            )
            for i in range(2)
        ]
        square = Square(line, units, scratch[21:])

        def place(k, f, replica):
            if k in (3, 5):
                at = pl.ds(pl.multiple_of(replica * qkv_rows, 16), qkv_rows)
                if k == 3:
                    return q_out.at[at, pl.ds(pl.multiple_of(f * q_cols, 128), q_cols)]
                return kv_out.at[at, pl.ds(pl.multiple_of(f * 2 * HD, 128), 2 * HD)]
            if k == 4:
                return out_out.at[pl.ds(pl.multiple_of(replica * 2 * out_rows + f * out_rows, 16), out_rows)]
            return outs[k].at[:, pl.ds(pl.multiple_of(f * own + replica * fb, 128), fb)]

        def block(k, f):
            if k in (3, 5):
                half, inner = lax.div(f, 4), lax.rem(f, 4)
                cols = pl.ds(0, q_cols) if k == 3 else pl.ds(q_cols, 2 * HD)
                return qkv_land.at[half, 0, pl.ds(pl.multiple_of(inner * qkv_rows, 16), qkv_rows), cols]
            return quarters[k].at[pl.ds(pl.multiple_of(f * w_rows, 16), w_rows)]

        def exchange(k, to, at):
            return remote(block(k, to), place(k, at, rep), a_send.at[k, to], a_recv.at[k, at], (rep, to))

        def exchange_at(d, kinds):
            if d == 0:
                for k in kinds:
                    exchange(k, 2 * line.z + 1 - line.c, me).start()
                return
            for to in (line.z + d, line.z - d):

                @pl.when((to >= 0) & (to < line.chips))
                def _():
                    for core in range(2):
                        for k in kinds:
                            exchange(k, 2 * to + core, me).start()

        def send(way, k, f, src, replica, device):
            return remote(src, place(k, f, replica), x_send.at[way, k, f], x_recv.at[way, k, f], (device, me))

        def share(k, f, src):
            send(0, k, f, src, rep, line.xn).start()
            send(1, k, f, src, rep, line.yn).start()

        def corner(core):
            return (0, line.xn, line.yn) if core % 2 == 0 else (1, line.yn, line.xn)

        def forward_all(z, kinds):
            for k in kinds:
                for core in range(2):
                    forward(k, 2 * z + core, core)

        def forward(k, f, core):
            way, replica, device = corner(core)
            src = place(k, f, replica)
            send(way, k, f, src, replica, replica).wait_recv()
            send(2 + way, k, f, src, replica, device).start()

        def local(i, src, dst):
            return pltpu.make_async_copy(src, dst, local_sem.at[i])

        def mine(k):
            return local(k, block(k, me), place(k, me, rep))

        def mine_out(i):
            return local(6 + i, out_land.at[i, 0], place(4, i, rep))

        def stream(src, use):
            tile = slots.shape[2]
            count = width // tile

            def copy(t):
                return pltpu.make_async_copy(src.at[:, pl.ds(t * tile, tile)], slots.at[t % 2], slot_sem.at[t % 2])

            copy(0).start()
            for t in range(count):
                copy(t).wait()
                if t + 1 < count:
                    copy(t + 1).start()
                use(t * tile, slots[t % 2])

        def out_tile(at, x):
            part = tdot(attended[...], x).astype(BF16)
            for b in range(4):
                out_parts[b, :, at : at + x.shape[1]] = part[b * 2 * out_rows : (b + 1) * 2 * out_rows]

        def qkv_tile(at, x):
            part = tdot(x, grads[...]).astype(BF16)
            for i in range(x.shape[1] // w_rows):
                f = at // w_rows + i
                for b in range(4):
                    piece = part[i * w_rows + b * qkv_rows : i * w_rows + (b + 1) * qkv_rows]
                    qkv_parts[b, f * qkv_rows : (f + 1) * qkv_rows, :] = piece

        for k in range(2):
            share(k, me, block(k, me))
            mine(k).start()
        exchange_at(0, (0, 1))
        exchange_at(1, (0, 1))
        stream(gml, out_tile)
        square.start(2)
        square.start(3)
        exchange_at(2, (0, 1))

    def pass_on(z, kinds):
        for core in range(2):
            f = 2 * z + core

            @pl.when(f != me)
            def _():
                for k in kinds:
                    exchange(k, me, f).wait_recv()
                    share(k, f, place(k, f, rep))

    def after_block(b):
        if not spread:
            return
        if b == 0:
            pass_on(line.near_first(0), (0, 1))
        if b == 2:
            for d in range(3, line.chips):
                exchange_at(d, (0, 1))
        if b == 4:
            pass_on(line.near_first(1), (0, 1))

    attention_back_kernel(
        heads, long_len, q_in, kv, lse, att_t, grad_att, rank_row, rank_col, seg_row, seg_col, cos_t, sin_t, grads,
        *att_scratch, after_block,
    )
    if spread:
        stream(normed, qkv_tile)
        square.start(0)
        square.start(1)

    def normed_part(d):
        x = grads[rows_of(d, rows), :]
        for t in range(0, width, 512):
            part = dot_t(x, w[t : t + 512, :]).astype(BF16)
            scatter.part[rows_of(d, rows), t : t + 512] = part

    scatter.produce(normed_part)
    if spread:
        for u in (2, 3, 0, 1):
            square.fold(u)
        pass_on(line.near_first(2), (0, 1))
    for s in range(line.chips - 1):
        scatter.duty(s)
        if spread:
            if s == 0:
                pass_on(line.near_first(3), (0, 1))
                forward_all(line.near_first(0), (0, 1))
                forward_all(line.near_first(1), (0, 1))
            if s == 1:
                for u in (2, 3, 0, 1):
                    square.result(u)
                for d in range(line.chips):
                    exchange_at(d, (3, 5))
                for k in (3, 5):
                    share(k, me, block(k, me))
                    mine(k).start()
                for i in range(2):
                    share(4, i, out_land.at[i, 0])
                    mine_out(i).start()
                forward_all(line.near_first(2), (0, 1))
            if s == 2:
                forward_all(line.near_first(3), (0, 1))
    scatter.own_sum()
    gain_sum[...] = jnp.zeros_like(gain_sum)

    def back(at):
        through, gain_term = norm_back(scatter.total[at, :], tok[at, :].astype(F32), gain[...])
        grad_tok[at, :] = grad_mid[at, :] + through
        gain_sum[...] += jnp.sum(gain_term, 0, keepdims=True)

    row_chunks(rows, back)

    g_rows = gain_grads.shape[1]
    gain_src[...] = jnp.zeros_like(gain_src)
    for f in range(n):
        gain_src[f, 0:1, :] = gain_sum[:, f * g_rows : (f + 1) * g_rows]
        gain_src[f, 1:2, :] = gain_m_sum[:, f * g_rows : (f + 1) * g_rows]

    def gain_copy(i, to, slot):
        return remote(gain_src.at[to], gain_land.at[slot], g_send.at[0, i], g_recv.at[0, slot], (rep, to))

    def gain_share(i, to, slot):
        return remote(gain_all.at[slot], gain_all.at[slot], g_send.at[1, i], g_recv.at[1, slot], (to, me))

    for i in range(1, n):
        gain_copy(i, line.other(i), me).start()
    gain_land[me] = gain_src[me]
    if spread:
        for j in range(line.chips):
            pass_on(line.near_first(j), (3, 5))
    for i in range(1, n):
        gain_copy(i, me, line.other(i)).wait_recv()
    gain_all[rep] = functools.reduce(lambda a, b: a + b, [gain_land[i] for i in range(n)])
    for i in range(1, reps):
        gain_share(i, lax.rem(rep + i, reps), rep).start()
    if spread:
        for f in range(2):
            forward(4, f, f)
        for j in range(line.chips):
            forward_all(line.near_first(j), (3, 5))
    for i in range(1, reps):
        gain_share(i, rep, lax.rem(rep + i, reps)).wait_recv()
    gain_grads[...] = functools.reduce(lambda a, b: a + b, [gain_all[i] for i in range(reps)])
    for i in range(1, n):
        gain_copy(i, line.other(i), me).wait_send()
    for i in range(1, reps):
        gain_share(i, lax.rem(rep + i, reps), rep).wait_send()
    if spread:
        for k in (0, 1, 3, 5):
            mine(k).wait()
        for i in range(2):
            mine_out(i).wait()
        for k in (0, 1, 3, 5):
            for i in range(1, n):
                exchange(k, line.other(i), me).wait_send()
        for k in range(6):
            for f in range(counts[k]):
                src = place(k, f, rep)
                send(0, k, f, src, rep, line.xn).wait_send()
                send(1, k, f, src, rep, line.yn).wait_send()
                way, replica, device = corner(f)
                send(2 + way, k, f, src, replica, device).wait_send()
                send(2 + way, k, f, src, line.diag, replica).wait_recv()
                far = (line.yn, line.xn)[way]
                send(1 - way, k, f, src, far, far).wait_recv()
        square.finish()
    scatter.finish()


def end_layer(
    n, reps, spread, heads, long_len, q_in, kv, lse, att_t, grad_att, ranks, cos_t, sin_t,
    w, tok, grad_mid, gain, gain_m_sum, attended, gate_q, up_q, normed, gml,
):
    rows, width = tok.shape
    group = attended.shape[0]
    n_blocks = group // QBLK
    cols = w.shape[1]
    w_rows = width // n
    shapes, scratch = [(16, 128)] * 5, []
    if spread:
        fb = gate_q.shape[-1]
        own = 4 * fb
        heads_rows = attended.shape[1] // 4
        q_rows = w_rows // 4
        shapes = [(w_rows, n * own)] * 2 + [(w_rows, n * heads * HD), (w_rows, n * 2 * HD), (4 * heads_rows, width)]
        scratch = [
            DMA((6, n)),
            DMA((6, n)),
            DMA((4, 6, n)),
            DMA((4, 6, n)),
            DMA((8,)),
            pltpu.VMEM((2, 2, 4 * q_rows, cols), BF16),
            pltpu.VMEM((2, 4 * q_rows, cols), BF16),
            pltpu.VMEM((2, 2, heads_rows // 2, width), BF16),
            pltpu.VMEM((2, heads_rows // 2, width), BF16),
            pltpu.VMEM((4 * q_rows, cols), BF16),
            pltpu.VMEM((heads_rows // 2, width), BF16),
            pltpu.VMEM((4, width // 4, cols), BF16),
            pltpu.VMEM((4, heads_rows, width), BF16),
            pltpu.VMEM((2, group, 512), BF16),
            DMA((2,)),
        ] + Square.scratch(4, 1)
    return pl.pallas_call(
        functools.partial(end_kernel, n, reps, spread, heads, long_len),
        name="end_layer",
        out_shape=(
            jax.ShapeDtypeStruct((rows, width), F32),
            jax.ShapeDtypeStruct((8, w_rows), F32),
            jax.ShapeDtypeStruct((group, cols), BF16),
            *[jax.ShapeDtypeStruct(shape, BF16) for shape in shapes],
        ),
        in_specs=[VMEM] * 17 + [ANY] * 4,
        out_specs=(VMEM, VMEM, VMEM) + (ANY,) * 5,
        scratch_shapes=Scatter.scratch(n, rows, width)
        + [
            pltpu.VMEM((2, group, HD), F32),
            pltpu.VMEM((cols, group), BF16),
            pltpu.VMEM((HD, group), BF16),
            pltpu.VMEM((n_blocks, heads * QBLK, HD), BF16),
            pltpu.VMEM((heads * HD, group), F32),
            pltpu.VMEM((1, width), F32),
            pltpu.VMEM((n, 8, w_rows), F32),
            pltpu.VMEM((n, 8, w_rows), F32),
            pltpu.VMEM((reps, 8, w_rows), F32),
            DMA((2, max(n, reps))),
            DMA((2, max(n, reps))),
        ]
        + scratch,
        compiler_params=pltpu.CompilerParams(collective_id=3, has_side_effects=True, vmem_limit_bytes=VMEM_BYTES),
        cost_estimate=pl.CostEstimate(flops=2 * group * width * cols, bytes_accessed=400 * 2**20, transcendentals=0),
    )(
        q_in, kv, lse, att_t, grad_att, *ranks, cos_t, sin_t, w, tok, grad_mid, gain, gain_m_sum, attended,
        gate_q, up_q, normed, gml,
    )


def body(
    tokens, segment, position, attn_gain, w_query, w_key, w_value, w_out, mlp_gain, w_gate, w_up, w_down, cotangent
):
    rows, width = tokens.shape
    group = segment.shape[0]
    long_len = group * 2 // 3
    n = lax.axis_size("fsdp")
    reps = lax.axis_size("replica")
    w_rows = w_query.shape[0]
    ff_own = w_gate.shape[1] // n
    ff_blk = ff_own // reps
    heads = H // n
    q_cols = heads * HD
    dup = n // KVH
    spread = reps == 4 and ff_blk % 128 == 0

    def swap(x):
        return lax.all_to_all(x, "fsdp", 0, 0, tiled=True)

    ids = jnp.concatenate([segment[None], position[None], jnp.zeros((6, group), jnp.int32)]).astype(F32)
    gains = jnp.concatenate([attn_gain[None], mlp_gain[None], jnp.zeros((14, w_rows), BF16)])
    kv_w = jnp.concatenate([w_key.reshape(w_rows, KVH, HD), w_value.reshape(w_rows, KVH, HD)], -1)
    kv_w = jnp.repeat(kv_w, dup, axis=1)
    qkv_w = jnp.concatenate([w_query.reshape(w_rows, n, q_cols), kv_w], -1).transpose(1, 0, 2)
    (
        q_in, kv, lse, att_t, attended, *ranks, cos_back, sin_back, gain_a, gain_m, normed_all, qkv_w, gu_own,
    ) = start_layer(
        n, reps, spread, heads, long_len, tokens, gains, ids, qkv_w, w_gate, w_up
    )
    normed_all = normed_all.reshape(group, width)
    qkv_w = qkv_w.reshape(width, q_cols + 2 * HD)
    if not spread:
        gate_up = jnp.stack([w.reshape(w_rows, n, ff_own).transpose(1, 0, 2) for w in (w_gate, w_up)], 1)
        gu_own = swap(gate_up).transpose(1, 0, 2, 3).reshape(1, 2, width, ff_own)
    normed_mlp, middle, hidden, grads, gate_up, cot_all = mlp_forward(
        n, reps, spread, attended, w_out, tokens, gain_m, gu_own, cotangent, w_down
    )
    normed_mlp, cot_all = normed_mlp.reshape(group, width), cot_all.reshape(group, width)
    if not spread:
        gate_up = gu_own

    def over_replicas(x):
        return lax.psum_scatter(x, "replica", scatter_dimension=0, tiled=True)

    grad_mid, gml, grad_att, gain_m_sum, output, _, _, _, gate_q, up_q, grad_down = middle_backward(
        n, spread, grads, gate_up, middle, cotangent, gain_m, w_out, normed_mlp, hidden, cot_all, w_down
    )
    gml = gml.reshape(group, width)
    if not spread:

        def column_blocks(first):
            grad = tdot(normed_mlp, grads[:, first : first + ff_own]).astype(BF16)
            return grad.reshape(width, reps, ff_blk).transpose(1, 0, 2).reshape(reps * width, ff_blk)

        gate_q, up_q = over_replicas(column_blocks(0)), over_replicas(column_blocks(ff_own))
        down_q = over_replicas(tdot(hidden, cot_all).astype(BF16))
        down = lax.psum_scatter(dot(hidden, w_down).astype(BF16), "fsdp", scatter_dimension=0, tiled=True)
        output = (middle + down.astype(F32)).astype(BF16)
    grad_tokens, gain_grads, grad_qkv, grad_gate, grad_up, grad_w_query, grad_kv, grad_out_w = end_layer(
        n, reps, spread, heads, long_len, q_in, kv, lse, att_t, grad_att, ranks, cos_back, sin_back,
        qkv_w, tokens, grad_mid, gain_a, gain_m_sum, attended, gate_q, up_q, normed_all, gml,
    )
    if not spread:

        def by_rows(grad):
            grad = swap(grad.reshape(n, w_rows, -1))
            grad = lax.all_gather(grad, "replica", axis=0, tiled=False)
            return grad.transpose(2, 1, 0, 3).reshape(w_rows, -1)

        grad_gate, grad_up = by_rows(gate_q), by_rows(up_q)
        grad_down = lax.all_gather(down_q, "replica", axis=0, tiled=True)
        grad_w = tdot(normed_all, grad_qkv).astype(BF16)
        grad_w = grad_w.reshape(n, reps, w_rows // reps, -1).transpose(1, 0, 2, 3)
        grad_w = over_replicas(grad_w)[0]
        grad_w = lax.all_gather(swap(grad_w), "replica", axis=0, tiled=False)
        grad_w = grad_w.transpose(0, 2, 1, 3).reshape(w_rows, n, -1)
        grad_w_query, grad_kv = grad_w[:, :, :q_cols].reshape(w_rows, H * HD), grad_w[:, :, q_cols:]
        grad_out_w = lax.psum(tdot(attended, gml).astype(BF16), "replica")
    grad_kv = grad_kv.reshape(w_rows, KVH, dup, 2 * HD).astype(F32).sum(2)
    grad_w_key = grad_kv[:, :, :HD].reshape(w_rows, KVH * HD)
    grad_w_value = grad_kv[:, :, HD:].reshape(w_rows, KVH * HD)
    return (
        output,
        grad_tokens,
        gain_grads[0],
        grad_w_query.astype(F32),
        grad_w_key,
        grad_w_value,
        grad_out_w.astype(F32),
        gain_grads[1],
        grad_gate.astype(F32),
        grad_up.astype(F32),
        grad_down.astype(F32),
    )


def solution(mesh):
    both = P(("replica", "fsdp"), None)
    mat = P("fsdp", None)
    vec = P("fsdp")
    return jax.shard_map(
        body,
        mesh=mesh,
        in_specs=(both, P("replica"), P("replica"), vec, mat, mat, mat, mat, vec, mat, mat, mat, both),
        out_specs=(both, both, vec, mat, mat, mat, mat, vec, mat, mat, mat),
        check_vma=False,
    )
```

```python
import functools
import math

import jax
import jax.numpy as jnp
from jax import lax
from jax.experimental import pallas as pl
from jax.experimental.pallas import tpu as pltpu
from jax.sharding import PartitionSpec as P

H = 32
KVH = 8
HD = 64
EPSILON = 1e-05
ROPE_BASE = 500000.0
MASKED = -1e30
QBLK = 256
F32 = jnp.float32
BF16 = jnp.bfloat16
MESH = pl.DeviceIdType.MESH
VMEM = pl.BlockSpec(memory_space=pltpu.VMEM)
ANY = pl.BlockSpec(memory_space=pl.ANY)
DMA = pltpu.SemaphoreType.DMA
VMEM_BYTES = 60 * 2**20


def dot(a, b):
    return jnp.dot(a, b, preferred_element_type=F32)


def tdot(a, b):
    return lax.dot_general(a, b, (((0,), (0,)), ((), ())), preferred_element_type=F32)


def dot_t(a, b):
    return lax.dot_general(a, b, (((1,), (1,)), ((), ())), preferred_element_type=F32)


class Line:
    def __init__(self, n):
        f = lax.axis_index("fsdp")
        self.n = n
        self.replica = lax.axis_index("replica")
        self.chips = n // 2
        self.z = lax.div(f, 2)
        self.c = lax.rem(f, 2)
        self.me = f
        x, y = lax.rem(self.replica, 2), lax.div(self.replica, 2)
        self.xn, self.yn = self.replica + 1 - 2 * x, self.replica + 2 - 4 * y
        self.diag = 3 - self.replica

    def dev(self, z, c):
        return (self.replica, 2 * z + c)

    def other(self, i):
        return lax.rem(self.me + i, self.n)

    def enter(self, square=False):
        barrier = pltpu.get_barrier_semaphore()
        z, c = self.z, self.c

        def greet(device):
            pl.semaphore_signal(barrier, inc=1, device_id=device, device_id_type=MESH)

        greet(self.dev(z, 1 - c))

        @pl.when(z > 0)
        def _():
            greet(self.dev(z - 1, c))

        @pl.when(z < self.chips - 1)
        def _():
            greet(self.dev(z + 1, c))

        count = 1 + (z > 0).astype(jnp.int32) + (z < self.chips - 1).astype(jnp.int32)
        if square:
            greet((self.xn, self.me))
            greet((self.yn, self.me))
            count = count + 2
        pl.semaphore_wait(barrier, count)

    def enter_all(self, reps, square=False):
        barrier = pltpu.get_barrier_semaphore()

        def greet(device):
            pl.semaphore_signal(barrier, inc=1, device_id=device, device_id_type=MESH)

        for i in range(1, self.n):
            greet((self.replica, self.other(i)))
        if square:
            greet((self.xn, self.me))
            greet((self.yn, self.me))
        else:
            for i in range(1, reps):
                greet((lax.rem(self.replica + i, reps), self.me))
        pl.semaphore_wait(barrier, self.n - 1 + (2 if square else reps - 1))

    def far_first(self, s):
        z, last = self.z, self.chips - 1
        right = last - z
        low = jnp.where(s < right, last - s, s - right)
        high = jnp.where(s < z, s, last - (s - z))
        return jnp.where(2 * z < self.chips, low, high)

    def near_first(self, j):
        z, last = self.z, self.chips - 1
        short = jnp.minimum(z, last - z)
        half = lax.div(j + 1, 2)
        both = jnp.where(lax.rem(j, 2) == 1, z - half, z + half)
        rest = jnp.where(2 * z < self.chips, j, last - j)
        return jnp.where(j <= 2 * short, both, rest)


def remote(src, dst, send, recv, device):
    return pltpu.make_async_remote_copy(
        src_ref=src, dst_ref=dst, send_sem=send, recv_sem=recv, device_id=device, device_id_type=MESH
    )


def row_step(rows):
    return 32 if rows % 32 == 0 else 16


def row_chunks(rows, fn):
    step = row_step(rows)

    @pl.loop(0, rows // step)
    def _(i):
        fn(pl.ds(pl.multiple_of(i * step, step), step))


PARTS = 2


class Scatter:
    @staticmethod
    def scratch(n, rows, width):
        chips = n // 2
        return [
            pltpu.VMEM((n * rows, width), BF16),
            pltpu.VMEM((chips, rows, width), BF16),
            pltpu.VMEM((chips + 1, rows, width), BF16),
            pltpu.VMEM((rows, width), F32),
            DMA((chips,)),
            DMA((chips,)),
            DMA((chips, PARTS)),
            DMA((chips + 1, PARTS)),
        ]

    def __init__(self, line, scratch):
        self.line = line
        self.part, self.sib, self.rx, self.total = scratch[:4]
        self.sib_send, self.sib_recv, self.line_send, self.line_recv = scratch[4:]
        self.rows, self.width = self.total.shape
        self.rows_q = self.rows // PARTS

    def rows_at(self, d, c, first=0, count=None):
        at = (2 * d + c) * self.rows + first
        return pl.ds(pl.multiple_of(at, 16), self.rows if count is None else count)

    def to_sibling(self, d):
        line = self.line
        return remote(
            self.part.at[self.rows_at(d, 1 - line.c)], self.sib.at[d], self.sib_send.at[d], self.sib_recv.at[d], line.dev(line.z, 1 - line.c)
        )

    def along(self, d, slot, q, z):
        c = self.line.c
        at = pl.ds(q * self.rows_q, self.rows_q)
        return remote(
            self.part.at[self.rows_at(d, c, q * self.rows_q, self.rows_q)], self.rx.at[slot, at], self.line_send.at[d, q], self.line_recv.at[slot, q], self.line.dev(z, c)
        )

    def to_right(self, d, q):
        return self.along(d, d, q, self.line.z + 1)

    def to_left(self, d, q):
        z = self.line.z
        return self.along(d, jnp.where(d == z - 1, self.line.chips, d), q, z - 1)

    def wait_line(self, slot, q):
        line = self.line
        at = pl.ds(q * self.rows_q, self.rows_q)
        here = self.rx.at[slot, at]
        remote(here, here, self.line_send.at[0, q], self.line_recv.at[slot, q], line.dev(line.z, 1 - line.c)).wait_recv()

    def add(self, d, q, with_line):
        step = row_step(self.rows_q)
        c = self.line.c

        @pl.loop(0, self.rows_q // step)
        def _(i):
            at = pl.ds(pl.multiple_of(q * self.rows_q + i * step, step), step)
            here = self.rows_at(d, c, q * self.rows_q + i * step, step)
            value = self.part[here, :].astype(F32) + self.sib[d, at, :].astype(F32)
            if with_line:
                value = value + self.rx[d, at, :].astype(F32)
            self.part[here, :] = value.astype(BF16)

    def emit(self, d):
        z = self.line.z
        self.to_sibling(d).wait_recv()
        for q in range(PARTS):
            self.add(d, q, False)

            @pl.when(z == 0)
            def _():
                self.to_right(d, q).start()

            @pl.when(z > 0)
            def _():
                self.to_left(d, q).start()

    def emit_last(self):
        line = self.line

        @pl.when((line.z == 0) | (line.z == line.chips - 1))
        def _():
            self.emit(line.far_first(line.chips - 2))

    def produce(self, compute, after_first=None, between=None, hold_last=False):
        line = self.line
        chips, z = line.chips, line.z

        def step(s):
            d = line.far_first(s)
            compute(d)
            self.to_sibling(d).start()

            @pl.when(((z == 0) | (z == chips - 1)) & (s > 0) & (s < (chips - 1 if hold_last else chips)))
            def _():
                self.emit(line.far_first(s - 1))
                if after_first is not None:

                    @pl.when(s == 1)
                    def _():
                        after_first()

        if between is None:
            pl.loop(0, chips)(step)
        else:
            for s in range(chips):
                step(s)
                between(s)

    def duty(self, s, sides=(True, False)):
        chips, z, c = self.line.chips, self.line.z, self.line.c
        for near in sides:
            right = (2 * z < chips) if near else (2 * z >= chips)
            d = jnp.where(right, chips - 1 - s, s)
            active = jnp.where(right, (z > 0) & (d > z), (z < chips - 1) & (d < z))

            @pl.when(active)
            def _():
                self.to_sibling(d).wait_recv()
                for q in range(PARTS):
                    self.wait_line(d, q)
                    self.add(d, q, True)
                    slot = jnp.where(~right & (d == z - 1), chips, d)
                    self.along(d, slot, q, jnp.where(right, z + 1, z - 1)).start()

    def own_sum(self):
        chips, z, c = self.line.chips, self.line.z, self.line.c
        total, rx = self.total, self.rx
        self.to_sibling(z).wait_recv()
        for q in range(PARTS):

            @pl.when(z > 0)
            def _():
                self.wait_line(z, q)

            @pl.when(z < chips - 1)
            def _():
                self.wait_line(chips, q)

        def add_up(at):
            total[at, :] = self.part[self.rows_at(z, c, at.start, at.size), :].astype(F32) + self.sib[z, at, :].astype(F32)

            @pl.when(z > 0)
            def _():
                total[at, :] += rx[z, at, :].astype(F32)

            @pl.when(z < chips - 1)
            def _():
                total[at, :] += rx[chips, at, :].astype(F32)

        row_chunks(self.rows, add_up)

    def finish(self):
        z = self.line.z

        @pl.loop(0, self.line.chips)
        def _(d):
            self.to_sibling(d).wait_send()
            for q in range(PARTS):

                @pl.when(d > z)
                def _():
                    self.to_right(d, q).wait_send()

                @pl.when(d < z)
                def _():
                    self.to_left(d, q).wait_send()


class Gather:
    @staticmethod
    def scratch(n):
        return [DMA((3, n)), DMA((n,)), DMA(())]

    def __init__(self, line, own, buf, scratch):
        self.line, self.own, self.buf = line, own, buf
        self.send, self.recv, self.local_sem = scratch

    def copy(self, way, slot, mine=False):
        line, z, c = self.line, self.line.z, self.line.c
        src = self.own if mine else self.buf.at[slot]
        device = (line.dev(z, 1 - c), line.dev(z + 1, c), line.dev(z - 1, c))[way]
        return remote(src, self.buf.at[slot], self.send.at[way, slot], self.recv.at[slot], device)

    def local(self):
        return pltpu.make_async_copy(self.own, self.buf.at[self.line.me], self.local_sem)

    def along(self, at, mine=False):
        z, slot = self.line.z, 2 * at + self.line.c

        @pl.when((z < self.line.chips - 1) & (at <= z))
        def _():
            self.copy(1, slot, mine).start()

        @pl.when((z > 0) & (at >= z))
        def _():
            self.copy(2, slot, mine).start()

    def pass_on(self, at, mine=False):
        self.along(at, mine)
        self.copy(0, 2 * at + self.line.c, mine).start()

    def start(self, ends_later=False):
        line = self.line
        if ends_later:

            @pl.when((line.z > 0) & (line.z < line.chips - 1))
            def _():
                self.along(line.z, True)

            self.copy(0, line.me, True).start()
        else:
            self.pass_on(line.z, True)
        self.local().start()

    def start_ends(self):
        self.along(self.line.z, True)

    def arrive(self, t, sides=(True, False)):
        z, chips = self.line.z, self.line.chips
        for far in sides:
            at = jnp.where((2 * z < chips) == far, z + t, z - t)
            there = (at >= 0) & (at < chips)

            @pl.when(there)
            def _():
                self.copy(0, 2 * at + self.line.c).wait_recv()
                self.pass_on(at)

    def ready(self, j):
        at = self.line.near_first(j)
        if isinstance(j, int):
            if j == 0:
                self.local().wait()
        else:

            @pl.when(j == 0)
            def _():
                self.local().wait()

        self.copy(0, 2 * at + 1 - self.line.c).wait_recv()
        return at

    def finish(self):
        z = self.line.z

        @pl.loop(0, self.line.chips)
        def _(at):
            slot = 2 * at + self.line.c
            self.copy(0, slot).wait_send()

            @pl.when((z < self.line.chips - 1) & (at <= z))
            def _():
                self.copy(1, slot).wait_send()

            @pl.when((z > 0) & (at >= z))
            def _():
                self.copy(2, slot).wait_send()


def load(src, dst, sem):
    copy = pltpu.make_async_copy(src, dst, sem)
    copy.start()
    copy.wait()


def rows_of(z, rows):
    return pl.ds(pl.multiple_of(z * 2 * rows, 2 * rows), 2 * rows)


class Square:
    @staticmethod
    def scratch(units, tiles):
        return [DMA((units, 2, tiles)), DMA((units, 2, tiles)), DMA((units,)), DMA((units,)), DMA(())]

    def __init__(self, line, units, scratch):
        self.line, self.units = line, units
        self.send1, self.recv1, self.send2, self.recv2, self.sem = scratch
        self.tiles = self.send1.shape[2]

    def ways(self, u):
        line = self.line
        return (line.xn, line.yn) if self.units[u]["x_first"] else (line.yn, line.xn)

    def whole(self, u, block):
        unit = self.units[u]
        return unit["parts"].at[block, pl.ds(unit["row"], unit["rows"])]

    def first(self, u, slot, t):
        unit = self.units[u]
        one, _ = self.ways(u)
        block = one if slot == 0 else self.line.diag
        src, dst = self.whole(u, block), unit["land1"].at[slot]
        if self.tiles > 1:
            axis = unit["axis"]
            step = dst.shape[axis] // self.tiles
            at = (pl.ds(t * step, step),) if axis == 0 else (slice(None), pl.ds(t * step, step))
            src, dst = src.at[at], dst.at[at]
        return remote(src, dst, self.send1.at[u, slot, t], self.recv1.at[u, slot, t], (one, self.line.me))

    def start(self, u, t=0):
        for slot in range(2):
            self.first(u, slot, t).start()

    def add(self, u, slot, block, also=None):
        unit = self.units[u]
        for t in range(self.tiles):
            self.first(u, slot, t).wait_recv()
        land, tmp = unit["land1"], unit["tmp"].at[pl.ds(0, unit["rows"])]
        load(self.whole(u, block), tmp, self.sem)

        def one(at):
            value = land[slot, at, :].astype(F32) + tmp[at, :].astype(F32)
            if also is not None:
                value = value + also[at, :].astype(F32)
            land[slot, at, :] = value.astype(BF16)

        row_chunks(unit["rows"], one)

    def second(self, u):
        unit = self.units[u]
        _, two = self.ways(u)
        return remote(unit["land1"].at[1], unit["land2"], self.send2.at[u], self.recv2.at[u], (two, self.line.me))

    def fold(self, u):
        self.add(u, 1, self.ways(u)[1])
        self.second(u).start()

    def result(self, u):
        self.second(u).wait_recv()
        self.add(u, 0, self.line.replica, self.units[u]["land2"])

    def finish(self):
        for u in range(len(self.units)):
            self.second(u).wait_send()
            for slot in range(2):
                for t in range(self.tiles):
                    self.first(u, slot, t).wait_send()


def key_range(block, long_len):
    longs = long_len // QBLK
    return (0, block + 1, False) if block < longs else (longs, block + 1 - longs, True)


def score_mask(q_block, k_block, seg_row, seg_col, heads, compare):
    visible = None
    shape = (QBLK, QBLK)
    if q_block == k_block:
        visible = lax.broadcasted_iota(jnp.int32, shape, 0) <= lax.broadcasted_iota(jnp.int32, shape, 1)
    if compare:
        k_at, q_at = k_block * QBLK, q_block * QBLK
        same = seg_col[k_at : k_at + QBLK, :] == seg_row[:, q_at : q_at + QBLK]
        visible = same if visible is None else visible & same
    if visible is None:
        return None
    bias = jnp.where(visible, 0.0, MASKED)
    return jnp.concatenate([bias] * heads, 1)


def one_hot_rows(rank_row, start):
    group = rank_row.shape[1]
    places = start + lax.broadcasted_iota(jnp.int32, (QBLK, group), 0)
    return jnp.where(rank_row[...] == places, 1.0, 0.0).astype(BF16)


def one_hot_back(rank_col, start):
    group = rank_col.shape[0]
    places = lax.broadcasted_iota(jnp.int32, (QBLK, group), 1)
    return jnp.where(rank_col[pl.ds(start, QBLK), :] == places, 1.0, 0.0).astype(BF16)


def attention_kernel(heads, long_len, qkv, rank_row, rank_col, seg_row, seg_col, q_out, kv_out, lse, att_t, att, s_buf, v_t):
    group = qkv.shape[0]
    q_cols = heads * HD
    n_blocks = group // QBLK
    for b in range(n_blocks):
        ordered = dot(one_hot_rows(rank_row, b * QBLK), qkv[...])
        for h in range(heads):
            q_out[b, h * QBLK : (h + 1) * QBLK, :] = (ordered[:, h * HD : (h + 1) * HD] * 0.125).astype(BF16)
        kv_out[0, b * QBLK : (b + 1) * QBLK, :] = ordered[:, q_cols : q_cols + HD].astype(BF16)
        values = ordered[:, q_cols + HD :]
        kv_out[1, b * QBLK : (b + 1) * QBLK, :] = values.astype(BF16)
        v_t[:, b * QBLK : (b + 1) * QBLK] = values.T.astype(BF16)
    for b in range(n_blocks):
        first, count, compare = key_range(b, long_len)
        queries = q_out[b]
        top = None
        for i in range(count):
            k_at = (first + i) * QBLK
            scores = dot_t(kv_out[0, k_at : k_at + QBLK, :], queries)
            bias = score_mask(b, first + i, seg_row, seg_col, heads, compare)
            if bias is not None:
                scores = scores + bias
            s_buf[i] = scores
            high = jnp.max(scores, 0, keepdims=True)
            top = high if top is None else jnp.maximum(top, high)
        total, out = 0.0, 0.0
        for i in range(count):
            k_at = (first + i) * QBLK
            terms = jnp.exp(s_buf[i] - top)
            total = total + jnp.sum(terms, 0, keepdims=True)
            out = out + dot(v_t[:, k_at : k_at + QBLK], terms.astype(BF16))
        lse[b] = top + jnp.log(total)
        out = out / total
        for h in range(heads):
            att_t[h * HD : (h + 1) * HD, b * QBLK : (b + 1) * QBLK] = out[:, h * QBLK : (h + 1) * QBLK]
    low = att_t[...].astype(BF16)

    @pl.loop(0, n_blocks)
    def _(b):
        at = pl.multiple_of(b * QBLK, QBLK)
        att[pl.ds(at, QBLK), :] = dot_t(one_hot_back(rank_col, at), low).astype(BF16)


def attention_back_kernel(
    heads, long_len, q_in, kv, lse, att_t, grad_att, rank_row, rank_col, seg_row, seg_col, cos_t, sin_t, out,
    grad_kv, grad_t, k_t, go_rows, go_t, after_block,
):
    group = kv.shape[1]
    n_blocks = group // QBLK
    half = HD // 2
    q_cols = heads * HD
    for b in range(n_blocks):
        at = b * QBLK
        ordered = dot(one_hot_rows(rank_row, at), grad_att[...])
        for h in range(heads):
            go_rows[b, h * QBLK : (h + 1) * QBLK, :] = ordered[:, h * HD : (h + 1) * HD].astype(BF16)
        go_t[:, at : at + QBLK] = ordered.T
        k_t[:, at : at + QBLK] = kv[0, at : at + QBLK, :].astype(F32).T.astype(BF16)
    grad_kv[...] = jnp.zeros_like(grad_kv)
    for b in range(n_blocks):
        first, count, compare = key_range(b, long_len)
        q_at = b * QBLK
        queries, grad_rows = q_in[b], go_rows[b]
        centre = jnp.concatenate(
            [
                jnp.sum(
                    go_t[h * HD : (h + 1) * HD, q_at : q_at + QBLK] * att_t[h * HD : (h + 1) * HD, q_at : q_at + QBLK],
                    0,
                    keepdims=True,
                )
                for h in range(heads)
            ],
            1,
        )
        grad_q = 0.0
        for i in range(count):
            k_at = (first + i) * QBLK
            scores = dot_t(kv[0, k_at : k_at + QBLK, :], queries)
            bias = score_mask(b, first + i, seg_row, seg_col, heads, compare)
            if bias is not None:
                scores = scores + bias
            probs = jnp.exp(scores - lse[b])
            grad_probs = dot_t(kv[1, k_at : k_at + QBLK, :], grad_rows)
            grad_scores = (probs * (grad_probs - centre)).astype(BF16)
            grad_kv[0, k_at : k_at + QBLK, :] += dot(grad_scores, queries)
            grad_kv[1, k_at : k_at + QBLK, :] += dot(probs.astype(BF16), grad_rows)
            grad_q = grad_q + dot(k_t[:, k_at : k_at + QBLK], grad_scores)
        cos_b, sin_b = cos_t[:, q_at : q_at + QBLK], sin_t[:, q_at : q_at + QBLK]

        def turned(value):
            front, back = value[:half], value[half:]
            return jnp.concatenate([front * cos_b + back * sin_b, back * cos_b - front * sin_b], 0).astype(BF16)

        for h in range(heads):
            grad_t[h * HD : (h + 1) * HD, q_at : q_at + QBLK] = turned(grad_q[:, h * QBLK : (h + 1) * QBLK] * 0.125)
        after_block(b)
    for b in range(n_blocks):
        at = b * QBLK
        cos_b, sin_b = cos_t[:, at : at + QBLK], sin_t[:, at : at + QBLK]
        value = grad_kv[0, at : at + QBLK, :].T
        front, back = value[:half], value[half:]
        grad_t[q_cols : q_cols + half, at : at + QBLK] = (front * cos_b + back * sin_b).astype(BF16)
        grad_t[q_cols + half : q_cols + HD, at : at + QBLK] = (back * cos_b - front * sin_b).astype(BF16)
        grad_t[q_cols + HD :, at : at + QBLK] = grad_kv[1, at : at + QBLK, :].T.astype(BF16)

    @pl.loop(0, n_blocks)
    def _(b):
        at = pl.multiple_of(b * QBLK, QBLK)
        out[pl.ds(at, QBLK), :] = dot_t(one_hot_back(rank_col, at), grad_t[...]).astype(BF16)


def order_group(long_len, ids, ids_col, rank_row, rank_col, seg_row_out, seg_col_out, pos_out, key_col, acc):
    group = ids.shape[1]
    seg_row, pos_row = ids.at[0:1, :], ids.at[1:2, :]

    def chunks(fn):
        @pl.loop(0, group // QBLK)
        def _(i):
            fn(pl.multiple_of(i * QBLK, QBLK))

    def ones(mask):
        return jnp.where(mask, 1.0, 0.0)

    acc[...] = jnp.zeros_like(acc)

    def lengths(at):
        here = pl.ds(at, QBLK)
        same = ones(ids_col[here, 0:1] == seg_row[...])
        acc[0:1, :] += jnp.sum(same, 0, keepdims=True)
        first = jnp.sum(same, 1, keepdims=True) == float(long_len)
        key_col[here, :] = jnp.where(first, -1.0, ids_col[here, 0:1]) * float(group) + ids_col[here, 1:2]

    chunks(lengths)
    key_row = jnp.where(acc[0:1, :] == float(long_len), -1.0, seg_row[...]) * float(group)
    acc[1:2, :] = key_row + pos_row[...]

    def ranks(at):
        here = pl.ds(at, QBLK)
        mine, others = key_col[here, :], acc[1:2, :]
        rank_col[here, :] = jnp.sum(ones(others < mine), 1, keepdims=True).astype(jnp.int32)
        acc[2:3, :] += jnp.sum(ones(mine < others), 0, keepdims=True)

    chunks(ranks)
    rank_row[...] = acc[2:3, :].astype(jnp.int32)

    def ordered(at):
        here = pl.ds(at, QBLK)
        places = at + lax.broadcasted_iota(jnp.int32, (QBLK, group), 0)
        seg = jnp.sum(jnp.where(rank_row[...] == places, seg_row[...], 0.0), 1, keepdims=True)
        seg_col_out[here, :] = seg.astype(jnp.int32)
        moved = rank_col[here, :] == lax.broadcasted_iota(jnp.int32, (QBLK, group), 1)
        acc[3:4, :] += jnp.sum(jnp.where(moved, ids_col[here, 0:1], 0.0), 0, keepdims=True)
        acc[4:5, :] += jnp.sum(jnp.where(moved, ids_col[here, 1:2], 0.0), 0, keepdims=True)

    chunks(ordered)
    seg_row_out[...] = acc[3:4, :].astype(jnp.int32)
    pos_out[...] = acc[4:5, :]


def frequencies(index):
    return jnp.exp(-math.log(ROPE_BASE) * index.astype(F32) * (2.0 / HD))


def start_kernel(
    n, reps, spread, heads, long_len, tok, gains, ids, wqkv, wg, wu,
    q_out, kv_out, lse, att_t, att, rank_row, rank_col, seg_row_out, seg_col_out, cos_back, sin_back, gain_a, gain_m,
    normed, w_all, gu_own,
    gains_buf, own, wv, blk, qkv, cos, sin, ids_col, key_col, acc, pos_out, s_buf, v_t,
    g_send, g_recv, a_send, a_recv, r_send, r_recv, u_send, u_recv, local_sem, load_sem, *ag_scratch,
):
    line = Line(n)
    me, rep = line.me, line.replica
    rows, width = tok.shape
    w_rows = gains.shape[1]
    fb = gu_own.shape[-1]
    own_cols = fb * reps
    line.enter_all(reps)

    def gain_copy(i, to, slot):
        return remote(gains, gains_buf.at[slot], g_send.at[i], g_recv.at[slot], (rep, to))

    def qkv_copy(i, to, slot):
        piece = wqkv.at[to, pl.ds(rep * (w_rows // reps), w_rows // reps)]
        return remote(piece, w_all.at[slot, rep], a_send.at[i], a_recv.at[slot], (rep, to))

    def gu_copy(k, to, slot):
        piece = (wg, wu)[k].at[:, pl.ds(pl.multiple_of(to * own_cols + rep * fb, 128), fb)]
        at = pl.ds(pl.multiple_of(slot * w_rows, 16), w_rows)
        return remote(piece, gu_own.at[k, at], u_send.at[k, to], u_recv.at[k, slot], (rep, to))

    def spread_weights(stage):
        if not spread:
            return
        if stage == 0:
            for k in range(2):
                gu_copy(k, 2 * line.z + 1 - line.c, me).start()
            return
        last = line.chips - 1

        @pl.loop(1, line.chips)
        def _(d):
            for to in (line.z + d, line.z - d):
                to_end = (to == 0) | (to == last)
                next_to_end = ((line.z == 0) | (line.z == last)) & (d == 1)
                now = (to_end, (~to_end) & next_to_end, (~to_end) & (~next_to_end))[stage % 3]

                @pl.when((to >= 0) & (to <= last) & now)
                def _():
                    for core in range(2):
                        for k in range(2):
                            gu_copy(k, 2 * to + core, me).start()

    for i in range(1, n):
        gain_copy(i, line.other(i), me).start()
    for i in range(1, n):
        qkv_copy(i, line.other(i), me).start()
    mine = [
        pltpu.make_async_copy(
            wqkv.at[me, pl.ds(rep * (w_rows // reps), w_rows // reps)], w_all.at[me, rep], local_sem.at[0]
        )
    ]
    if spread:
        for k in range(2):
            piece = (wg, wu)[k].at[:, pl.ds(pl.multiple_of(me * own_cols + rep * fb, 128), fb)]
            at = pl.ds(pl.multiple_of(me * w_rows, 16), w_rows)
            mine.append(pltpu.make_async_copy(piece, gu_own.at[k, at], local_sem.at[1 + k]))
    for copy in mine:
        copy.start()
    gains_buf[me] = gains[...]
    for i in range(1, n):
        gain_copy(i, me, line.other(i)).wait_recv()
    gain_a[...] = jnp.concatenate([gains_buf[i, 0:1, :].astype(F32) for i in range(n)], 1)
    gain_m[...] = jnp.concatenate([gains_buf[i, 1:2, :].astype(F32) for i in range(n)], 1)

    def norm(at):
        resid = tok[at, :].astype(F32)
        inverse = lax.rsqrt(jnp.mean(resid * resid, -1, keepdims=True) + EPSILON)
        own[at, :] = (resid * inverse * gain_a[...]).astype(BF16)

    row_chunks(rows, norm)
    gather = Gather(line, own, normed, ag_scratch)
    gather.start()
    spread_weights(0)
    for at in range(0, ids.shape[1], QBLK):
        ids_col[at : at + QBLK, :] = ids[:, at : at + QBLK].T
    order_group(long_len, ids, ids_col, rank_row, rank_col, seg_row_out, seg_col_out, pos_out, key_col, acc)
    for i in range(1, n):
        qkv_copy(i, me, line.other(i)).wait_recv()
    mine[0].wait()

    def share(i, to, slot):
        return remote(w_all.at[:, slot], w_all.at[:, slot], r_send.at[i], r_recv.at[slot], (to, me))

    for i in range(1, reps):
        share(i, lax.rem(rep + i, reps), rep).start()
    lanes = lax.broadcasted_iota(jnp.int32, (1, 128), 1)
    freq = frequencies(lax.rem(lanes, HD // 2))
    sign = jnp.where(lax.rem(lanes, HD) < HD // 2, -1.0, 1.0)

    def table(at):
        angles = ids_col[at, 1:2] * freq
        cos[at, :] = jnp.cos(angles)
        sin[at, :] = jnp.sin(angles) * sign

    row_chunks(ids_col.shape[0], table)
    gather.arrive(1)
    spread_weights(1)
    angles = frequencies(lax.broadcasted_iota(jnp.int32, (HD // 2, 1), 0)) * pos_out[...]
    cos_back[...] = jnp.cos(angles)
    sin_back[...] = jnp.sin(angles)
    for i in range(1, reps):
        share(i, rep, lax.rem(rep + i, reps)).wait_recv()
    load(w_all, wv, load_sem)
    cols = wv.shape[-1]
    lane = lax.broadcasted_iota(jnp.int32, (2 * rows, 128), 1)
    front = lax.rem(lane, HD) < HD // 2

    def project(j):
        z = gather.ready(j)
        load(normed.at[pl.ds(2 * z, 2)], blk, load_sem)
        at = rows_of(z, rows)
        raw = dot(blk[...].reshape(2 * rows, width), wv[...].reshape(width, cols))
        for t in range(0, cols, 128):
            part = raw[:, t : t + 128]
            cos_t, sin_t = cos[at, :], sin[at, :]
            if t == cols - 128:
                cos_t, sin_t = jnp.where(lane < HD, cos_t, 1.0), jnp.where(lane < HD, sin_t, 0.0)
            partner = jnp.where(front, pltpu.roll(part, 128 - HD // 2, 1), pltpu.roll(part, HD // 2, 1))
            qkv[at, t : t + 128] = (part * cos_t + partner * sin_t).astype(BF16)

    project(0)
    gather.arrive(2)
    spread_weights(2)

    is_end = (line.z == 0) | (line.z == line.chips - 1)

    @pl.when(is_end)
    def _():
        spread_weights(3)

    @pl.loop(1, line.chips)
    def _(j):
        @pl.when(j + 2 < line.chips)
        def _():
            gather.arrive(j + 2)

        project(j)

    @pl.when(~is_end)
    def _():
        spread_weights(3)

    attention_kernel(
        heads, long_len, qkv, rank_row, rank_col, seg_row_out, seg_col_out, q_out, kv_out, lse, att_t, att, s_buf, v_t
    )
    for i in range(1, n):
        gain_copy(i, line.other(i), me).wait_send()
        qkv_copy(i, line.other(i), me).wait_send()
    for i in range(1, reps):
        share(i, lax.rem(rep + i, reps), rep).wait_send()
    if spread:
        for k in range(2):
            mine[1 + k].wait()
            for i in range(1, n):
                gu_copy(k, line.other(i), me).wait_send()
                gu_copy(k, me, line.other(i)).wait_recv()
    gather.finish()


def start_layer(n, reps, spread, heads, long_len, tok, gains, ids, wqkv, wg, wu):
    rows, width = tok.shape
    w_rows = gains.shape[1]
    cols = wqkv.shape[-1]
    group = ids.shape[1]
    n_blocks = group // QBLK
    fb = wg.shape[1] // n // reps
    return pl.pallas_call(
        functools.partial(start_kernel, n, reps, spread, heads, long_len),
        name="start_layer",
        out_shape=(
            jax.ShapeDtypeStruct((n_blocks, heads * QBLK, HD), BF16),
            jax.ShapeDtypeStruct((2, group, HD), BF16),
            jax.ShapeDtypeStruct((n_blocks, 1, heads * QBLK), F32),
            jax.ShapeDtypeStruct((heads * HD, group), F32),
            jax.ShapeDtypeStruct((group, heads * HD), BF16),
            jax.ShapeDtypeStruct((1, group), jnp.int32),
            jax.ShapeDtypeStruct((group, 1), jnp.int32),
            jax.ShapeDtypeStruct((1, group), jnp.int32),
            jax.ShapeDtypeStruct((group, 1), jnp.int32),
            jax.ShapeDtypeStruct((HD // 2, group), F32),
            jax.ShapeDtypeStruct((HD // 2, group), F32),
            jax.ShapeDtypeStruct((1, width), F32),
            jax.ShapeDtypeStruct((1, width), F32),
            jax.ShapeDtypeStruct((n, rows, width), BF16),
            jax.ShapeDtypeStruct((n, reps, w_rows // reps, cols), BF16),
            jax.ShapeDtypeStruct((2, width, fb), BF16),
        ),
        in_specs=[VMEM] * 3 + [ANY] * 3,
        out_specs=(VMEM,) * 13 + (ANY,) * 3,
        scratch_shapes=[
            pltpu.VMEM((n, 16, w_rows), BF16),
            pltpu.VMEM((rows, width), BF16),
            pltpu.VMEM((n, reps, w_rows // reps, cols), BF16),
            pltpu.VMEM((2, rows, width), BF16),
            pltpu.VMEM((group, cols), BF16),
            pltpu.VMEM((group, 128), F32),
            pltpu.VMEM((group, 128), F32),
            pltpu.VMEM((group, 8), F32),
            pltpu.VMEM((group, 1), F32),
            pltpu.VMEM((8, group), F32),
            pltpu.VMEM((1, group), F32),
            pltpu.VMEM((long_len // QBLK, QBLK, heads * QBLK), F32),
            pltpu.VMEM((HD, group), BF16),
            DMA((n,)),
            DMA((n,)),
            DMA((n,)),
            DMA((n,)),
            DMA((reps,)),
            DMA((reps,)),
            DMA((2, n)),
            DMA((2, n)),
            DMA((3,)),
            DMA(()),
        ]
        + Gather.scratch(n),
        compiler_params=pltpu.CompilerParams(collective_id=4, has_side_effects=True, vmem_limit_bytes=VMEM_BYTES),
        cost_estimate=pl.CostEstimate(flops=2 * group * width * cols, bytes_accessed=300 * 2**20, transcendentals=0),
    )(tok, gains, ids, wqkv, wg, wu)


def weight_copies(gu, wbuf, w_sem):
    blocks, _, _, fb = gu.shape
    own = blocks * fb

    def copy(b, k):
        at = k * own + b * fb
        if not isinstance(at, int):
            at = pl.multiple_of(at, 128)
        return pltpu.make_async_copy(gu.at[b, k], wbuf.at[:, pl.ds(at, fb)], w_sem.at[k, b])

    return copy


def mlp_kernel(
    n, blocks, spread, att, wo, tok, gain, gu_in, cot, wd, normed, middle, hidden, grads, gu_out, cot_all, *scratch
):
    scatter_scratch, scratch = scratch[:8], scratch[8:]
    ag_scratch, cot_scratch, scratch = scratch[:3], scratch[3:6], scratch[6:]
    own_normed, blk, wbuf, wd_buf, grad_hid, hid_stage, grad_stage, w_sem, out_sem, load_sem, x_send, x_recv = scratch
    line = Line(n)
    rows, width = tok.shape
    fb = gu_in.shape[-1]
    own = blocks * fb
    rep = line.replica
    scatter = Scatter(line, scatter_scratch)
    cots = Gather(line, cot, cot_all, cot_scratch)
    gather = Gather(line, own_normed, normed, ag_scratch)
    wd_copy = pltpu.make_async_copy(wd, wd_buf, load_sem.at[1])
    wd_copy.start()
    line.enter(spread)
    cots.start(True)
    if spread:
        gu = gu_out

        def gu_copy(way, k, src, slot, device):
            return remote(src, gu.at[slot, k], x_send.at[way, k], x_recv.at[way, k], (device, line.me))

        firsts = [(0, 0, line.xn), (1, 1, line.yn), (0, 1, line.xn), (1, 0, line.yn)]
        for way, k, device in firsts[:2]:
            gu_copy(way, k, gu_in.at[k], rep, device).start()
        for k in range(2):
            pltpu.make_async_copy(gu_in.at[k], wbuf.at[:, pl.ds(pl.multiple_of(k * own + rep * fb, 128), fb)], w_sem.at[k, rep]).start()
            pltpu.make_async_copy(gu_in.at[k], gu.at[rep, k], load_sem.at[2 + k]).start()
    else:
        gu = gu_in
    weight_copy = weight_copies(gu, wbuf, w_sem)
    if not spread:
        for b in range(blocks):
            for k in range(2):
                weight_copy(b, k).start()

    def out_part(d):
        x = att[rows_of(d, rows), :]
        for t in range(0, width, 512):
            part = dot(x, wo[:, t : t + 512]).astype(BF16)
            scatter.part[rows_of(d, rows), t : t + 512] = part

    scatter.produce(out_part, cots.start_ends)
    wd_copy.wait()

    def grad_hidden(j):
        z = cots.ready(j)
        load(cot_all.at[pl.ds(2 * z, 2)], blk, load_sem.at[0])
        x = blk[...].reshape(2 * rows, width)
        tile = min(256, own)
        for t in range(0, own, tile):
            grad_hid[rows_of(z, rows), t : t + tile] = dot_t(x, wd_buf[t : t + tile, :]).astype(BF16)

    cots.arrive(1, (True,))
    if spread:
        for way, k, device in firsts[2:]:
            gu_copy(way, k, gu_in.at[k], rep, device).start()
    scatter.duty(0)
    cots.arrive(1, (False,))
    grad_hidden(0)
    if spread:
        for way, k, slot, device in ((0, 0, line.xn, line.yn), (1, 1, line.yn, line.xn)):
            gu_copy(way, k, gu.at[slot, k], slot, device).wait_recv()
            gu_copy(2 + way, k, gu.at[slot, k], slot, device).start()
            weight_copy(slot, k).start()

    @pl.loop(1, line.chips - 2)
    def _(s):
        scatter.duty(s)
        cots.arrive(s + 1)
        grad_hidden(s)

    scatter.duty(line.chips - 2)
    scatter.own_sum()

    def norm(at):
        mid = tok[at, :].astype(F32) + scatter.total[at, :]
        middle[at, :] = mid
        inverse = lax.rsqrt(jnp.mean(mid * mid, -1, keepdims=True) + EPSILON)
        own_normed[at, :] = (mid * inverse * gain[...]).astype(BF16)

    row_chunks(rows, norm)
    gather.start()
    cots.arrive(line.chips - 1)
    grad_hidden(line.chips - 2)
    grad_hidden(line.chips - 1)
    if spread:
        for way, k, slot in ((0, 1, line.xn), (1, 0, line.yn)):
            gu_copy(way, k, gu.at[slot, k], slot, line.xn).wait_recv()
            weight_copy(slot, k).start()
        for way, k, device in ((2, 0, line.yn), (3, 1, line.xn)):
            gu_copy(way, k, gu.at[line.diag, k], line.diag, device).wait_recv()
            weight_copy(line.diag, k).start()
    for b in range(blocks):
        for k in range(2):
            weight_copy(b, k).wait()

    def out_copies(z):
        at = rows_of(z, rows)
        return (
            pltpu.make_async_copy(hid_stage, hidden.at[at], out_sem.at[0]),
            pltpu.make_async_copy(grad_stage, grads.at[at], out_sem.at[1]),
        )

    @pl.loop(0, line.chips)
    def _(j):
        @pl.when(j > 0)
        def _():
            gather.arrive(j)

        z = gather.ready(j)
        load(normed.at[pl.ds(2 * z, 2)], blk, load_sem.at[0])

        @pl.when(j > 0)
        def _():
            for copy in out_copies(line.near_first(j - 1)):
                copy.wait()

        at = rows_of(z, rows)
        x = blk[...].reshape(2 * rows, width)
        tile = min(256, own)
        for t in range(0, own, tile):
            gate = dot(x, wbuf[:, t : t + tile])
            up = dot(x, wbuf[:, own + t : own + t + tile])
            sig = 1.0 / (1.0 + jnp.exp(-gate))
            gated = gate * sig
            gh = grad_hid[at, t : t + tile].astype(F32)
            hid_stage[:, t : t + tile] = (gated * up).astype(BF16)
            grad_stage[:, t : t + tile] = (gh * up * sig * (1.0 + gate * (1.0 - sig))).astype(BF16)
            grad_stage[:, own + t : own + t + tile] = (gh * gated).astype(BF16)
        for copy in out_copies(z):
            copy.start()

    for copy in out_copies(line.near_first(line.chips - 1)):
        copy.wait()
    if spread:
        for k in range(2):
            pltpu.make_async_copy(gu_in.at[k], gu.at[rep, k], load_sem.at[2 + k]).wait()
        for way, k, device in firsts:
            gu_copy(way, k, gu_in.at[k], rep, device).wait_send()
        for way, k, slot, device in ((2, 0, line.xn, line.yn), (3, 1, line.yn, line.xn)):
            gu_copy(way, k, gu.at[slot, k], slot, device).wait_send()
    scatter.finish()
    cots.finish()
    gather.finish()


def mlp_forward(n, reps, spread, att, wo, tok, gain, gu, cot, wd):
    rows, width = tok.shape
    group = att.shape[0]
    fb = gu.shape[-1]
    blocks = reps if spread else gu.shape[0]
    own = blocks * fb
    kept = (blocks, 2, width, fb) if spread else (1, 16, 128)
    return pl.pallas_call(
        functools.partial(mlp_kernel, n, blocks, spread),
        name="mlp_forward",
        out_shape=(
            jax.ShapeDtypeStruct((n, rows, width), BF16),
            jax.ShapeDtypeStruct((rows, width), F32),
            jax.ShapeDtypeStruct((group, own), BF16),
            jax.ShapeDtypeStruct((group, 2 * own), BF16),
            jax.ShapeDtypeStruct(kept, BF16),
            jax.ShapeDtypeStruct((n, rows, width), BF16),
        ),
        in_specs=[VMEM, VMEM, VMEM, VMEM, ANY, VMEM, ANY],
        out_specs=(ANY, VMEM, ANY, ANY, ANY, ANY),
        scratch_shapes=Scatter.scratch(n, rows, width)
        + Gather.scratch(n)
        + Gather.scratch(n)
        + [
            pltpu.VMEM((rows, width), BF16),
            pltpu.VMEM((2, rows, width), BF16),
            pltpu.VMEM((width, 2 * own), BF16),
            pltpu.VMEM((own, width), BF16),
            pltpu.VMEM((group, own), BF16),
            pltpu.VMEM((2 * rows, own), BF16),
            pltpu.VMEM((2 * rows, 2 * own), BF16),
            DMA((2, blocks)),
            DMA((2,)),
            DMA((4,)),
            DMA((4, 2)),
            DMA((4, 2)),
        ],
        compiler_params=pltpu.CompilerParams(collective_id=1, has_side_effects=True, vmem_limit_bytes=VMEM_BYTES),
        cost_estimate=pl.CostEstimate(flops=2 * group * width * own * 3, bytes_accessed=400 * 2**20, transcendentals=0),
    )(att, wo, tok, gain, gu, cot, wd)


def norm_back(grad_normed, resid, gain):
    inverse = lax.rsqrt(jnp.mean(resid * resid, -1, keepdims=True) + EPSILON)
    unit = resid * inverse
    scaled = grad_normed * gain
    return inverse * (scaled - unit * jnp.mean(scaled * unit, -1, keepdims=True)), grad_normed * unit


def middle_kernel(
    n, blocks, spread, grads_in, gu, mid, cot, gain, wo, normed, hidden, cot_all, wd, grad_mid, gml, grad_att, gain_sum, output,
    gate_parts, up_parts, down_parts, gate_q, up_q, down_q, down_out, *scratch,
):
    scatter_scratch, ag_scratch, scratch = scratch[:8], scratch[8:11], scratch[11:]
    grads, own_low, blk, wbuf, w_sem, load_sem = scratch[:6]
    line = Line(n)
    rows, width = mid.shape
    group = grads.shape[0]
    fb = gu.shape[-1]
    own = blocks * fb
    scatter = Scatter(line, scatter_scratch)
    gather = Gather(line, own_low, gml, ag_scratch)
    grads_copy = pltpu.make_async_copy(grads_in, grads, load_sem)
    weight_copy = weight_copies(gu, wbuf, w_sem)

    def start_loads():
        grads_copy.start()
        for b in range(blocks):
            for k in range(2):
                weight_copy(b, k).start()

    if not spread:
        start_loads()
    if not spread:
        line.enter(spread)

    def loaded():
        grads_copy.wait()
        for b in range(blocks):
            for k in range(2):
                weight_copy(b, k).wait()

    def normed_part(d):
        x = grads[rows_of(d, rows), :]
        for t in range(0, width, 512):
            part = dot_t(x, wbuf[t : t + 512, :]).astype(BF16)
            scatter.part[rows_of(d, rows), t : t + 512] = part

    if not spread:
        loaded()
        scatter.produce(normed_part)
    tiles = 4
    tile = width // tiles
    if spread:
        gate_land, up_land, down_land, gate_in, up_in, down_in, tmp, tmp_down, stage, part_sem, out_sem, hid_buf, tile_sem = scratch[6:19]
        half = fb // 2
        units = [
            dict(parts=gate_parts, row=0, rows=width, x_first=True, axis=0, land1=gate_land, land2=gate_in, tmp=tmp),
            dict(parts=up_parts, row=0, rows=width, x_first=False, axis=0, land1=up_land, land2=up_in, tmp=tmp),
        ]
        for i in range(2):
            units.append(
                dict(
                    parts=down_parts, row=i * half, rows=half, x_first=i == 0, axis=1,
                    land1=down_land.at[i], land2=down_in.at[i], tmp=tmp_down,
                )
            )
        square = Square(line, units, scratch[19:24])
        d_send, d_recv = scratch[24:26]
        rx, *sems = scratch[26:]
        output_sum = Scatter(line, (grads, scatter.sib, rx, scatter.total, *sems))
        slots = [hid_buf.at[:, pl.ds(own + i * tile, tile)] for i in range(2)]
        hid = hid_buf.at[:, pl.ds(0, own)]

        def column_copy(i):
            src = cot_all if i < tiles else normed
            return pltpu.make_async_copy(src.at[:, pl.ds(i % tiles * tile, tile)], slots[i % 2], tile_sem.at[i % 2])

        hid_copy = pltpu.make_async_copy(hidden, hid, tile_sem.at[2])
        hid_copy.start()
        column_copy(0).start()
        start_loads()
        line.enter(spread)

        def weight_tile(i):
            t = i % tiles
            column_copy(i).wait()
            if i + 1 < 2 * tiles:
                column_copy(i + 1).start()
            if i >= tiles:
                x = slots[i % 2][...]
                for k in range(2):
                    for b in range(blocks):
                        at = k * own + b * fb
                        stage[k, b] = tdot(x, grads[:, at : at + fb]).astype(BF16)
                copies = [
                    pltpu.make_async_copy(stage.at[k, b], parts.at[b, pl.ds(t * tile, tile)], part_sem.at[k, b])
                    for k, parts in enumerate((gate_parts, up_parts))
                    for b in range(blocks)
                ]
            else:
                if i == 0:
                    hid_copy.wait()
                x = slots[i % 2][...]
                for b in range(blocks):
                    part = tdot(hid[:, b * fb : (b + 1) * fb], x).astype(BF16)
                    for k in range(2):
                        stage[k, b, :fb, :] = part[:, k * fb : (k + 1) * fb]
                copies = [
                    pltpu.make_async_copy(
                        stage.at[k, b, pl.ds(0, fb)], down_parts.at[b, :, pl.ds(t * tile + k * fb, fb)], part_sem.at[k, b]
                    )
                    for k in range(2)
                    for b in range(blocks)
                ]
            for copy in copies:
                copy.start()
            for copy in copies:
                copy.wait()

        piece = half // 2

        def place(i, replica):
            at = replica * half + i * piece
            return down_out.at[pl.ds(pl.multiple_of(at, 16), piece)]

        def down_piece(i):
            return units[2]["land1"].at[0, pl.ds(i * piece, piece)]

        def down_send(way, i, src, replica, device):
            return remote(src, place(i, replica), d_send.at[way, i], d_recv.at[way, i], (device, line.me))

        def down_firsts(i):
            return [
                down_send(way, i, down_piece(i), line.replica, device) for way, device in enumerate((line.xn, line.yn))
            ]

        def down_second(i):
            replica, device = ((line.xn, line.yn), (line.yn, line.xn))[i]
            return down_send(2 + i, i, place(i, replica), replica, device)

        def down_local(i):
            return pltpu.make_async_copy(down_piece(i), place(i, line.replica), out_sem.at[2 + i])

        rest_copy = pltpu.make_async_copy(units[3]["land1"].at[0], down_q, out_sem.at[4])

        def down_tile(i):
            if i < tiles:
                weight_tile(i)
                square.start(2, i)
                square.start(3, i)

        down_tile(0)
        loaded()
        scatter.produce(normed_part, None, lambda s: down_tile(s + 1))
        for i in range(line.chips + 1, tiles):
            down_tile(i)
        scatter.duty(0, (True,))
        for i in range(2):
            weight_tile(tiles + i)
            square.start(0, i)
            square.start(1, i)
        scatter.duty(0, (False,))
        square.fold(2)
        square.fold(3)
        scatter.duty(1)
        for i in range(2, 4):
            weight_tile(tiles + i)
            square.start(0, i)
            square.start(1, i)
        scatter.duty(2)
    else:
        for s in range(line.chips - 1):
            scatter.duty(s)
    scatter.own_sum()
    gain_sum[...] = jnp.zeros_like(gain_sum)

    def back(at):
        through, gain_term = norm_back(scatter.total[at, :], mid[at, :], gain[...])
        value = cot[at, :].astype(F32) + through
        grad_mid[at, :] = value
        own_low[at, :] = value.astype(BF16)
        gain_sum[...] += jnp.sum(gain_term, 0, keepdims=True)

    row_chunks(rows, back)
    gather.start()

    def attended_part(j, z=None):
        if z is None:
            z = gather.ready(j)
        load(gml.at[pl.ds(2 * z, 2)], blk, load_sem)
        grad_att[rows_of(z, rows), :] = dot_t(blk[...].reshape(2 * rows, width), wo[...]).astype(BF16)

    if spread:

        def down_copy(i):
            place = wbuf.at[pl.ds(0, own), pl.ds(i % 2 * tile, tile)]
            return pltpu.make_async_copy(wd.at[:, pl.ds(i * tile, tile)], place, w_sem.at[0, i % 2])

        down_copy(0).start()
        for i in range(tiles):
            down_copy(i).wait()
            if i + 1 < tiles:
                down_copy(i + 1).start()
            for d in range(line.chips):
                at = pl.ds(d * 2 * rows, 2 * rows)
                x = dot(hid[at, :], wbuf[:own, i % 2 * tile : (i % 2 + 1) * tile])
                grads[at, i * tile : (i + 1) * tile] = x.astype(BF16)
        here = gather.ready(0)
        output_sum.produce(lambda d: None)
        gather.arrive(1)
        attended_part(0, here)
        square.result(2)
        for i in range(2):
            for copy in down_firsts(i):
                copy.start()
            down_local(i).start()
        square.result(3)
        rest_copy.start()
        square.fold(0)
        square.fold(1)
        gather.arrive(2)
        attended_part(1)
        output_sum.duty(0)
        gather.arrive(3)
        attended_part(2)
        attended_part(3)
        for i in range(2):
            replica = (line.xn, line.yn)[i]
            down_send(i, i, place(i, replica), replica, replica).wait_recv()
            down_second(i).start()
        output_sum.duty(1)
        output_sum.duty(2)
        copies = []
        for u, out in ((0, gate_q), (1, up_q)):
            square.result(u)
            copies.append(pltpu.make_async_copy(units[u]["land1"].at[0], out, out_sem.at[u]))
            copies[-1].start()
        output_sum.own_sum()

        def put(at):
            output[at, :] = (mid[at, :] + scatter.total[at, :]).astype(BF16)

        row_chunks(rows, put)
        output_sum.finish()
        rest_copy.wait()
        for i in range(2):
            for copy in down_firsts(i):
                copy.wait_send()
            down_second(i).wait_send()
            down_local(i).wait()
            replica, far = ((line.xn, line.yn), (line.yn, line.xn))[i]
            down_send(2 + i, i, place(i, line.diag), line.diag, replica).wait_recv()
            down_send(1 - i, i, place(i, far), far, far).wait_recv()
        for copy in copies:
            copy.wait()
        square.finish()
    else:

        @pl.loop(0, line.chips)
        def _(j):
            @pl.when(j > 0)
            def _():
                gather.arrive(j)

            attended_part(j)

    scatter.finish()
    gather.finish()


def middle_backward(n, spread, grads, gu, mid, cot, gain, wo, normed, hidden, cot_all, wd):
    rows, width = mid.shape
    group = grads.shape[0]
    blocks, _, _, fb = gu.shape
    own = blocks * fb
    parts = [(4, width, fb), (4, width, fb), (4, fb, width), (width, fb), (width, fb), (fb // 2, width), (2 * fb, width)]
    if not spread:
        parts = [(16, 128)] * 7
    scratch = []
    if spread:
        scratch = [
            pltpu.VMEM((2, width, fb), BF16),
            pltpu.VMEM((2, width, fb), BF16),
            pltpu.VMEM((2, 2, fb // 2, width), BF16),
            pltpu.VMEM((width, fb), BF16),
            pltpu.VMEM((width, fb), BF16),
            pltpu.VMEM((2, fb // 2, width), BF16),
            pltpu.VMEM((width, fb), BF16),
            pltpu.VMEM((fb // 2, width), BF16),
            pltpu.VMEM((2, blocks, width // 4, fb), BF16),
            DMA((2, blocks)),
            DMA((5,)),
            pltpu.VMEM((group, own + width // 2), BF16),
            DMA((3,)),
        ] + Square.scratch(4, 4) + [DMA((4, 2)), DMA((4, 2))]
        again = Scatter.scratch(n, rows, width)
        scratch += again[2:3] + again[4:]
    return pl.pallas_call(
        functools.partial(middle_kernel, n, blocks, spread),
        name="middle_backward",
        out_shape=(
            jax.ShapeDtypeStruct((rows, width), F32),
            jax.ShapeDtypeStruct((n, rows, width), BF16),
            jax.ShapeDtypeStruct((group, wo.shape[0]), BF16),
            jax.ShapeDtypeStruct((1, width), F32),
            jax.ShapeDtypeStruct((rows, width) if spread else (16, 128), BF16),
            *[jax.ShapeDtypeStruct(shape, BF16) for shape in parts],
        ),
        in_specs=[ANY, ANY, VMEM, VMEM, VMEM, VMEM, ANY, ANY, ANY, ANY],
        out_specs=(VMEM, ANY, VMEM, VMEM, VMEM) + (ANY,) * 7,
        scratch_shapes=Scatter.scratch(n, rows, width)
        + Gather.scratch(n)
        + [
            pltpu.VMEM((group, 2 * own), BF16),
            pltpu.VMEM((rows, width), BF16),
            pltpu.VMEM((2, rows, width), BF16),
            pltpu.VMEM((width, 2 * own), BF16),
            DMA((2, blocks)),
            DMA(()),
        ]
        + scratch,
        compiler_params=pltpu.CompilerParams(collective_id=2, has_side_effects=True, vmem_limit_bytes=62 * 2**20),
        cost_estimate=pl.CostEstimate(flops=2 * group * width * own * 3, bytes_accessed=400 * 2**20, transcendentals=0),
    )(grads, gu, mid, cot, gain, wo, normed, hidden, cot_all, wd)


def end_kernel(
    n, reps, spread, heads, long_len, q_in, kv, lse, att_t, grad_att, rank_row, rank_col, seg_row, seg_col, cos_t, sin_t,
    w, tok, grad_mid, gain, gain_m_sum, attended, gate_q, up_q, down_q, normed, gml,
    grad_tok, gain_grads, grads, gate_out, up_out, down_out, q_out, kv_out, out_out, *scratch,
):
    scatter_scratch, att_scratch, scratch = scratch[:8], scratch[8:13], scratch[13:]
    gain_sum, gain_src, gain_land, gain_all, g_send, g_recv = scratch[:6]
    line = Line(n)
    rows, width = tok.shape
    me, rep = line.me, line.replica
    scatter = Scatter(line, scatter_scratch)
    line.enter_all(reps)
    if spread:
        (
            a_send, a_recv, x_send, x_recv, local_sem, qkv_land, qkv_in, out_land, out_in, qkv_tmp, out_tmp,
            qkv_parts, out_parts, slots, slot_sem,
        ) = scratch[6:21]
        fb = gate_q.shape[-1]
        own = 4 * fb
        quarters, outs = (gate_q, up_q), (gate_out, up_out)
        w_rows = gate_out.shape[0]
        down_rows = down_q.shape[0] // 2
        q_cols = heads * HD
        qkv_rows = w_rows // 4
        out_rows = out_parts.shape[1] // 2
        counts = (n, n, 2, n, 2, n)
        units = [
            dict(
                parts=qkv_parts, row=i * 4 * qkv_rows, rows=4 * qkv_rows, x_first=i == 0,
                land1=qkv_land.at[i], land2=qkv_in.at[i], tmp=qkv_tmp,
            )
            for i in range(2)
        ] + [
            dict(
                parts=out_parts, row=i * out_rows, rows=out_rows, x_first=i == 0,
                land1=out_land.at[i], land2=out_in.at[i], tmp=out_tmp,
            )
            for i in range(2)
        ]
        square = Square(line, units, scratch[21:])

        def place(k, f, replica):
            if k == 2:
                return down_out.at[pl.ds(pl.multiple_of(replica * 2 * down_rows + f * down_rows, 16), down_rows)]
            if k in (3, 5):
                at = pl.ds(pl.multiple_of(replica * qkv_rows, 16), qkv_rows)
                if k == 3:
                    return q_out.at[at, pl.ds(pl.multiple_of(f * q_cols, 128), q_cols)]
                return kv_out.at[at, pl.ds(pl.multiple_of(f * 2 * HD, 128), 2 * HD)]
            if k == 4:
                return out_out.at[pl.ds(pl.multiple_of(replica * 2 * out_rows + f * out_rows, 16), out_rows)]
            return outs[k].at[:, pl.ds(pl.multiple_of(f * own + replica * fb, 128), fb)]

        def block(k, f):
            if k in (3, 5):
                half, inner = lax.div(f, 4), lax.rem(f, 4)
                cols = pl.ds(0, q_cols) if k == 3 else pl.ds(q_cols, 2 * HD)
                return qkv_land.at[half, 0, pl.ds(pl.multiple_of(inner * qkv_rows, 16), qkv_rows), cols]
            return quarters[k].at[pl.ds(pl.multiple_of(f * w_rows, 16), w_rows)]

        def exchange(k, to, at):
            return remote(block(k, to), place(k, at, rep), a_send.at[k, to], a_recv.at[k, at], (rep, to))

        def exchange_at(d, kinds):
            if d == 0:
                for k in kinds:
                    exchange(k, 2 * line.z + 1 - line.c, me).start()
                return
            for to in (line.z + d, line.z - d):

                @pl.when((to >= 0) & (to < line.chips))
                def _():
                    for core in range(2):
                        for k in kinds:
                            exchange(k, 2 * to + core, me).start()

        def send(way, k, f, src, replica, device):
            return remote(src, place(k, f, replica), x_send.at[way, k, f], x_recv.at[way, k, f], (device, me))

        def share(k, f, src):
            send(0, k, f, src, rep, line.xn).start()
            send(1, k, f, src, rep, line.yn).start()

        def corner(core):
            return (0, line.xn, line.yn) if core % 2 == 0 else (1, line.yn, line.xn)

        def forward_all(z, kinds):
            for k in kinds:
                for core in range(2):
                    forward(k, 2 * z + core, core)

        def forward(k, f, core):
            way, replica, device = corner(core)
            src = place(k, f, replica)
            send(way, k, f, src, replica, replica).wait_recv()
            send(2 + way, k, f, src, replica, device).start()

        def local(i, src, dst):
            return pltpu.make_async_copy(src, dst, local_sem.at[i])

        def mine(k):
            return local(k, block(k, me), place(k, me, rep))

        def down_piece(i):
            return down_q.at[pl.ds(i * down_rows, down_rows)]

        def mine_down(i):
            return local((2, 4)[i], down_piece(i), place(2, i, rep))

        def mine_out(i):
            return local(6 + i, out_land.at[i, 0], place(4, i, rep))

        fetches = [pltpu.make_async_copy(src, slots.at[i], slot_sem.at[i]) for i, src in enumerate((gml, normed))]

        def stream(i, use):
            fetches[i].wait()
            for t in range(0, width, 512):
                use(t, slots[i, :, t : t + 512])

        def out_tile(at, x):
            part = tdot(attended[...], x).astype(BF16)
            for b in range(4):
                out_parts[b, :, at : at + x.shape[1]] = part[b * 2 * out_rows : (b + 1) * 2 * out_rows]

        def qkv_tile(at, x):
            part = tdot(x, grads[...]).astype(BF16)
            for i in range(x.shape[1] // w_rows):
                f = at // w_rows + i
                for b in range(4):
                    piece = part[i * w_rows + b * qkv_rows : i * w_rows + (b + 1) * qkv_rows]
                    qkv_parts[b, f * qkv_rows : (f + 1) * qkv_rows, :] = piece

        for fetch in fetches:
            fetch.start()
        for k in range(2):
            share(k, me, block(k, me))
            mine(k).start()
        for i in range(2):
            share(2, i, down_piece(i))
            mine_down(i).start()
        exchange_at(0, (0, 1))
        exchange_at(1, (0, 1))
        stream(0, out_tile)
        square.start(2)
        square.start(3)

    def pass_on(z, kinds):
        for core in range(2):
            f = 2 * z + core

            @pl.when(f != me)
            def _():
                for k in kinds:
                    exchange(k, me, f).wait_recv()
                    share(k, f, place(k, f, rep))

    def after_block(b):
        if not spread:
            return
        if b == 0:
            pass_on(line.near_first(0), (0, 1))
            exchange_at(2, (0, 1))
        if b == 2:
            for d in range(3, line.chips):
                exchange_at(d, (0, 1))

    attention_back_kernel(
        heads, long_len, q_in, kv, lse, att_t, grad_att, rank_row, rank_col, seg_row, seg_col, cos_t, sin_t, grads,
        *att_scratch, after_block,
    )
    if spread:
        stream(1, qkv_tile)
        square.start(0)
        square.start(1)
        pass_on(line.near_first(1), (0, 1))

    def normed_part(d):
        x = grads[rows_of(d, rows), :]
        for t in range(0, width, 512):
            part = dot_t(x, w[t : t + 512, :]).astype(BF16)
            scatter.part[rows_of(d, rows), t : t + 512] = part

    scatter.produce(normed_part, hold_last=spread)
    if spread:
        for u in range(4):
            square.fold(u)
        for i in range(2):
            forward(2, i, i)
        forward_all(line.near_first(0), (0, 1))
        square.result(0)
        square.result(1)
        for d in range(line.chips):
            exchange_at(d, (3, 5))
        for k in (3, 5):
            share(k, me, block(k, me))
            mine(k).start()
        scatter.emit_last()
        square.result(2)
        square.result(3)
        for i in range(2):
            share(4, i, out_land.at[i, 0])
            mine_out(i).start()
        pass_on(line.near_first(2), (0, 1))
        forward_all(line.near_first(1), (0, 1))
    for s in range(line.chips - 1):
        scatter.duty(s)
        if spread:
            if s == 0:
                pass_on(line.near_first(3), (0, 1))
            if s == 1:
                forward_all(line.near_first(2), (0, 1))
                for i in range(2):
                    forward(4, i, i)
            if s == 2:
                forward_all(line.near_first(3), (0, 1))
    scatter.own_sum()
    gain_sum[...] = jnp.zeros_like(gain_sum)

    def back(at):
        through, gain_term = norm_back(scatter.total[at, :], tok[at, :].astype(F32), gain[...])
        grad_tok[at, :] = grad_mid[at, :] + through
        gain_sum[...] += jnp.sum(gain_term, 0, keepdims=True)

    row_chunks(rows, back)

    g_rows = gain_grads.shape[1]
    gain_src[...] = jnp.zeros_like(gain_src)
    for f in range(n):
        gain_src[f, 0:1, :] = gain_sum[:, f * g_rows : (f + 1) * g_rows]
        gain_src[f, 1:2, :] = gain_m_sum[:, f * g_rows : (f + 1) * g_rows]

    def gain_copy(i, to, slot):
        return remote(gain_src.at[to], gain_land.at[slot], g_send.at[0, i], g_recv.at[0, slot], (rep, to))

    def gain_share(i, to, slot):
        return remote(gain_all.at[slot], gain_all.at[slot], g_send.at[1, i], g_recv.at[1, slot], (to, me))

    for i in range(1, n):
        gain_copy(i, line.other(i), me).start()
    gain_land[me] = gain_src[me]
    if spread:
        for j in range(line.chips):
            pass_on(line.near_first(j), (3, 5))
    for i in range(1, n):
        gain_copy(i, me, line.other(i)).wait_recv()
    gain_all[rep] = functools.reduce(lambda a, b: a + b, [gain_land[i] for i in range(n)])
    for i in range(1, reps):
        gain_share(i, lax.rem(rep + i, reps), rep).start()
    if spread:
        for j in range(line.chips):
            forward_all(line.near_first(j), (3, 5))
    for i in range(1, reps):
        gain_share(i, rep, lax.rem(rep + i, reps)).wait_recv()
    gain_grads[...] = functools.reduce(lambda a, b: a + b, [gain_all[i] for i in range(reps)])
    for i in range(1, n):
        gain_copy(i, line.other(i), me).wait_send()
    for i in range(1, reps):
        gain_share(i, lax.rem(rep + i, reps), rep).wait_send()
    if spread:
        for k in (0, 1, 3, 5):
            mine(k).wait()
        for i in range(2):
            mine_out(i).wait()
            mine_down(i).wait()
        for k in (0, 1, 3, 5):
            for i in range(1, n):
                exchange(k, line.other(i), me).wait_send()
        for k in range(6):
            for f in range(counts[k]):
                src = place(k, f, rep)
                send(0, k, f, src, rep, line.xn).wait_send()
                send(1, k, f, src, rep, line.yn).wait_send()
                way, replica, device = corner(f)
                send(2 + way, k, f, src, replica, device).wait_send()
                send(2 + way, k, f, src, line.diag, replica).wait_recv()
                far = (line.yn, line.xn)[way]
                send(1 - way, k, f, src, far, far).wait_recv()
        square.finish()
    scatter.finish()


def end_layer(
    n, reps, spread, heads, long_len, q_in, kv, lse, att_t, grad_att, ranks, cos_t, sin_t,
    w, tok, grad_mid, gain, gain_m_sum, attended, gate_q, up_q, down_q, normed, gml,
):
    rows, width = tok.shape
    group = attended.shape[0]
    n_blocks = group // QBLK
    cols = w.shape[1]
    w_rows = width // n
    shapes, scratch = [(16, 128)] * 6, []
    if spread:
        fb = gate_q.shape[-1]
        own = 4 * fb
        heads_rows = attended.shape[1] // 4
        q_rows = w_rows // 4
        shapes = [(w_rows, n * own)] * 2 + [(2 * fb, width), (w_rows, n * heads * HD), (w_rows, n * 2 * HD), (4 * heads_rows, width)]
        scratch = [
            DMA((6, n)),
            DMA((6, n)),
            DMA((4, 6, n)),
            DMA((4, 6, n)),
            DMA((8,)),
            pltpu.VMEM((2, 2, 4 * q_rows, cols), BF16),
            pltpu.VMEM((2, 4 * q_rows, cols), BF16),
            pltpu.VMEM((2, 2, heads_rows // 2, width), BF16),
            pltpu.VMEM((2, heads_rows // 2, width), BF16),
            pltpu.VMEM((4 * q_rows, cols), BF16),
            pltpu.VMEM((heads_rows // 2, width), BF16),
            pltpu.VMEM((4, width // 4, cols), BF16),
            pltpu.VMEM((4, heads_rows, width), BF16),
            pltpu.VMEM((2, group, width), BF16),
            DMA((2,)),
        ] + Square.scratch(4, 1)
    return pl.pallas_call(
        functools.partial(end_kernel, n, reps, spread, heads, long_len),
        name="end_layer",
        out_shape=(
            jax.ShapeDtypeStruct((rows, width), F32),
            jax.ShapeDtypeStruct((8, w_rows), F32),
            jax.ShapeDtypeStruct((group, cols), BF16),
            *[jax.ShapeDtypeStruct(shape, BF16) for shape in shapes],
        ),
        in_specs=[VMEM] * 17 + [ANY] * 5,
        out_specs=(VMEM, VMEM, VMEM) + (ANY,) * 6,
        scratch_shapes=Scatter.scratch(n, rows, width)
        + [
            pltpu.VMEM((2, group, HD), F32),
            pltpu.VMEM((cols, group), BF16),
            pltpu.VMEM((HD, group), BF16),
            pltpu.VMEM((n_blocks, heads * QBLK, HD), BF16),
            pltpu.VMEM((heads * HD, group), F32),
            pltpu.VMEM((1, width), F32),
            pltpu.VMEM((n, 8, w_rows), F32),
            pltpu.VMEM((n, 8, w_rows), F32),
            pltpu.VMEM((reps, 8, w_rows), F32),
            DMA((2, max(n, reps))),
            DMA((2, max(n, reps))),
        ]
        + scratch,
        compiler_params=pltpu.CompilerParams(collective_id=3, has_side_effects=True, vmem_limit_bytes=VMEM_BYTES),
        cost_estimate=pl.CostEstimate(flops=2 * group * width * cols, bytes_accessed=400 * 2**20, transcendentals=0),
    )(
        q_in, kv, lse, att_t, grad_att, *ranks, cos_t, sin_t, w, tok, grad_mid, gain, gain_m_sum, attended,
        gate_q, up_q, down_q, normed, gml,
    )


def body(
    tokens, segment, position, attn_gain, w_query, w_key, w_value, w_out, mlp_gain, w_gate, w_up, w_down, cotangent
):
    rows, width = tokens.shape
    group = segment.shape[0]
    long_len = group * 2 // 3
    n = lax.axis_size("fsdp")
    reps = lax.axis_size("replica")
    w_rows = w_query.shape[0]
    ff_own = w_gate.shape[1] // n
    ff_blk = ff_own // reps
    heads = H // n
    q_cols = heads * HD
    dup = n // KVH
    spread = reps == 4 and ff_blk % 128 == 0

    def swap(x):
        return lax.all_to_all(x, "fsdp", 0, 0, tiled=True)

    ids = jnp.concatenate([segment[None], position[None], jnp.zeros((6, group), jnp.int32)]).astype(F32)
    gains = jnp.concatenate([attn_gain[None], mlp_gain[None], jnp.zeros((14, w_rows), BF16)])
    kv_w = jnp.concatenate([w_key.reshape(w_rows, KVH, HD), w_value.reshape(w_rows, KVH, HD)], -1)
    kv_w = jnp.repeat(kv_w, dup, axis=1)
    qkv_w = jnp.concatenate([w_query.reshape(w_rows, n, q_cols), kv_w], -1).transpose(1, 0, 2)
    (
        q_in, kv, lse, att_t, attended, *ranks, cos_back, sin_back, gain_a, gain_m, normed_all, qkv_w, gu_own,
    ) = start_layer(
        n, reps, spread, heads, long_len, tokens, gains, ids, qkv_w, w_gate, w_up
    )
    normed_all = normed_all.reshape(group, width)
    qkv_w = qkv_w.reshape(width, q_cols + 2 * HD)
    if not spread:
        gate_up = jnp.stack([w.reshape(w_rows, n, ff_own).transpose(1, 0, 2) for w in (w_gate, w_up)], 1)
        gu_own = swap(gate_up).transpose(1, 0, 2, 3).reshape(1, 2, width, ff_own)
    normed_mlp, middle, hidden, grads, gate_up, cot_all = mlp_forward(
        n, reps, spread, attended, w_out, tokens, gain_m, gu_own, cotangent, w_down
    )
    normed_mlp, cot_all = normed_mlp.reshape(group, width), cot_all.reshape(group, width)
    if not spread:
        gate_up = gu_own

    def over_replicas(x):
        return lax.psum_scatter(x, "replica", scatter_dimension=0, tiled=True)

    grad_mid, gml, grad_att, gain_m_sum, output, _, _, _, gate_q, up_q, down_q, down_first = middle_backward(
        n, spread, grads, gate_up, middle, cotangent, gain_m, w_out, normed_mlp, hidden, cot_all, w_down
    )
    gml = gml.reshape(group, width)
    if not spread:

        def column_blocks(first):
            grad = tdot(normed_mlp, grads[:, first : first + ff_own]).astype(BF16)
            return grad.reshape(width, reps, ff_blk).transpose(1, 0, 2).reshape(reps * width, ff_blk)

        gate_q, up_q = over_replicas(column_blocks(0)), over_replicas(column_blocks(ff_own))
        down_q = over_replicas(tdot(hidden, cot_all).astype(BF16))
        down = lax.psum_scatter(dot(hidden, w_down).astype(BF16), "fsdp", scatter_dimension=0, tiled=True)
        output = (middle + down.astype(F32)).astype(BF16)
    grad_tokens, gain_grads, grad_qkv, grad_gate, grad_up, down_second, grad_w_query, grad_kv, grad_out_w = end_layer(
        n, reps, spread, heads, long_len, q_in, kv, lse, att_t, grad_att, ranks, cos_back, sin_back,
        qkv_w, tokens, grad_mid, gain_a, gain_m_sum, attended, gate_q, up_q, down_q, normed_all, gml,
    )
    if spread:
        halves = [x.reshape(reps, ff_blk // 2, width) for x in (down_first, down_second)]
        grad_down = jnp.stack(halves, 1).reshape(ff_own, width)
    else:

        def by_rows(grad):
            grad = swap(grad.reshape(n, w_rows, -1))
            grad = lax.all_gather(grad, "replica", axis=0, tiled=False)
            return grad.transpose(2, 1, 0, 3).reshape(w_rows, -1)

        grad_gate, grad_up = by_rows(gate_q), by_rows(up_q)
        grad_down = lax.all_gather(down_q, "replica", axis=0, tiled=True)
        grad_w = tdot(normed_all, grad_qkv).astype(BF16)
        grad_w = grad_w.reshape(n, reps, w_rows // reps, -1).transpose(1, 0, 2, 3)
        grad_w = over_replicas(grad_w)[0]
        grad_w = lax.all_gather(swap(grad_w), "replica", axis=0, tiled=False)
        grad_w = grad_w.transpose(0, 2, 1, 3).reshape(w_rows, n, -1)
        grad_w_query, grad_kv = grad_w[:, :, :q_cols].reshape(w_rows, H * HD), grad_w[:, :, q_cols:]
        grad_out_w = lax.psum(tdot(attended, gml).astype(BF16), "replica")
    grad_kv = grad_kv.reshape(w_rows, KVH, dup, 2 * HD).astype(F32).sum(2)
    grad_w_key = grad_kv[:, :, :HD].reshape(w_rows, KVH * HD)
    grad_w_value = grad_kv[:, :, HD:].reshape(w_rows, KVH * HD)
    return (
        output,
        grad_tokens,
        gain_grads[0],
        grad_w_query.astype(F32),
        grad_w_key,
        grad_w_value,
        grad_out_w.astype(F32),
        gain_grads[1],
        grad_gate.astype(F32),
        grad_up.astype(F32),
        grad_down.astype(F32),
    )


def solution(mesh):
    both = P(("replica", "fsdp"), None)
    mat = P("fsdp", None)
    vec = P("fsdp")
    return jax.shard_map(
        body,
        mesh=mesh,
        in_specs=(both, P("replica"), P("replica"), vec, mat, mat, mat, mat, vec, mat, mat, mat, both),
        out_specs=(both, both, vec, mat, mat, mat, mat, vec, mat, mat, mat),
        check_vma=False,
    )
```

```python
import functools
import math

import jax
import jax.numpy as jnp
from jax import lax
from jax.experimental import pallas as pl
from jax.experimental.pallas import tpu as pltpu
from jax.sharding import PartitionSpec as P

H = 32
KVH = 8
HD = 64
EPSILON = 1e-05
ROPE_BASE = 500000.0
MASKED = -1e30
QBLK = 256
F32 = jnp.float32
BF16 = jnp.bfloat16
MESH = pl.DeviceIdType.MESH
VMEM = pl.BlockSpec(memory_space=pltpu.VMEM)
ANY = pl.BlockSpec(memory_space=pl.ANY)
DMA = pltpu.SemaphoreType.DMA
VMEM_BYTES = 60 * 2**20


def dot(a, b):
    return jnp.dot(a, b, preferred_element_type=F32)


def tdot(a, b):
    return lax.dot_general(a, b, (((0,), (0,)), ((), ())), preferred_element_type=F32)


def dot_t(a, b):
    return lax.dot_general(a, b, (((1,), (1,)), ((), ())), preferred_element_type=F32)


class Line:
    def __init__(self, n):
        f = lax.axis_index("fsdp")
        self.n = n
        self.replica = lax.axis_index("replica")
        self.chips = n // 2
        self.z = lax.div(f, 2)
        self.c = lax.rem(f, 2)
        self.me = f
        x, y = lax.rem(self.replica, 2), lax.div(self.replica, 2)
        self.xn, self.yn = self.replica + 1 - 2 * x, self.replica + 2 - 4 * y
        self.diag = 3 - self.replica

    def dev(self, z, c):
        return (self.replica, 2 * z + c)

    def other(self, i):
        return lax.rem(self.me + i, self.n)

    def enter(self, square=False):
        barrier = pltpu.get_barrier_semaphore()
        z, c = self.z, self.c

        def greet(device):
            pl.semaphore_signal(barrier, inc=1, device_id=device, device_id_type=MESH)

        greet(self.dev(z, 1 - c))

        @pl.when(z > 0)
        def _():
            greet(self.dev(z - 1, c))

        @pl.when(z < self.chips - 1)
        def _():
            greet(self.dev(z + 1, c))

        count = 1 + (z > 0).astype(jnp.int32) + (z < self.chips - 1).astype(jnp.int32)
        if square:
            greet((self.xn, self.me))
            greet((self.yn, self.me))
            count = count + 2
        pl.semaphore_wait(barrier, count)

    def enter_all(self, reps, square=False):
        barrier = pltpu.get_barrier_semaphore()

        def greet(device):
            pl.semaphore_signal(barrier, inc=1, device_id=device, device_id_type=MESH)

        for i in range(1, self.n):
            greet((self.replica, self.other(i)))
        if square:
            greet((self.xn, self.me))
            greet((self.yn, self.me))
        else:
            for i in range(1, reps):
                greet((lax.rem(self.replica + i, reps), self.me))
        pl.semaphore_wait(barrier, self.n - 1 + (2 if square else reps - 1))

    def far_first(self, s):
        z, last = self.z, self.chips - 1
        right = last - z
        low = jnp.where(s < right, last - s, s - right)
        high = jnp.where(s < z, s, last - (s - z))
        return jnp.where(2 * z < self.chips, low, high)

    def near_first(self, j):
        z, last = self.z, self.chips - 1
        short = jnp.minimum(z, last - z)
        half = lax.div(j + 1, 2)
        both = jnp.where(lax.rem(j, 2) == 1, z - half, z + half)
        rest = jnp.where(2 * z < self.chips, j, last - j)
        return jnp.where(j <= 2 * short, both, rest)


def remote(src, dst, send, recv, device):
    return pltpu.make_async_remote_copy(
        src_ref=src, dst_ref=dst, send_sem=send, recv_sem=recv, device_id=device, device_id_type=MESH
    )


def row_step(rows):
    return 32 if rows % 32 == 0 else 16


def row_chunks(rows, fn):
    step = row_step(rows)

    @pl.loop(0, rows // step)
    def _(i):
        fn(pl.ds(pl.multiple_of(i * step, step), step))


PARTS = 2


class Scatter:
    @staticmethod
    def scratch(n, rows, width):
        chips = n // 2
        return [
            pltpu.VMEM((n * rows, width), BF16),
            pltpu.VMEM((chips, rows, width), BF16),
            pltpu.VMEM((chips + 1, rows, width), BF16),
            pltpu.VMEM((rows, width), F32),
            DMA((chips,)),
            DMA((chips,)),
            DMA((chips, PARTS)),
            DMA((chips + 1, PARTS)),
        ]

    def __init__(self, line, scratch):
        self.line = line
        self.part, self.sib, self.rx, self.total = scratch[:4]
        self.sib_send, self.sib_recv, self.line_send, self.line_recv = scratch[4:]
        self.rows, self.width = self.total.shape
        self.rows_q = self.rows // PARTS

    def rows_at(self, d, c, first=0, count=None):
        at = (2 * d + c) * self.rows + first
        return pl.ds(pl.multiple_of(at, 16), self.rows if count is None else count)

    def to_sibling(self, d):
        line = self.line
        return remote(
            self.part.at[self.rows_at(d, 1 - line.c)], self.sib.at[d], self.sib_send.at[d], self.sib_recv.at[d], line.dev(line.z, 1 - line.c)
        )

    def along(self, d, slot, q, z):
        c = self.line.c
        at = pl.ds(q * self.rows_q, self.rows_q)
        return remote(
            self.part.at[self.rows_at(d, c, q * self.rows_q, self.rows_q)], self.rx.at[slot, at], self.line_send.at[d, q], self.line_recv.at[slot, q], self.line.dev(z, c)
        )

    def to_right(self, d, q):
        return self.along(d, d, q, self.line.z + 1)

    def to_left(self, d, q):
        z = self.line.z
        return self.along(d, jnp.where(d == z - 1, self.line.chips, d), q, z - 1)

    def wait_line(self, slot, q):
        line = self.line
        at = pl.ds(q * self.rows_q, self.rows_q)
        here = self.rx.at[slot, at]
        remote(here, here, self.line_send.at[0, q], self.line_recv.at[slot, q], line.dev(line.z, 1 - line.c)).wait_recv()

    def add(self, d, q, with_line):
        step = row_step(self.rows_q)
        c = self.line.c

        @pl.loop(0, self.rows_q // step)
        def _(i):
            at = pl.ds(pl.multiple_of(q * self.rows_q + i * step, step), step)
            here = self.rows_at(d, c, q * self.rows_q + i * step, step)
            value = self.part[here, :].astype(F32) + self.sib[d, at, :].astype(F32)
            if with_line:
                value = value + self.rx[d, at, :].astype(F32)
            self.part[here, :] = value.astype(BF16)

    def emit(self, d):
        z = self.line.z
        self.to_sibling(d).wait_recv()
        for q in range(PARTS):
            self.add(d, q, False)

            @pl.when(z == 0)
            def _():
                self.to_right(d, q).start()

            @pl.when(z > 0)
            def _():
                self.to_left(d, q).start()

    def emit_last(self):
        line = self.line

        @pl.when((line.z == 0) | (line.z == line.chips - 1))
        def _():
            self.emit(line.far_first(line.chips - 2))

    def produce(self, compute, after_first=None, between=None, hold_last=False):
        line = self.line
        chips, z = line.chips, line.z

        def step(s):
            d = line.far_first(s)
            compute(d)
            self.to_sibling(d).start()

            @pl.when(((z == 0) | (z == chips - 1)) & (s > 0) & (s < (chips - 1 if hold_last else chips)))
            def _():
                self.emit(line.far_first(s - 1))
                if after_first is not None:

                    @pl.when(s == 1)
                    def _():
                        after_first()

        if between is None:
            pl.loop(0, chips)(step)
        else:
            for s in range(chips):
                step(s)
                between(s)

    def duty(self, s, sides=(True, False)):
        chips, z, c = self.line.chips, self.line.z, self.line.c
        for near in sides:
            right = (2 * z < chips) if near else (2 * z >= chips)
            d = jnp.where(right, chips - 1 - s, s)
            active = jnp.where(right, (z > 0) & (d > z), (z < chips - 1) & (d < z))

            @pl.when(active)
            def _():
                self.to_sibling(d).wait_recv()
                for q in range(PARTS):
                    self.wait_line(d, q)
                    self.add(d, q, True)
                    slot = jnp.where(~right & (d == z - 1), chips, d)
                    self.along(d, slot, q, jnp.where(right, z + 1, z - 1)).start()

    def own_sum(self):
        chips, z, c = self.line.chips, self.line.z, self.line.c
        total, rx = self.total, self.rx
        self.to_sibling(z).wait_recv()
        for q in range(PARTS):

            @pl.when(z > 0)
            def _():
                self.wait_line(z, q)

            @pl.when(z < chips - 1)
            def _():
                self.wait_line(chips, q)

        def add_up(at):
            total[at, :] = self.part[self.rows_at(z, c, at.start, at.size), :].astype(F32) + self.sib[z, at, :].astype(F32)

            @pl.when(z > 0)
            def _():
                total[at, :] += rx[z, at, :].astype(F32)

            @pl.when(z < chips - 1)
            def _():
                total[at, :] += rx[chips, at, :].astype(F32)

        row_chunks(self.rows, add_up)

    def finish(self):
        z = self.line.z

        @pl.loop(0, self.line.chips)
        def _(d):
            self.to_sibling(d).wait_send()
            for q in range(PARTS):

                @pl.when(d > z)
                def _():
                    self.to_right(d, q).wait_send()

                @pl.when(d < z)
                def _():
                    self.to_left(d, q).wait_send()


class Gather:
    @staticmethod
    def scratch(n):
        return [DMA((3, n)), DMA((n,)), DMA(())]

    def __init__(self, line, own, buf, scratch):
        self.line, self.own, self.buf = line, own, buf
        self.send, self.recv, self.local_sem = scratch

    def copy(self, way, slot, mine=False):
        line, z, c = self.line, self.line.z, self.line.c
        src = self.own if mine else self.buf.at[slot]
        device = (line.dev(z, 1 - c), line.dev(z + 1, c), line.dev(z - 1, c))[way]
        return remote(src, self.buf.at[slot], self.send.at[way, slot], self.recv.at[slot], device)

    def local(self):
        return pltpu.make_async_copy(self.own, self.buf.at[self.line.me], self.local_sem)

    def along(self, at, mine=False):
        z, slot = self.line.z, 2 * at + self.line.c

        @pl.when((z < self.line.chips - 1) & (at <= z))
        def _():
            self.copy(1, slot, mine).start()

        @pl.when((z > 0) & (at >= z))
        def _():
            self.copy(2, slot, mine).start()

    def pass_on(self, at, mine=False):
        self.along(at, mine)
        self.copy(0, 2 * at + self.line.c, mine).start()

    def start(self, ends_later=False):
        line = self.line
        if ends_later:

            @pl.when((line.z > 0) & (line.z < line.chips - 1))
            def _():
                self.along(line.z, True)

            self.copy(0, line.me, True).start()
        else:
            self.pass_on(line.z, True)
        self.local().start()

    def start_ends(self):
        self.along(self.line.z, True)

    def arrive(self, t, sides=(True, False)):
        z, chips = self.line.z, self.line.chips
        for far in sides:
            at = jnp.where((2 * z < chips) == far, z + t, z - t)
            there = (at >= 0) & (at < chips)

            @pl.when(there)
            def _():
                self.copy(0, 2 * at + self.line.c).wait_recv()
                self.pass_on(at)

    def ready(self, j):
        at = self.line.near_first(j)
        if isinstance(j, int):
            if j == 0:
                self.local().wait()
        else:

            @pl.when(j == 0)
            def _():
                self.local().wait()

        self.copy(0, 2 * at + 1 - self.line.c).wait_recv()
        return at

    def finish(self):
        z = self.line.z

        @pl.loop(0, self.line.chips)
        def _(at):
            slot = 2 * at + self.line.c
            self.copy(0, slot).wait_send()

            @pl.when((z < self.line.chips - 1) & (at <= z))
            def _():
                self.copy(1, slot).wait_send()

            @pl.when((z > 0) & (at >= z))
            def _():
                self.copy(2, slot).wait_send()


def load(src, dst, sem):
    copy = pltpu.make_async_copy(src, dst, sem)
    copy.start()
    copy.wait()


def rows_of(z, rows):
    return pl.ds(pl.multiple_of(z * 2 * rows, 2 * rows), 2 * rows)


class Square:
    @staticmethod
    def scratch(units, tiles):
        return [DMA((units, 2, tiles)), DMA((units, 2, tiles)), DMA((units,)), DMA((units,)), DMA(())]

    def __init__(self, line, units, scratch):
        self.line, self.units = line, units
        self.send1, self.recv1, self.send2, self.recv2, self.sem = scratch
        self.tiles = self.send1.shape[2]

    def ways(self, u):
        line = self.line
        return (line.xn, line.yn) if self.units[u]["x_first"] else (line.yn, line.xn)

    def whole(self, u, block):
        unit = self.units[u]
        return unit["parts"].at[block, pl.ds(unit["row"], unit["rows"])]

    def first(self, u, slot, t):
        unit = self.units[u]
        one, _ = self.ways(u)
        block = one if slot == 0 else self.line.diag
        src, dst = self.whole(u, block), unit["land1"].at[slot]
        if self.tiles > 1:
            axis = unit["axis"]
            step = dst.shape[axis] // self.tiles
            at = (pl.ds(t * step, step),) if axis == 0 else (slice(None), pl.ds(t * step, step))
            src, dst = src.at[at], dst.at[at]
        return remote(src, dst, self.send1.at[u, slot, t], self.recv1.at[u, slot, t], (one, self.line.me))

    def start(self, u, t=0):
        for slot in range(2):
            self.first(u, slot, t).start()

    def add(self, u, slot, block, also=None):
        unit = self.units[u]
        for t in range(self.tiles):
            self.first(u, slot, t).wait_recv()
        land, tmp = unit["land1"], unit["tmp"].at[pl.ds(0, unit["rows"])]
        load(self.whole(u, block), tmp, self.sem)

        def one(at):
            value = land[slot, at, :].astype(F32) + tmp[at, :].astype(F32)
            if also is not None:
                value = value + also[at, :].astype(F32)
            land[slot, at, :] = value.astype(BF16)

        row_chunks(unit["rows"], one)

    def second(self, u):
        unit = self.units[u]
        _, two = self.ways(u)
        return remote(unit["land1"].at[1], unit["land2"], self.send2.at[u], self.recv2.at[u], (two, self.line.me))

    def fold(self, u):
        self.add(u, 1, self.ways(u)[1])
        self.second(u).start()

    def result(self, u):
        self.second(u).wait_recv()
        self.add(u, 0, self.line.replica, self.units[u]["land2"])

    def finish(self):
        for u in range(len(self.units)):
            self.second(u).wait_send()
            for slot in range(2):
                for t in range(self.tiles):
                    self.first(u, slot, t).wait_send()


def key_range(block, long_len):
    longs = long_len // QBLK
    return (0, block + 1, False) if block < longs else (longs, block + 1 - longs, True)


def score_mask(q_block, k_block, seg_row, seg_col, heads, compare):
    visible = None
    shape = (QBLK, QBLK)
    if q_block == k_block:
        visible = lax.broadcasted_iota(jnp.int32, shape, 0) <= lax.broadcasted_iota(jnp.int32, shape, 1)
    if compare:
        k_at, q_at = k_block * QBLK, q_block * QBLK
        same = seg_col[k_at : k_at + QBLK, :] == seg_row[:, q_at : q_at + QBLK]
        visible = same if visible is None else visible & same
    if visible is None:
        return None
    bias = jnp.where(visible, 0.0, MASKED)
    return jnp.concatenate([bias] * heads, 1)


def one_hot_rows(rank_row, start):
    group = rank_row.shape[1]
    places = start + lax.broadcasted_iota(jnp.int32, (QBLK, group), 0)
    return jnp.where(rank_row[...] == places, 1.0, 0.0).astype(BF16)


def one_hot_back(rank_col, start):
    group = rank_col.shape[0]
    places = lax.broadcasted_iota(jnp.int32, (QBLK, group), 1)
    return jnp.where(rank_col[pl.ds(start, QBLK), :] == places, 1.0, 0.0).astype(BF16)


def attention_kernel(heads, long_len, qkv, rank_row, rank_col, seg_row, seg_col, q_out, kv_out, lse, att_t, att, s_buf, v_t):
    group = qkv.shape[0]
    q_cols = heads * HD
    n_blocks = group // QBLK
    for b in range(n_blocks):
        ordered = dot(one_hot_rows(rank_row, b * QBLK), qkv[...])
        for h in range(heads):
            q_out[b, h * QBLK : (h + 1) * QBLK, :] = (ordered[:, h * HD : (h + 1) * HD] * 0.125).astype(BF16)
        kv_out[0, b * QBLK : (b + 1) * QBLK, :] = ordered[:, q_cols : q_cols + HD].astype(BF16)
        values = ordered[:, q_cols + HD :]
        kv_out[1, b * QBLK : (b + 1) * QBLK, :] = values.astype(BF16)
        v_t[:, b * QBLK : (b + 1) * QBLK] = values.T.astype(BF16)
    for b in range(n_blocks):
        first, count, compare = key_range(b, long_len)
        queries = q_out[b]
        top = None
        for i in range(count):
            k_at = (first + i) * QBLK
            scores = dot_t(kv_out[0, k_at : k_at + QBLK, :], queries)
            bias = score_mask(b, first + i, seg_row, seg_col, heads, compare)
            if bias is not None:
                scores = scores + bias
            s_buf[i] = scores
            high = jnp.max(scores, 0, keepdims=True)
            top = high if top is None else jnp.maximum(top, high)
        total, out = 0.0, 0.0
        for i in range(count):
            k_at = (first + i) * QBLK
            terms = jnp.exp(s_buf[i] - top)
            total = total + jnp.sum(terms, 0, keepdims=True)
            out = out + dot(v_t[:, k_at : k_at + QBLK], terms.astype(BF16))
        lse[b] = top + jnp.log(total)
        out = out / total
        for h in range(heads):
            att_t[h * HD : (h + 1) * HD, b * QBLK : (b + 1) * QBLK] = out[:, h * QBLK : (h + 1) * QBLK]
    low = att_t[...].astype(BF16)

    @pl.loop(0, n_blocks)
    def _(b):
        at = pl.multiple_of(b * QBLK, QBLK)
        att[pl.ds(at, QBLK), :] = dot_t(one_hot_back(rank_col, at), low).astype(BF16)


def attention_back_kernel(
    heads, long_len, q_in, kv, lse, att_t, grad_att, rank_row, rank_col, seg_row, seg_col, cos_t, sin_t, out,
    grad_kv, grad_t, k_t, go_rows, go_t, after_block,
):
    group = kv.shape[1]
    n_blocks = group // QBLK
    half = HD // 2
    q_cols = heads * HD
    for b in range(n_blocks):
        at = b * QBLK
        ordered = dot(one_hot_rows(rank_row, at), grad_att[...])
        for h in range(heads):
            go_rows[b, h * QBLK : (h + 1) * QBLK, :] = ordered[:, h * HD : (h + 1) * HD].astype(BF16)
        go_t[:, at : at + QBLK] = ordered.T
        k_t[:, at : at + QBLK] = kv[0, at : at + QBLK, :].astype(F32).T.astype(BF16)
    grad_kv[...] = jnp.zeros_like(grad_kv)
    for b in range(n_blocks):
        first, count, compare = key_range(b, long_len)
        q_at = b * QBLK
        queries, grad_rows = q_in[b], go_rows[b]
        centre = jnp.concatenate(
            [
                jnp.sum(
                    go_t[h * HD : (h + 1) * HD, q_at : q_at + QBLK] * att_t[h * HD : (h + 1) * HD, q_at : q_at + QBLK],
                    0,
                    keepdims=True,
                )
                for h in range(heads)
            ],
            1,
        )
        grad_q = 0.0
        for i in range(count):
            k_at = (first + i) * QBLK
            scores = dot_t(kv[0, k_at : k_at + QBLK, :], queries)
            bias = score_mask(b, first + i, seg_row, seg_col, heads, compare)
            if bias is not None:
                scores = scores + bias
            probs = jnp.exp(scores - lse[b])
            grad_probs = dot_t(kv[1, k_at : k_at + QBLK, :], grad_rows)
            grad_scores = (probs * (grad_probs - centre)).astype(BF16)
            grad_kv[0, k_at : k_at + QBLK, :] += dot(grad_scores, queries)
            grad_kv[1, k_at : k_at + QBLK, :] += dot(probs.astype(BF16), grad_rows)
            grad_q = grad_q + dot(k_t[:, k_at : k_at + QBLK], grad_scores)
        cos_b, sin_b = cos_t[:, q_at : q_at + QBLK], sin_t[:, q_at : q_at + QBLK]

        def turned(value):
            front, back = value[:half], value[half:]
            return jnp.concatenate([front * cos_b + back * sin_b, back * cos_b - front * sin_b], 0).astype(BF16)

        for h in range(heads):
            grad_t[h * HD : (h + 1) * HD, q_at : q_at + QBLK] = turned(grad_q[:, h * QBLK : (h + 1) * QBLK] * 0.125)
        after_block(b)
    for b in range(n_blocks):
        at = b * QBLK
        cos_b, sin_b = cos_t[:, at : at + QBLK], sin_t[:, at : at + QBLK]
        value = grad_kv[0, at : at + QBLK, :].T
        front, back = value[:half], value[half:]
        grad_t[q_cols : q_cols + half, at : at + QBLK] = (front * cos_b + back * sin_b).astype(BF16)
        grad_t[q_cols + half : q_cols + HD, at : at + QBLK] = (back * cos_b - front * sin_b).astype(BF16)
        grad_t[q_cols + HD :, at : at + QBLK] = grad_kv[1, at : at + QBLK, :].T.astype(BF16)

    @pl.loop(0, n_blocks)
    def _(b):
        at = pl.multiple_of(b * QBLK, QBLK)
        out[pl.ds(at, QBLK), :] = dot_t(one_hot_back(rank_col, at), grad_t[...]).astype(BF16)


def order_group(long_len, ids, ids_col, rank_row, rank_col, seg_row_out, seg_col_out, pos_out, key_col, acc):
    group = ids.shape[1]
    seg_row, pos_row = ids.at[0:1, :], ids.at[1:2, :]

    def chunks(fn):
        @pl.loop(0, group // QBLK)
        def _(i):
            fn(pl.multiple_of(i * QBLK, QBLK))

    def ones(mask):
        return jnp.where(mask, 1.0, 0.0)

    acc[...] = jnp.zeros_like(acc)

    def lengths(at):
        here = pl.ds(at, QBLK)
        same = ones(ids_col[here, 0:1] == seg_row[...])
        acc[0:1, :] += jnp.sum(same, 0, keepdims=True)
        first = jnp.sum(same, 1, keepdims=True) == float(long_len)
        key_col[here, :] = jnp.where(first, -1.0, ids_col[here, 0:1]) * float(group) + ids_col[here, 1:2]

    chunks(lengths)
    key_row = jnp.where(acc[0:1, :] == float(long_len), -1.0, seg_row[...]) * float(group)
    acc[1:2, :] = key_row + pos_row[...]

    def ranks(at):
        here = pl.ds(at, QBLK)
        mine, others = key_col[here, :], acc[1:2, :]
        rank_col[here, :] = jnp.sum(ones(others < mine), 1, keepdims=True).astype(jnp.int32)
        acc[2:3, :] += jnp.sum(ones(mine < others), 0, keepdims=True)

    chunks(ranks)
    rank_row[...] = acc[2:3, :].astype(jnp.int32)

    def ordered(at):
        here = pl.ds(at, QBLK)
        places = at + lax.broadcasted_iota(jnp.int32, (QBLK, group), 0)
        seg = jnp.sum(jnp.where(rank_row[...] == places, seg_row[...], 0.0), 1, keepdims=True)
        seg_col_out[here, :] = seg.astype(jnp.int32)
        moved = rank_col[here, :] == lax.broadcasted_iota(jnp.int32, (QBLK, group), 1)
        acc[3:4, :] += jnp.sum(jnp.where(moved, ids_col[here, 0:1], 0.0), 0, keepdims=True)
        acc[4:5, :] += jnp.sum(jnp.where(moved, ids_col[here, 1:2], 0.0), 0, keepdims=True)

    chunks(ordered)
    seg_row_out[...] = acc[3:4, :].astype(jnp.int32)
    pos_out[...] = acc[4:5, :]


def frequencies(index):
    return jnp.exp(-math.log(ROPE_BASE) * index.astype(F32) * (2.0 / HD))


def start_kernel(
    n, reps, spread, heads, long_len, tok, gain_a_in, gain_m_in, seg_in, pos_in, wk, wv_in, wq, wg, wu,
    q_out, kv_out, lse, att_t, att, rank_row, rank_col, seg_row_out, seg_col_out, cos_back, sin_back, gain_a, gain_m,
    normed, w_all, gu_own,
    gains, ids, wkv, gains_buf, own, wv, blk, qkv, cos, sin, ids_col, key_col, acc, pos_out, s_buf, v_t,
    g_send, g_recv, a_send, a_recv, r_send, r_recv, u_send, u_recv, local_sem, load_sem, *ag_scratch,
):
    line = Line(n)
    me, rep = line.me, line.replica
    rows, width = tok.shape
    w_rows = wq.shape[0]
    fb = gu_own.shape[-1]
    own_cols = fb * reps
    gains[...] = jnp.zeros_like(gains)
    gains[0:1, :] = gain_a_in[...].astype(F32)
    gains[1:2, :] = gain_m_in[...].astype(F32)
    ids[...] = jnp.zeros_like(ids)
    ids[0:1, :] = seg_in[...].astype(F32)
    ids[1:2, :] = pos_in[...].astype(F32)
    line.enter_all(reps)

    def gain_copy(i, to, slot):
        return remote(gains, gains_buf.at[slot], g_send.at[i], g_recv.at[slot], (rep, to))

    q_cols = heads * HD
    mine_at = pl.ds(rep * (w_rows // reps), w_rows // reps)

    def qkv_pieces(to, slot):
        return (
            (wq.at[mine_at, pl.ds(pl.multiple_of(to * q_cols, 128), q_cols)], w_all.at[slot, rep, :, pl.ds(0, q_cols)]),
            (wkv.at[to, mine_at], w_all.at[slot, rep, :, pl.ds(q_cols, 2 * HD)]),
        )

    def qkv_copy(k, i, to, slot):
        src, dst = qkv_pieces(to, slot)[k]
        return remote(src, dst, a_send.at[k, i], a_recv.at[k, slot], (rep, to))

    def gu_copy(k, to, slot):
        piece = (wg, wu)[k].at[:, pl.ds(pl.multiple_of(to * own_cols + rep * fb, 128), fb)]
        at = pl.ds(pl.multiple_of(slot * w_rows, 16), w_rows)
        return remote(piece, gu_own.at[k, at], u_send.at[k, to], u_recv.at[k, slot], (rep, to))

    def spread_weights(stage):
        if not spread:
            return
        if stage == 0:
            for k in range(2):
                gu_copy(k, 2 * line.z + 1 - line.c, me).start()
            return
        last = line.chips - 1

        @pl.loop(1, line.chips)
        def _(d):
            for to in (line.z + d, line.z - d):
                to_end = (to == 0) | (to == last)
                next_to_end = ((line.z == 0) | (line.z == last)) & (d == 1)
                now = (to_end, (~to_end) & next_to_end, (~to_end) & (~next_to_end))[stage % 3]

                @pl.when((to >= 0) & (to <= last) & now)
                def _():
                    for core in range(2):
                        for k in range(2):
                            gu_copy(k, 2 * to + core, me).start()

    for i in range(1, n):
        gain_copy(i, line.other(i), me).start()
    for i in range(1, n):
        qkv_copy(0, i, line.other(i), me).start()
    for i in range(n):
        at = i * KVH // n * HD
        wkv[i] = jnp.concatenate([wk[:, at : at + HD], wv_in[:, at : at + HD]], 1)
    for i in range(1, n):
        qkv_copy(1, i, line.other(i), me).start()
    own_pieces = qkv_pieces(me, me)
    mine = [
        pltpu.make_async_copy(*own_pieces[0], local_sem.at[0]),
        pltpu.make_async_copy(*own_pieces[1], local_sem.at[3]),
    ]
    if spread:
        for k in range(2):
            piece = (wg, wu)[k].at[:, pl.ds(pl.multiple_of(me * own_cols + rep * fb, 128), fb)]
            at = pl.ds(pl.multiple_of(me * w_rows, 16), w_rows)
            mine.append(pltpu.make_async_copy(piece, gu_own.at[k, at], local_sem.at[1 + k]))
    for copy in mine:
        copy.start()
    gains_buf[me] = gains[...]
    for i in range(1, n):
        gain_copy(i, me, line.other(i)).wait_recv()
    gain_a[...] = jnp.concatenate([gains_buf[i, 0:1, :] for i in range(n)], 1)
    gain_m[...] = jnp.concatenate([gains_buf[i, 1:2, :] for i in range(n)], 1)

    def norm(at):
        resid = tok[at, :].astype(F32)
        inverse = lax.rsqrt(jnp.mean(resid * resid, -1, keepdims=True) + EPSILON)
        own[at, :] = (resid * inverse * gain_a[...]).astype(BF16)

    row_chunks(rows, norm)
    gather = Gather(line, own, normed, ag_scratch)
    gather.start()
    spread_weights(0)
    for at in range(0, ids.shape[1], QBLK):
        ids_col[at : at + QBLK, :] = ids[:, at : at + QBLK].T
    order_group(long_len, ids, ids_col, rank_row, rank_col, seg_row_out, seg_col_out, pos_out, key_col, acc)
    for i in range(1, n):
        for k in range(2):
            qkv_copy(k, i, me, line.other(i)).wait_recv()
    for copy in mine[:2]:
        copy.wait()

    def share(i, to, slot):
        return remote(w_all.at[:, slot], w_all.at[:, slot], r_send.at[i], r_recv.at[slot], (to, me))

    for i in range(1, reps):
        share(i, lax.rem(rep + i, reps), rep).start()
    lanes = lax.broadcasted_iota(jnp.int32, (1, 128), 1)
    freq = frequencies(lax.rem(lanes, HD // 2))
    sign = jnp.where(lax.rem(lanes, HD) < HD // 2, -1.0, 1.0)

    def table(at):
        angles = ids_col[at, 1:2] * freq
        cos[at, :] = jnp.cos(angles)
        sin[at, :] = jnp.sin(angles) * sign

    row_chunks(ids_col.shape[0], table)
    gather.arrive(1)
    spread_weights(1)
    angles = frequencies(lax.broadcasted_iota(jnp.int32, (HD // 2, 1), 0)) * pos_out[...]
    cos_back[...] = jnp.cos(angles)
    sin_back[...] = jnp.sin(angles)
    for i in range(1, reps):
        share(i, rep, lax.rem(rep + i, reps)).wait_recv()
    load(w_all, wv, load_sem)
    cols = wv.shape[-1]
    lane = lax.broadcasted_iota(jnp.int32, (2 * rows, 128), 1)
    front = lax.rem(lane, HD) < HD // 2

    def project(j):
        z = gather.ready(j)
        load(normed.at[pl.ds(2 * z, 2)], blk, load_sem)
        at = rows_of(z, rows)
        raw = dot(blk[...].reshape(2 * rows, width), wv[...].reshape(width, cols))
        for t in range(0, cols, 128):
            part = raw[:, t : t + 128]
            cos_t, sin_t = cos[at, :], sin[at, :]
            if t == cols - 128:
                cos_t, sin_t = jnp.where(lane < HD, cos_t, 1.0), jnp.where(lane < HD, sin_t, 0.0)
            partner = jnp.where(front, pltpu.roll(part, 128 - HD // 2, 1), pltpu.roll(part, HD // 2, 1))
            qkv[at, t : t + 128] = (part * cos_t + partner * sin_t).astype(BF16)

    project(0)
    gather.arrive(2)
    spread_weights(2)

    is_end = (line.z == 0) | (line.z == line.chips - 1)

    @pl.loop(1, line.chips)
    def _(j):
        @pl.when(j + 2 < line.chips)
        def _():
            gather.arrive(j + 2)

        @pl.when(is_end & (j == max(1, line.chips - 3)))
        def _():
            spread_weights(3)

        project(j)

    @pl.when(~is_end)
    def _():
        spread_weights(3)

    attention_kernel(
        heads, long_len, qkv, rank_row, rank_col, seg_row_out, seg_col_out, q_out, kv_out, lse, att_t, att, s_buf, v_t
    )
    for i in range(1, n):
        gain_copy(i, line.other(i), me).wait_send()
        for k in range(2):
            qkv_copy(k, i, line.other(i), me).wait_send()
    for i in range(1, reps):
        share(i, lax.rem(rep + i, reps), rep).wait_send()
    if spread:
        for k in range(2):
            mine[2 + k].wait()
            for i in range(1, n):
                gu_copy(k, line.other(i), me).wait_send()
                gu_copy(k, me, line.other(i)).wait_recv()
    gather.finish()


def start_layer(n, reps, spread, heads, long_len, tok, gain_a, gain_m, seg, pos, wk, wv, wq, wg, wu):
    rows, width = tok.shape
    w_rows = wq.shape[0]
    cols = heads * HD + 2 * HD
    group = seg.shape[0]
    n_blocks = group // QBLK
    fb = wg.shape[1] // n // reps
    return pl.pallas_call(
        functools.partial(start_kernel, n, reps, spread, heads, long_len),
        name="start_layer",
        out_shape=(
            jax.ShapeDtypeStruct((n_blocks, heads * QBLK, HD), BF16),
            jax.ShapeDtypeStruct((2, group, HD), BF16),
            jax.ShapeDtypeStruct((n_blocks, 1, heads * QBLK), F32),
            jax.ShapeDtypeStruct((heads * HD, group), F32),
            jax.ShapeDtypeStruct((group, heads * HD), BF16),
            jax.ShapeDtypeStruct((1, group), jnp.int32),
            jax.ShapeDtypeStruct((group, 1), jnp.int32),
            jax.ShapeDtypeStruct((1, group), jnp.int32),
            jax.ShapeDtypeStruct((group, 1), jnp.int32),
            jax.ShapeDtypeStruct((HD // 2, group), F32),
            jax.ShapeDtypeStruct((HD // 2, group), F32),
            jax.ShapeDtypeStruct((1, width), F32),
            jax.ShapeDtypeStruct((1, width), F32),
            jax.ShapeDtypeStruct((n, rows, width), BF16),
            jax.ShapeDtypeStruct((n, reps, w_rows // reps, cols), BF16),
            jax.ShapeDtypeStruct((2, width, fb), BF16),
        ),
        in_specs=[VMEM] * 7 + [ANY] * 3,
        out_specs=(VMEM,) * 13 + (ANY,) * 3,
        scratch_shapes=[
            pltpu.VMEM((8, w_rows), F32),
            pltpu.VMEM((8, group), F32),
            pltpu.VMEM((n, w_rows, 2 * HD), BF16),
            pltpu.VMEM((n, 8, w_rows), F32),
            pltpu.VMEM((rows, width), BF16),
            pltpu.VMEM((n, reps, w_rows // reps, cols), BF16),
            pltpu.VMEM((2, rows, width), BF16),
            pltpu.VMEM((group, cols), BF16),
            pltpu.VMEM((group, 128), F32),
            pltpu.VMEM((group, 128), F32),
            pltpu.VMEM((group, 8), F32),
            pltpu.VMEM((group, 1), F32),
            pltpu.VMEM((8, group), F32),
            pltpu.VMEM((1, group), F32),
            pltpu.VMEM((long_len // QBLK, QBLK, heads * QBLK), F32),
            pltpu.VMEM((HD, group), BF16),
            DMA((n,)),
            DMA((n,)),
            DMA((2, n)),
            DMA((2, n)),
            DMA((reps,)),
            DMA((reps,)),
            DMA((2, n)),
            DMA((2, n)),
            DMA((4,)),
            DMA(()),
        ]
        + Gather.scratch(n),
        compiler_params=pltpu.CompilerParams(collective_id=4, has_side_effects=True, vmem_limit_bytes=VMEM_BYTES),
        cost_estimate=pl.CostEstimate(flops=2 * group * width * cols, bytes_accessed=300 * 2**20, transcendentals=0),
    )(tok, gain_a[None], gain_m[None], seg[None], pos[None], wk, wv, wq, wg, wu)


def weight_copies(gu, wbuf, w_sem):
    blocks, _, _, fb = gu.shape
    own = blocks * fb

    def copy(b, k):
        at = k * own + b * fb
        if not isinstance(at, int):
            at = pl.multiple_of(at, 128)
        return pltpu.make_async_copy(gu.at[b, k], wbuf.at[:, pl.ds(at, fb)], w_sem.at[k, b])

    return copy


def mlp_kernel(
    n, blocks, spread, att, wo, tok, gain, gu_in, cot, wd, normed, middle, hidden, grads, gu_out, cot_all, *scratch
):
    scatter_scratch, scratch = scratch[:8], scratch[8:]
    ag_scratch, cot_scratch, scratch = scratch[:3], scratch[3:6], scratch[6:]
    own_normed, blk, wbuf, wd_buf, grad_hid, hid_stage, grad_stage, w_sem, out_sem, load_sem, x_send, x_recv = scratch
    line = Line(n)
    rows, width = tok.shape
    fb = gu_in.shape[-1]
    own = blocks * fb
    rep = line.replica
    scatter = Scatter(line, scatter_scratch)
    cots = Gather(line, cot, cot_all, cot_scratch)
    gather = Gather(line, own_normed, normed, ag_scratch)
    wd_copy = pltpu.make_async_copy(wd, wd_buf, load_sem.at[1])
    wd_copy.start()
    line.enter(spread)
    cots.start(True)
    if spread:
        gu = gu_out

        def gu_copy(way, k, src, slot, device):
            return remote(src, gu.at[slot, k], x_send.at[way, k], x_recv.at[way, k], (device, line.me))

        firsts = [(0, 0, line.xn), (1, 1, line.yn), (0, 1, line.xn), (1, 0, line.yn)]
        for way, k, device in firsts[:2]:
            gu_copy(way, k, gu_in.at[k], rep, device).start()
        for k in range(2):
            pltpu.make_async_copy(gu_in.at[k], wbuf.at[:, pl.ds(pl.multiple_of(k * own + rep * fb, 128), fb)], w_sem.at[k, rep]).start()
            pltpu.make_async_copy(gu_in.at[k], gu.at[rep, k], load_sem.at[2 + k]).start()
    else:
        gu = gu_in
    weight_copy = weight_copies(gu, wbuf, w_sem)
    if not spread:
        for b in range(blocks):
            for k in range(2):
                weight_copy(b, k).start()

    def out_part(d):
        x = att[rows_of(d, rows), :]
        for t in range(0, width, 512):
            part = dot(x, wo[:, t : t + 512]).astype(BF16)
            scatter.part[rows_of(d, rows), t : t + 512] = part

    scatter.produce(out_part, cots.start_ends)
    wd_copy.wait()

    def grad_hidden(j):
        z = cots.ready(j)
        load(cot_all.at[pl.ds(2 * z, 2)], blk, load_sem.at[0])
        x = blk[...].reshape(2 * rows, width)
        tile = min(256, own)
        for t in range(0, own, tile):
            grad_hid[rows_of(z, rows), t : t + tile] = dot_t(x, wd_buf[t : t + tile, :]).astype(BF16)

    cots.arrive(1, (True,))
    if spread:
        for way, k, device in firsts[2:]:
            gu_copy(way, k, gu_in.at[k], rep, device).start()
    scatter.duty(0)
    cots.arrive(1, (False,))
    grad_hidden(0)
    if spread:
        for way, k, slot, device in ((0, 0, line.xn, line.yn), (1, 1, line.yn, line.xn)):
            gu_copy(way, k, gu.at[slot, k], slot, device).wait_recv()
            gu_copy(2 + way, k, gu.at[slot, k], slot, device).start()
            weight_copy(slot, k).start()

    @pl.loop(1, line.chips - 2)
    def _(s):
        scatter.duty(s)
        cots.arrive(s + 1)
        grad_hidden(s)

    scatter.duty(line.chips - 2)
    scatter.own_sum()

    def norm(at):
        mid = tok[at, :].astype(F32) + scatter.total[at, :]
        middle[at, :] = mid
        inverse = lax.rsqrt(jnp.mean(mid * mid, -1, keepdims=True) + EPSILON)
        own_normed[at, :] = (mid * inverse * gain[...]).astype(BF16)

    row_chunks(rows, norm)
    gather.start()
    cots.arrive(line.chips - 1)
    grad_hidden(line.chips - 2)
    grad_hidden(line.chips - 1)
    if spread:
        for way, k, slot in ((0, 1, line.xn), (1, 0, line.yn)):
            gu_copy(way, k, gu.at[slot, k], slot, line.xn).wait_recv()
            weight_copy(slot, k).start()
        for way, k, device in ((2, 0, line.yn), (3, 1, line.xn)):
            gu_copy(way, k, gu.at[line.diag, k], line.diag, device).wait_recv()
            weight_copy(line.diag, k).start()
    for b in range(blocks):
        for k in range(2):
            weight_copy(b, k).wait()

    def out_copies(z):
        at = rows_of(z, rows)
        return (
            pltpu.make_async_copy(hid_stage, hidden.at[at], out_sem.at[0]),
            pltpu.make_async_copy(grad_stage, grads.at[at], out_sem.at[1]),
        )

    @pl.loop(0, line.chips)
    def _(j):
        @pl.when(j > 0)
        def _():
            gather.arrive(j)

        z = gather.ready(j)
        load(normed.at[pl.ds(2 * z, 2)], blk, load_sem.at[0])

        @pl.when(j > 0)
        def _():
            for copy in out_copies(line.near_first(j - 1)):
                copy.wait()

        at = rows_of(z, rows)
        x = blk[...].reshape(2 * rows, width)
        tile = min(256, own)
        for t in range(0, own, tile):
            gate = dot(x, wbuf[:, t : t + tile])
            up = dot(x, wbuf[:, own + t : own + t + tile])
            sig = 1.0 / (1.0 + jnp.exp(-gate))
            gated = gate * sig
            gh = grad_hid[at, t : t + tile].astype(F32)
            hid_stage[:, t : t + tile] = (gated * up).astype(BF16)
            grad_stage[:, t : t + tile] = (gh * up * sig * (1.0 + gate * (1.0 - sig))).astype(BF16)
            grad_stage[:, own + t : own + t + tile] = (gh * gated).astype(BF16)
        for copy in out_copies(z):
            copy.start()

    for copy in out_copies(line.near_first(line.chips - 1)):
        copy.wait()
    if spread:
        for k in range(2):
            pltpu.make_async_copy(gu_in.at[k], gu.at[rep, k], load_sem.at[2 + k]).wait()
        for way, k, device in firsts:
            gu_copy(way, k, gu_in.at[k], rep, device).wait_send()
        for way, k, slot, device in ((2, 0, line.xn, line.yn), (3, 1, line.yn, line.xn)):
            gu_copy(way, k, gu.at[slot, k], slot, device).wait_send()
    scatter.finish()
    cots.finish()
    gather.finish()


def mlp_forward(n, reps, spread, att, wo, tok, gain, gu, cot, wd):
    rows, width = tok.shape
    group = att.shape[0]
    fb = gu.shape[-1]
    blocks = reps if spread else gu.shape[0]
    own = blocks * fb
    kept = (blocks, 2, width, fb) if spread else (1, 16, 128)
    return pl.pallas_call(
        functools.partial(mlp_kernel, n, blocks, spread),
        name="mlp_forward",
        out_shape=(
            jax.ShapeDtypeStruct((n, rows, width), BF16),
            jax.ShapeDtypeStruct((rows, width), F32),
            jax.ShapeDtypeStruct((group, own), BF16),
            jax.ShapeDtypeStruct((group, 2 * own), BF16),
            jax.ShapeDtypeStruct(kept, BF16),
            jax.ShapeDtypeStruct((n, rows, width), BF16),
        ),
        in_specs=[VMEM, VMEM, VMEM, VMEM, ANY, VMEM, ANY],
        out_specs=(ANY, VMEM, ANY, ANY, ANY, ANY),
        scratch_shapes=Scatter.scratch(n, rows, width)
        + Gather.scratch(n)
        + Gather.scratch(n)
        + [
            pltpu.VMEM((rows, width), BF16),
            pltpu.VMEM((2, rows, width), BF16),
            pltpu.VMEM((width, 2 * own), BF16),
            pltpu.VMEM((own, width), BF16),
            pltpu.VMEM((group, own), BF16),
            pltpu.VMEM((2 * rows, own), BF16),
            pltpu.VMEM((2 * rows, 2 * own), BF16),
            DMA((2, blocks)),
            DMA((2,)),
            DMA((4,)),
            DMA((4, 2)),
            DMA((4, 2)),
        ],
        compiler_params=pltpu.CompilerParams(collective_id=1, has_side_effects=True, vmem_limit_bytes=VMEM_BYTES),
        cost_estimate=pl.CostEstimate(flops=2 * group * width * own * 3, bytes_accessed=400 * 2**20, transcendentals=0),
    )(att, wo, tok, gain, gu, cot, wd)


def norm_back(grad_normed, resid, gain):
    inverse = lax.rsqrt(jnp.mean(resid * resid, -1, keepdims=True) + EPSILON)
    unit = resid * inverse
    scaled = grad_normed * gain
    return inverse * (scaled - unit * jnp.mean(scaled * unit, -1, keepdims=True)), grad_normed * unit


def middle_kernel(
    n, blocks, spread, grads_in, gu, mid_in, cot_in, gain, wo_in, normed, hidden, cot_all, wd,
    grad_mid, gml, grad_att, gain_sum, output,
    gate_parts, up_parts, down_parts, gate_q, up_q, down_q, down_out, *scratch,
):
    scatter_scratch, ag_scratch, scratch = scratch[:8], scratch[8:11], scratch[11:]
    mid, cot, wo, late_sem, *scratch = scratch
    late = [pltpu.make_async_copy(src, dst, late_sem.at[i]) for i, (src, dst) in enumerate(zip((mid_in, cot_in, wo_in), (mid, cot, wo)))]
    grads, own_low, blk, wbuf, w_sem, load_sem = scratch[:6]
    line = Line(n)
    rows, width = mid.shape
    group = grads.shape[0]
    fb = gu.shape[-1]
    own = blocks * fb
    scatter = Scatter(line, scatter_scratch)
    gather = Gather(line, own_low, gml, ag_scratch)
    grads_copy = pltpu.make_async_copy(grads_in, grads, load_sem)
    weight_copy = weight_copies(gu, wbuf, w_sem)

    def start_loads():
        grads_copy.start()
        for b in range(blocks):
            for k in range(2):
                weight_copy(b, k).start()
        for copy in late:
            copy.start()

    if not spread:
        start_loads()
    if not spread:
        line.enter(spread)

    def loaded():
        grads_copy.wait()
        for b in range(blocks):
            for k in range(2):
                weight_copy(b, k).wait()

    def normed_part(d):
        x = grads[rows_of(d, rows), :]
        for t in range(0, width, 512):
            part = dot_t(x, wbuf[t : t + 512, :]).astype(BF16)
            scatter.part[rows_of(d, rows), t : t + 512] = part

    if not spread:
        loaded()
        scatter.produce(normed_part)
    tiles = 4
    tile = width // tiles
    if spread:
        gate_land, up_land, down_land, gate_in, up_in, down_in, tmp, tmp_down, stage, part_sem, out_sem, hid_buf, tile_sem = scratch[6:19]
        half = fb // 2
        units = [
            dict(parts=gate_parts, row=0, rows=width, x_first=True, axis=0, land1=gate_land, land2=gate_in, tmp=tmp),
            dict(parts=up_parts, row=0, rows=width, x_first=False, axis=0, land1=up_land, land2=up_in, tmp=tmp),
        ]
        for i in range(2):
            units.append(
                dict(
                    parts=down_parts, row=i * half, rows=half, x_first=i == 0, axis=1,
                    land1=down_land.at[i], land2=down_in.at[i], tmp=tmp_down,
                )
            )
        square = Square(line, units, scratch[19:24])
        d_send, d_recv = scratch[24:26]
        rx, *sems = scratch[26:]
        output_sum = Scatter(line, (grads, scatter.sib, rx, scatter.total, *sems))
        slots = [hid_buf.at[:, pl.ds(own + i * tile, tile)] for i in range(2)]
        hid = hid_buf.at[:, pl.ds(0, own)]

        def column_copy(i):
            src = cot_all if i < tiles else normed
            return pltpu.make_async_copy(src.at[:, pl.ds(i % tiles * tile, tile)], slots[i % 2], tile_sem.at[i % 2])

        hid_copy = pltpu.make_async_copy(hidden, hid, tile_sem.at[2])
        hid_copy.start()
        column_copy(0).start()
        start_loads()
        line.enter(spread)

        def weight_tile(i):
            t = i % tiles
            column_copy(i).wait()
            if i + 1 < 2 * tiles:
                column_copy(i + 1).start()
            if i >= tiles:
                x = slots[i % 2][...]
                for k in range(2):
                    for b in range(blocks):
                        at = k * own + b * fb
                        stage[k, b] = tdot(x, grads[:, at : at + fb]).astype(BF16)
                copies = [
                    pltpu.make_async_copy(stage.at[k, b], parts.at[b, pl.ds(t * tile, tile)], part_sem.at[k, b])
                    for k, parts in enumerate((gate_parts, up_parts))
                    for b in range(blocks)
                ]
            else:
                if i == 0:
                    hid_copy.wait()
                x = slots[i % 2][...]
                for b in range(blocks):
                    part = tdot(hid[:, b * fb : (b + 1) * fb], x).astype(BF16)
                    for k in range(2):
                        stage[k, b, :fb, :] = part[:, k * fb : (k + 1) * fb]
                copies = [
                    pltpu.make_async_copy(
                        stage.at[k, b, pl.ds(0, fb)], down_parts.at[b, :, pl.ds(t * tile + k * fb, fb)], part_sem.at[k, b]
                    )
                    for k in range(2)
                    for b in range(blocks)
                ]
            for copy in copies:
                copy.start()
            for copy in copies:
                copy.wait()

        quarter = half // 2
        pieces = ((2, 0, quarter), (2, quarter, quarter), (3, 0, quarter // 2), (3, quarter // 2, quarter // 2))

        def place(i, replica):
            unit, row, count = pieces[i]
            at = replica * 3 * quarter + (unit - 2) * half + row
            return down_out.at[pl.ds(pl.multiple_of(at, 16), count)]

        def down_piece(i):
            unit, row, count = pieces[i]
            return units[unit]["land1"].at[0, pl.ds(row, count)]

        def down_send(way, i, src, replica, device):
            return remote(src, place(i, replica), d_send.at[way, i], d_recv.at[way, i], (device, line.me))

        def down_firsts(i):
            return [
                down_send(way, i, down_piece(i), line.replica, device) for way, device in enumerate((line.xn, line.yn))
            ]

        def down_second(i):
            replica, device = ((line.xn, line.yn), (line.yn, line.xn))[i % 2]
            return down_send(2 + i % 2, i, place(i, replica), replica, device)

        def down_local(i):
            return pltpu.make_async_copy(down_piece(i), place(i, line.replica), out_sem.at[3 + i])

        rest_copy = pltpu.make_async_copy(units[3]["land1"].at[0, pl.ds(quarter, quarter)], down_q, out_sem.at[2])

        def down_tile(i):
            if i < tiles:
                weight_tile(i)
                square.start(2, i)
                square.start(3, i)

        down_tile(0)
        loaded()
        scatter.produce(normed_part, None, lambda s: down_tile(s + 1))
        for i in range(line.chips + 1, tiles):
            down_tile(i)
        scatter.duty(0, (True,))
        for i in range(2):
            weight_tile(tiles + i)
            square.start(0, i)
            square.start(1, i)
        scatter.duty(0, (False,))
        square.fold(2)
        square.fold(3)
        scatter.duty(1)
        for i in range(2, 4):
            weight_tile(tiles + i)
            square.start(0, i)
            square.start(1, i)
        scatter.duty(2)
    else:
        for s in range(line.chips - 1):
            scatter.duty(s)
    scatter.own_sum()
    for copy in late:
        copy.wait()
    gain_sum[...] = jnp.zeros_like(gain_sum)

    def back(at):
        through, gain_term = norm_back(scatter.total[at, :], mid[at, :], gain[...])
        value = cot[at, :].astype(F32) + through
        grad_mid[at, :] = value
        own_low[at, :] = value.astype(BF16)
        gain_sum[...] += jnp.sum(gain_term, 0, keepdims=True)

    row_chunks(rows, back)
    gather.start()

    def attended_part(j, z=None):
        if z is None:
            z = gather.ready(j)
        load(gml.at[pl.ds(2 * z, 2)], blk, load_sem)
        grad_att[rows_of(z, rows), :] = dot_t(blk[...].reshape(2 * rows, width), wo[...]).astype(BF16)

    if spread:

        def down_copy(i):
            place = wbuf.at[pl.ds(0, own), pl.ds(i % 2 * tile, tile)]
            return pltpu.make_async_copy(wd.at[:, pl.ds(i * tile, tile)], place, w_sem.at[0, i % 2])

        down_copy(0).start()
        for i in range(tiles):
            down_copy(i).wait()
            if i + 1 < tiles:
                down_copy(i + 1).start()
            for d in range(line.chips):
                at = pl.ds(d * 2 * rows, 2 * rows)
                x = dot(hid[at, :], wbuf[:own, i % 2 * tile : (i % 2 + 1) * tile])
                grads[at, i * tile : (i + 1) * tile] = x.astype(BF16)
        here = gather.ready(0)
        output_sum.produce(lambda d: None)
        gather.arrive(1)
        attended_part(0, here)
        for u in (2, 3):
            square.result(u)
            for i in range(2 * u - 4, 2 * u - 2):
                for copy in down_firsts(i):
                    copy.start()
                down_local(i).start()
        rest_copy.start()
        square.fold(0)
        square.fold(1)
        gather.arrive(2)
        attended_part(1)
        output_sum.duty(0)
        gather.arrive(3)
        attended_part(2)
        attended_part(3)
        for i in range(4):
            replica = (line.xn, line.yn)[i % 2]
            down_send(i % 2, i, place(i, replica), replica, replica).wait_recv()
            down_second(i).start()
        output_sum.duty(1)
        output_sum.duty(2)
        copies = []
        for u, out in ((0, gate_q), (1, up_q)):
            square.result(u)
            copies.append(pltpu.make_async_copy(units[u]["land1"].at[0], out, out_sem.at[u]))
            copies[-1].start()
        output_sum.own_sum()

        def put(at):
            output[at, :] = (mid[at, :] + scatter.total[at, :]).astype(BF16)

        row_chunks(rows, put)
        output_sum.finish()
        rest_copy.wait()
        for i in range(4):
            for copy in down_firsts(i):
                copy.wait_send()
            down_second(i).wait_send()
            down_local(i).wait()
            replica, far = ((line.xn, line.yn), (line.yn, line.xn))[i % 2]
            down_send(2 + i % 2, i, place(i, line.diag), line.diag, replica).wait_recv()
            down_send(1 - i % 2, i, place(i, far), far, far).wait_recv()
        for copy in copies:
            copy.wait()
        square.finish()
    else:

        @pl.loop(0, line.chips)
        def _(j):
            @pl.when(j > 0)
            def _():
                gather.arrive(j)

            attended_part(j)

    scatter.finish()
    gather.finish()


def middle_backward(n, spread, grads, gu, mid, cot, gain, wo, normed, hidden, cot_all, wd):
    rows, width = mid.shape
    group = grads.shape[0]
    blocks, _, _, fb = gu.shape
    own = blocks * fb
    parts = [(4, width, fb), (4, width, fb), (4, fb, width), (width, fb), (width, fb), (fb // 4, width), (3 * fb, width)]
    if not spread:
        parts = [(16, 128)] * 7
    scratch = []
    if spread:
        scratch = [
            pltpu.VMEM((2, width, fb), BF16),
            pltpu.VMEM((2, width, fb), BF16),
            pltpu.VMEM((2, 2, fb // 2, width), BF16),
            pltpu.VMEM((width, fb), BF16),
            pltpu.VMEM((width, fb), BF16),
            pltpu.VMEM((2, fb // 2, width), BF16),
            pltpu.VMEM((width, fb), BF16),
            pltpu.VMEM((fb // 2, width), BF16),
            pltpu.VMEM((2, blocks, width // 4, fb), BF16),
            DMA((2, blocks)),
            DMA((7,)),
            pltpu.VMEM((group, own + width // 2), BF16),
            DMA((3,)),
        ] + Square.scratch(4, 4) + [DMA((4, 4)), DMA((4, 4))]
        again = Scatter.scratch(n, rows, width)
        scratch += again[2:3] + again[4:]
    return pl.pallas_call(
        functools.partial(middle_kernel, n, blocks, spread),
        name="middle_backward",
        out_shape=(
            jax.ShapeDtypeStruct((rows, width), F32),
            jax.ShapeDtypeStruct((n, rows, width), BF16),
            jax.ShapeDtypeStruct((group, wo.shape[0]), BF16),
            jax.ShapeDtypeStruct((1, width), F32),
            jax.ShapeDtypeStruct((rows, width) if spread else (16, 128), BF16),
            *[jax.ShapeDtypeStruct(shape, BF16) for shape in parts],
        ),
        in_specs=[ANY, ANY, ANY, ANY, VMEM, ANY, ANY, ANY, ANY, ANY],
        out_specs=(VMEM, ANY, VMEM, VMEM, VMEM) + (ANY,) * 7,
        scratch_shapes=Scatter.scratch(n, rows, width)
        + Gather.scratch(n)
        + [
            pltpu.VMEM(mid.shape, F32),
            pltpu.VMEM(cot.shape, BF16),
            pltpu.VMEM(wo.shape, BF16),
            DMA((3,)),
            pltpu.VMEM((group, 2 * own), BF16),
            pltpu.VMEM((rows, width), BF16),
            pltpu.VMEM((2, rows, width), BF16),
            pltpu.VMEM((width, 2 * own), BF16),
            DMA((2, blocks)),
            DMA(()),
        ]
        + scratch,
        compiler_params=pltpu.CompilerParams(collective_id=2, has_side_effects=True, vmem_limit_bytes=62 * 2**20),
        cost_estimate=pl.CostEstimate(flops=2 * group * width * own * 3, bytes_accessed=400 * 2**20, transcendentals=0),
    )(grads, gu, mid, cot, gain, wo, normed, hidden, cot_all, wd)


STAGED = 15


def end_kernel(
    n, reps, spread, heads, long_len, *refs,
):
    operands, refs = refs[:STAGED], refs[STAGED:]
    gain, gain_m_sum, gate_q, up_q, down_q, normed, gml, grad_tok, gain_grads, grads = refs[:10]
    gate_out, up_out, down_out, q_out, kv_out, out_out, *scratch = refs[10:]
    staged, stage_sem, scratch = scratch[:STAGED], scratch[STAGED], scratch[STAGED + 1 :]
    (
        q_in, kv, lse, att_t, grad_att, rank_row, rank_col, seg_row, seg_col, cos_t, sin_t, w, tok, grad_mid, attended,
    ) = staged
    stage_copies = [pltpu.make_async_copy(src, dst, stage_sem.at[i]) for i, (src, dst) in enumerate(zip(operands, staged))]
    for copy in stage_copies:
        copy.start()
    scatter_scratch, att_scratch, scratch = scratch[:8], scratch[8:13], scratch[13:]
    gain_sum, gain_src, gain_land, gain_all, g_send, g_recv = scratch[:6]
    line = Line(n)
    rows, width = tok.shape
    me, rep = line.me, line.replica
    scatter = Scatter(line, scatter_scratch)
    line.enter_all(reps)
    if spread:
        (
            a_send, a_recv, x_send, x_recv, local_sem, qkv_land, qkv_in, out_land, out_in, qkv_tmp, out_tmp,
            qkv_parts, out_parts, slots, slot_sem,
        ) = scratch[6:21]
        fb = gate_q.shape[-1]
        own = 4 * fb
        quarters, outs = (gate_q, up_q), (gate_out, up_out)
        w_rows = gate_out.shape[0]
        down_rows = down_q.shape[0] // 2
        q_cols = heads * HD
        qkv_rows = w_rows // 4
        out_rows = out_parts.shape[1] // 2
        counts = (n, n, 2, n, 2, n)
        units = [
            dict(
                parts=qkv_parts, row=i * 4 * qkv_rows, rows=4 * qkv_rows, x_first=i == 0,
                land1=qkv_land.at[i], land2=qkv_in.at[i], tmp=qkv_tmp,
            )
            for i in range(2)
        ] + [
            dict(
                parts=out_parts, row=i * out_rows, rows=out_rows, x_first=i == 0,
                land1=out_land.at[i], land2=out_in.at[i], tmp=out_tmp,
            )
            for i in range(2)
        ]
        square = Square(line, units, scratch[21:])

        def place(k, f, replica):
            if k == 2:
                return down_out.at[pl.ds(pl.multiple_of(replica * 2 * down_rows + f * down_rows, 16), down_rows)]
            if k in (3, 5):
                at = pl.ds(pl.multiple_of(replica * qkv_rows, 16), qkv_rows)
                if k == 3:
                    return q_out.at[at, pl.ds(pl.multiple_of(f * q_cols, 128), q_cols)]
                return kv_out.at[at, pl.ds(pl.multiple_of(f * 2 * HD, 128), 2 * HD)]
            if k == 4:
                return out_out.at[pl.ds(pl.multiple_of(replica * 2 * out_rows + f * out_rows, 16), out_rows)]
            return outs[k].at[:, pl.ds(pl.multiple_of(f * own + replica * fb, 128), fb)]

        def block(k, f):
            if k in (3, 5):
                half, inner = lax.div(f, 4), lax.rem(f, 4)
                cols = pl.ds(0, q_cols) if k == 3 else pl.ds(q_cols, 2 * HD)
                return qkv_land.at[half, 0, pl.ds(pl.multiple_of(inner * qkv_rows, 16), qkv_rows), cols]
            return quarters[k].at[pl.ds(pl.multiple_of(f * w_rows, 16), w_rows)]

        def exchange(k, to, at):
            return remote(block(k, to), place(k, at, rep), a_send.at[k, to], a_recv.at[k, at], (rep, to))

        def exchange_at(d, kinds):
            if d == 0:
                for k in kinds:
                    exchange(k, 2 * line.z + 1 - line.c, me).start()
                return
            for to in (line.z + d, line.z - d):

                @pl.when((to >= 0) & (to < line.chips))
                def _():
                    for core in range(2):
                        for k in kinds:
                            exchange(k, 2 * to + core, me).start()

        def send(way, k, f, src, replica, device):
            return remote(src, place(k, f, replica), x_send.at[way, k, f], x_recv.at[way, k, f], (device, me))

        def share(k, f, src):
            send(0, k, f, src, rep, line.xn).start()
            send(1, k, f, src, rep, line.yn).start()

        def corner(core):
            return (0, line.xn, line.yn) if core % 2 == 0 else (1, line.yn, line.xn)

        def forward_all(z, kinds):
            for k in kinds:
                for core in range(2):
                    forward(k, 2 * z + core, core)

        def forward(k, f, core):
            way, replica, device = corner(core)
            src = place(k, f, replica)
            send(way, k, f, src, replica, replica).wait_recv()
            send(2 + way, k, f, src, replica, device).start()

        def local(i, src, dst):
            return pltpu.make_async_copy(src, dst, local_sem.at[i])

        def mine(k):
            return local(k, block(k, me), place(k, me, rep))

        def down_piece(i):
            return down_q.at[pl.ds(i * down_rows, down_rows)]

        def mine_down(i):
            return local((2, 4)[i], down_piece(i), place(2, i, rep))

        def mine_out(i):
            return local(6 + i, out_land.at[i, 0], place(4, i, rep))

        fetches = [pltpu.make_async_copy(src, slots.at[i], slot_sem.at[i]) for i, src in enumerate((gml, normed))]

        def stream(i, use):
            fetches[i].wait()
            for t in range(0, width, 512):
                use(t, slots[i, :, t : t + 512])

        def out_tile(at, x):
            part = tdot(attended[...], x).astype(BF16)
            for b in range(4):
                out_parts[b, :, at : at + x.shape[1]] = part[b * 2 * out_rows : (b + 1) * 2 * out_rows]

        def qkv_tile(at, x):
            part = tdot(x, grads[...]).astype(BF16)
            for i in range(x.shape[1] // w_rows):
                f = at // w_rows + i
                for b in range(4):
                    piece = part[i * w_rows + b * qkv_rows : i * w_rows + (b + 1) * qkv_rows]
                    qkv_parts[b, f * qkv_rows : (f + 1) * qkv_rows, :] = piece

        for fetch in fetches:
            fetch.start()
        for k in range(2):
            share(k, me, block(k, me))
            mine(k).start()
        for i in range(2):
            share(2, i, down_piece(i))
            mine_down(i).start()
        exchange_at(0, (0, 1))
        exchange_at(1, (0, 1))
        for copy in stage_copies:
            copy.wait()
        stream(0, out_tile)
        square.start(2)
        square.start(3)

    def pass_on(z, kinds):
        for core in range(2):
            f = 2 * z + core

            @pl.when(f != me)
            def _():
                for k in kinds:
                    exchange(k, me, f).wait_recv()
                    share(k, f, place(k, f, rep))

    if not spread:
        for copy in stage_copies:
            copy.wait()

    def after_block(b):
        if not spread:
            return
        if b == 0:
            pass_on(line.near_first(0), (0, 1))
            exchange_at(2, (0, 1))
        if b == 2:
            for d in range(3, line.chips):
                exchange_at(d, (0, 1))

    attention_back_kernel(
        heads, long_len, q_in, kv, lse, att_t, grad_att, rank_row, rank_col, seg_row, seg_col, cos_t, sin_t, grads,
        *att_scratch, after_block,
    )
    if spread:
        stream(1, qkv_tile)
        square.start(0)
        square.start(1)
        pass_on(line.near_first(1), (0, 1))

    def normed_part(d):
        x = grads[rows_of(d, rows), :]
        for t in range(0, width, 512):
            part = dot_t(x, w[t : t + 512, :]).astype(BF16)
            scatter.part[rows_of(d, rows), t : t + 512] = part

    scatter.produce(normed_part, hold_last=spread)
    if spread:
        for u in range(4):
            square.fold(u)
        for i in range(2):
            forward(2, i, i)
        forward_all(line.near_first(0), (0, 1))
        square.result(0)
        square.result(1)
        for d in range(line.chips):
            exchange_at(d, (3, 5))
        for k in (3, 5):
            share(k, me, block(k, me))
            mine(k).start()
        scatter.emit_last()
        square.result(2)
        square.result(3)
        for i in range(2):
            share(4, i, out_land.at[i, 0])
            mine_out(i).start()
        pass_on(line.near_first(2), (0, 1))
        forward_all(line.near_first(1), (0, 1))
    for s in range(line.chips - 1):
        scatter.duty(s)
        if spread:
            if s == 0:
                pass_on(line.near_first(3), (0, 1))
            if s == 1:
                forward_all(line.near_first(2), (0, 1))
                for i in range(2):
                    forward(4, i, i)
            if s == 2:
                forward_all(line.near_first(3), (0, 1))
    scatter.own_sum()
    gain_sum[...] = jnp.zeros_like(gain_sum)

    def back(at):
        through, gain_term = norm_back(scatter.total[at, :], tok[at, :].astype(F32), gain[...])
        grad_tok[at, :] = grad_mid[at, :] + through
        gain_sum[...] += jnp.sum(gain_term, 0, keepdims=True)

    row_chunks(rows, back)

    g_rows = gain_grads.shape[1]
    gain_src[...] = jnp.zeros_like(gain_src)
    for f in range(n):
        gain_src[f, 0:1, :] = gain_sum[:, f * g_rows : (f + 1) * g_rows]
        gain_src[f, 1:2, :] = gain_m_sum[:, f * g_rows : (f + 1) * g_rows]

    def gain_copy(i, to, slot):
        return remote(gain_src.at[to], gain_land.at[slot], g_send.at[0, i], g_recv.at[0, slot], (rep, to))

    def gain_share(i, to, slot):
        return remote(gain_all.at[slot], gain_all.at[slot], g_send.at[1, i], g_recv.at[1, slot], (to, me))

    for i in range(1, n):
        gain_copy(i, line.other(i), me).start()
    gain_land[me] = gain_src[me]
    if spread:
        for j in range(line.chips):
            pass_on(line.near_first(j), (3, 5))
    for i in range(1, n):
        gain_copy(i, me, line.other(i)).wait_recv()
    gain_all[rep] = functools.reduce(lambda a, b: a + b, [gain_land[i] for i in range(n)])
    for i in range(1, reps):
        gain_share(i, lax.rem(rep + i, reps), rep).start()
    if spread:
        for j in range(line.chips):
            forward_all(line.near_first(j), (3, 5))
    for i in range(1, reps):
        gain_share(i, rep, lax.rem(rep + i, reps)).wait_recv()
    gain_grads[...] = functools.reduce(lambda a, b: a + b, [gain_all[i] for i in range(reps)])
    for i in range(1, n):
        gain_copy(i, line.other(i), me).wait_send()
    for i in range(1, reps):
        gain_share(i, lax.rem(rep + i, reps), rep).wait_send()
    if spread:
        for k in (0, 1, 3, 5):
            mine(k).wait()
        for i in range(2):
            mine_out(i).wait()
            mine_down(i).wait()
        for k in (0, 1, 3, 5):
            for i in range(1, n):
                exchange(k, line.other(i), me).wait_send()
        for k in range(6):
            for f in range(counts[k]):
                src = place(k, f, rep)
                send(0, k, f, src, rep, line.xn).wait_send()
                send(1, k, f, src, rep, line.yn).wait_send()
                way, replica, device = corner(f)
                send(2 + way, k, f, src, replica, device).wait_send()
                send(2 + way, k, f, src, line.diag, replica).wait_recv()
                far = (line.yn, line.xn)[way]
                send(1 - way, k, f, src, far, far).wait_recv()
        square.finish()
    scatter.finish()


def end_layer(
    n, reps, spread, heads, long_len, q_in, kv, lse, att_t, grad_att, ranks, cos_t, sin_t,
    w, tok, grad_mid, gain, gain_m_sum, attended, gate_q, up_q, down_q, normed, gml,
):
    rows, width = tok.shape
    group = attended.shape[0]
    n_blocks = group // QBLK
    cols = w.shape[1]
    w_rows = width // n
    shapes, scratch = [(16, 128)] * 6, []
    if spread:
        fb = gate_q.shape[-1]
        own = 4 * fb
        heads_rows = attended.shape[1] // 4
        q_rows = w_rows // 4
        shapes = [(w_rows, n * own)] * 2 + [(fb, width), (w_rows, n * heads * HD), (w_rows, n * 2 * HD), (4 * heads_rows, width)]
        scratch = [
            DMA((6, n)),
            DMA((6, n)),
            DMA((4, 6, n)),
            DMA((4, 6, n)),
            DMA((8,)),
            pltpu.VMEM((2, 2, 4 * q_rows, cols), BF16),
            pltpu.VMEM((2, 4 * q_rows, cols), BF16),
            pltpu.VMEM((2, 2, heads_rows // 2, width), BF16),
            pltpu.VMEM((2, heads_rows // 2, width), BF16),
            pltpu.VMEM((4 * q_rows, cols), BF16),
            pltpu.VMEM((heads_rows // 2, width), BF16),
            pltpu.VMEM((4, width // 4, cols), BF16),
            pltpu.VMEM((4, heads_rows, width), BF16),
            pltpu.VMEM((2, group, width), BF16),
            DMA((2,)),
        ] + Square.scratch(4, 1)
    operands = [q_in, kv, lse, att_t, grad_att, *ranks, cos_t, sin_t, w, tok, grad_mid, attended]
    return pl.pallas_call(
        functools.partial(end_kernel, n, reps, spread, heads, long_len),
        name="end_layer",
        out_shape=(
            jax.ShapeDtypeStruct((rows, width), F32),
            jax.ShapeDtypeStruct((8, w_rows), F32),
            jax.ShapeDtypeStruct((group, cols), BF16),
            *[jax.ShapeDtypeStruct(shape, BF16) for shape in shapes],
        ),
        in_specs=[ANY] * STAGED + [VMEM] * 2 + [ANY] * 5,
        out_specs=(VMEM, VMEM, VMEM) + (ANY,) * 6,
        scratch_shapes=[pltpu.VMEM(x.shape, x.dtype) for x in operands]
        + [DMA((STAGED,))]
        + Scatter.scratch(n, rows, width)
        + [
            pltpu.VMEM((2, group, HD), F32),
            pltpu.VMEM((cols, group), BF16),
            pltpu.VMEM((HD, group), BF16),
            pltpu.VMEM((n_blocks, heads * QBLK, HD), BF16),
            pltpu.VMEM((heads * HD, group), F32),
            pltpu.VMEM((1, width), F32),
            pltpu.VMEM((n, 8, w_rows), F32),
            pltpu.VMEM((n, 8, w_rows), F32),
            pltpu.VMEM((reps, 8, w_rows), F32),
            DMA((2, max(n, reps))),
            DMA((2, max(n, reps))),
        ]
        + scratch,
        compiler_params=pltpu.CompilerParams(collective_id=3, has_side_effects=True, vmem_limit_bytes=VMEM_BYTES),
        cost_estimate=pl.CostEstimate(flops=2 * group * width * cols, bytes_accessed=400 * 2**20, transcendentals=0),
    )(
        *operands, gain, gain_m_sum, gate_q, up_q, down_q, normed, gml,
    )


def body(
    tokens, segment, position, attn_gain, w_query, w_key, w_value, w_out, mlp_gain, w_gate, w_up, w_down, cotangent
):
    rows, width = tokens.shape
    group = segment.shape[0]
    long_len = group * 2 // 3
    n = lax.axis_size("fsdp")
    reps = lax.axis_size("replica")
    w_rows = w_query.shape[0]
    ff_own = w_gate.shape[1] // n
    ff_blk = ff_own // reps
    heads = H // n
    q_cols = heads * HD
    dup = n // KVH
    spread = reps == 4 and ff_blk % 128 == 0

    def swap(x):
        return lax.all_to_all(x, "fsdp", 0, 0, tiled=True)

    (
        q_in, kv, lse, att_t, attended, *ranks, cos_back, sin_back, gain_a, gain_m, normed_all, qkv_w, gu_own,
    ) = start_layer(
        n, reps, spread, heads, long_len, tokens, attn_gain, mlp_gain, segment, position, w_key, w_value, w_query, w_gate,
        w_up,
    )
    normed_all = normed_all.reshape(group, width)
    qkv_w = qkv_w.reshape(width, q_cols + 2 * HD)
    if not spread:
        gate_up = jnp.stack([w.reshape(w_rows, n, ff_own).transpose(1, 0, 2) for w in (w_gate, w_up)], 1)
        gu_own = swap(gate_up).transpose(1, 0, 2, 3).reshape(1, 2, width, ff_own)
    normed_mlp, middle, hidden, grads, gate_up, cot_all = mlp_forward(
        n, reps, spread, attended, w_out, tokens, gain_m, gu_own, cotangent, w_down
    )
    normed_mlp, cot_all = normed_mlp.reshape(group, width), cot_all.reshape(group, width)
    if not spread:
        gate_up = gu_own

    def over_replicas(x):
        return lax.psum_scatter(x, "replica", scatter_dimension=0, tiled=True)

    grad_mid, gml, grad_att, gain_m_sum, output, _, _, _, gate_q, up_q, down_q, down_first = middle_backward(
        n, spread, grads, gate_up, middle, cotangent, gain_m, w_out, normed_mlp, hidden, cot_all, w_down
    )
    gml = gml.reshape(group, width)
    if not spread:

        def column_blocks(first):
            grad = tdot(normed_mlp, grads[:, first : first + ff_own]).astype(BF16)
            return grad.reshape(width, reps, ff_blk).transpose(1, 0, 2).reshape(reps * width, ff_blk)

        gate_q, up_q = over_replicas(column_blocks(0)), over_replicas(column_blocks(ff_own))
        down_q = over_replicas(tdot(hidden, cot_all).astype(BF16))
        down = lax.psum_scatter(dot(hidden, w_down).astype(BF16), "fsdp", scatter_dimension=0, tiled=True)
        output = (middle + down.astype(F32)).astype(BF16)
    grad_tokens, gain_grads, grad_qkv, grad_gate, grad_up, down_second, grad_w_query, grad_kv, grad_out_w = end_layer(
        n, reps, spread, heads, long_len, q_in, kv, lse, att_t, grad_att, ranks, cos_back, sin_back,
        qkv_w, tokens, grad_mid, gain_a, gain_m_sum, attended, gate_q, up_q, down_q, normed_all, gml,
    )
    if spread:
        parts = [x.reshape(reps, -1, width) for x in (down_first, down_second)]
        grad_down = jnp.concatenate(parts, 1).reshape(ff_own, width)
    else:

        def by_rows(grad):
            grad = swap(grad.reshape(n, w_rows, -1))
            grad = lax.all_gather(grad, "replica", axis=0, tiled=False)
            return grad.transpose(2, 1, 0, 3).reshape(w_rows, -1)

        grad_gate, grad_up = by_rows(gate_q), by_rows(up_q)
        grad_down = lax.all_gather(down_q, "replica", axis=0, tiled=True)
        grad_w = tdot(normed_all, grad_qkv).astype(BF16)
        grad_w = grad_w.reshape(n, reps, w_rows // reps, -1).transpose(1, 0, 2, 3)
        grad_w = over_replicas(grad_w)[0]
        grad_w = lax.all_gather(swap(grad_w), "replica", axis=0, tiled=False)
        grad_w = grad_w.transpose(0, 2, 1, 3).reshape(w_rows, n, -1)
        grad_w_query, grad_kv = grad_w[:, :, :q_cols].reshape(w_rows, H * HD), grad_w[:, :, q_cols:]
        grad_out_w = lax.psum(tdot(attended, gml).astype(BF16), "replica")
    grad_kv = grad_kv.reshape(w_rows, KVH, dup, 2 * HD).astype(F32).sum(2)
    grad_w_key = grad_kv[:, :, :HD].reshape(w_rows, KVH * HD)
    grad_w_value = grad_kv[:, :, HD:].reshape(w_rows, KVH * HD)
    return (
        output,
        grad_tokens,
        gain_grads[0],
        grad_w_query.astype(F32),
        grad_w_key,
        grad_w_value,
        grad_out_w.astype(F32),
        gain_grads[1],
        grad_gate.astype(F32),
        grad_up.astype(F32),
        grad_down.astype(F32),
    )


def solution(mesh):
    both = P(("replica", "fsdp"), None)
    mat = P("fsdp", None)
    vec = P("fsdp")
    return jax.shard_map(
        body,
        mesh=mesh,
        in_specs=(both, P("replica"), P("replica"), vec, mat, mat, mat, mat, vec, mat, mat, mat, both),
        out_specs=(both, both, vec, mat, mat, mat, mat, vec, mat, mat, mat),
        check_vma=False,
    )
```

```python
import functools
import math

import jax
import jax.numpy as jnp
from jax import lax
from jax.experimental import pallas as pl
from jax.experimental.pallas import tpu as pltpu
from jax.sharding import PartitionSpec as P

H = 32
KVH = 8
HD = 64
EPSILON = 1e-05
ROPE_BASE = 500000.0
MASKED = -1e30
QBLK = 256
F32 = jnp.float32
BF16 = jnp.bfloat16
MESH = pl.DeviceIdType.MESH
VMEM = pl.BlockSpec(memory_space=pltpu.VMEM)
ANY = pl.BlockSpec(memory_space=pl.ANY)
DMA = pltpu.SemaphoreType.DMA
VMEM_BYTES = 60 * 2**20


def dot(a, b):
    return jnp.dot(a, b, preferred_element_type=F32)


def tdot(a, b):
    return lax.dot_general(a, b, (((0,), (0,)), ((), ())), preferred_element_type=F32)


def dot_t(a, b):
    return lax.dot_general(a, b, (((1,), (1,)), ((), ())), preferred_element_type=F32)


class Line:
    def __init__(self, n):
        f = lax.axis_index("fsdp")
        self.n = n
        self.replica = lax.axis_index("replica")
        self.chips = n // 2
        self.z = lax.div(f, 2)
        self.c = lax.rem(f, 2)
        self.me = f
        x, y = lax.rem(self.replica, 2), lax.div(self.replica, 2)
        self.xn, self.yn = self.replica + 1 - 2 * x, self.replica + 2 - 4 * y
        self.diag = 3 - self.replica

    def dev(self, z, c):
        return (self.replica, 2 * z + c)

    def other(self, i):
        return lax.rem(self.me + i, self.n)

    def enter(self, square=False):
        barrier = pltpu.get_barrier_semaphore()
        z, c = self.z, self.c

        def greet(device):
            pl.semaphore_signal(barrier, inc=1, device_id=device, device_id_type=MESH)

        greet(self.dev(z, 1 - c))

        @pl.when(z > 0)
        def _():
            greet(self.dev(z - 1, c))

        @pl.when(z < self.chips - 1)
        def _():
            greet(self.dev(z + 1, c))

        count = 1 + (z > 0).astype(jnp.int32) + (z < self.chips - 1).astype(jnp.int32)
        if square:
            greet((self.xn, self.me))
            greet((self.yn, self.me))
            count = count + 2
        pl.semaphore_wait(barrier, count)

    def enter_all(self, reps, square=False):
        barrier = pltpu.get_barrier_semaphore()

        def greet(device):
            pl.semaphore_signal(barrier, inc=1, device_id=device, device_id_type=MESH)

        for i in range(1, self.n):
            greet((self.replica, self.other(i)))
        if square:
            greet((self.xn, self.me))
            greet((self.yn, self.me))
        else:
            for i in range(1, reps):
                greet((lax.rem(self.replica + i, reps), self.me))
        pl.semaphore_wait(barrier, self.n - 1 + (2 if square else reps - 1))

    def far_first(self, s):
        z, last = self.z, self.chips - 1
        right = last - z
        low = jnp.where(s < right, last - s, s - right)
        high = jnp.where(s < z, s, last - (s - z))
        return jnp.where(2 * z < self.chips, low, high)

    def near_first(self, j):
        z, last = self.z, self.chips - 1
        short = jnp.minimum(z, last - z)
        half = lax.div(j + 1, 2)
        both = jnp.where(lax.rem(j, 2) == 1, z - half, z + half)
        rest = jnp.where(2 * z < self.chips, j, last - j)
        return jnp.where(j <= 2 * short, both, rest)


def remote(src, dst, send, recv, device):
    return pltpu.make_async_remote_copy(
        src_ref=src, dst_ref=dst, send_sem=send, recv_sem=recv, device_id=device, device_id_type=MESH
    )


def row_step(rows):
    return 32 if rows % 32 == 0 else 16


def row_chunks(rows, fn):
    step = row_step(rows)

    @pl.loop(0, rows // step)
    def _(i):
        fn(pl.ds(pl.multiple_of(i * step, step), step))


PARTS = 2


class Scatter:
    @staticmethod
    def scratch(n, rows, width):
        chips = n // 2
        return [
            pltpu.VMEM((n * rows, width), BF16),
            pltpu.VMEM((chips, rows, width), BF16),
            pltpu.VMEM((chips + 1, rows, width), BF16),
            pltpu.VMEM((rows, width), F32),
            DMA((chips,)),
            DMA((chips,)),
            DMA((chips, PARTS)),
            DMA((chips + 1, PARTS)),
        ]

    def __init__(self, line, scratch):
        self.line = line
        self.part, self.sib, self.rx, self.total = scratch[:4]
        self.sib_send, self.sib_recv, self.line_send, self.line_recv = scratch[4:]
        self.rows, self.width = self.total.shape
        self.rows_q = self.rows // PARTS

    def rows_at(self, d, c, first=0, count=None):
        at = (2 * d + c) * self.rows + first
        return pl.ds(pl.multiple_of(at, 16), self.rows if count is None else count)

    def to_sibling(self, d):
        line = self.line
        return remote(
            self.part.at[self.rows_at(d, 1 - line.c)], self.sib.at[d], self.sib_send.at[d], self.sib_recv.at[d], line.dev(line.z, 1 - line.c)
        )

    def along(self, d, slot, q, z):
        c = self.line.c
        at = pl.ds(q * self.rows_q, self.rows_q)
        return remote(
            self.part.at[self.rows_at(d, c, q * self.rows_q, self.rows_q)], self.rx.at[slot, at], self.line_send.at[d, q], self.line_recv.at[slot, q], self.line.dev(z, c)
        )

    def to_right(self, d, q):
        return self.along(d, d, q, self.line.z + 1)

    def to_left(self, d, q):
        z = self.line.z
        return self.along(d, jnp.where(d == z - 1, self.line.chips, d), q, z - 1)

    def wait_line(self, slot, q):
        line = self.line
        at = pl.ds(q * self.rows_q, self.rows_q)
        here = self.rx.at[slot, at]
        remote(here, here, self.line_send.at[0, q], self.line_recv.at[slot, q], line.dev(line.z, 1 - line.c)).wait_recv()

    def add(self, d, q, with_line):
        step = row_step(self.rows_q)
        c = self.line.c

        @pl.loop(0, self.rows_q // step)
        def _(i):
            at = pl.ds(pl.multiple_of(q * self.rows_q + i * step, step), step)
            here = self.rows_at(d, c, q * self.rows_q + i * step, step)
            value = self.part[here, :].astype(F32) + self.sib[d, at, :].astype(F32)
            if with_line:
                value = value + self.rx[d, at, :].astype(F32)
            self.part[here, :] = value.astype(BF16)

    def emit(self, d):
        z = self.line.z
        self.to_sibling(d).wait_recv()
        for q in range(PARTS):
            self.add(d, q, False)

            @pl.when(z == 0)
            def _():
                self.to_right(d, q).start()

            @pl.when(z > 0)
            def _():
                self.to_left(d, q).start()

    def emit_last(self):
        line = self.line

        @pl.when((line.z == 0) | (line.z == line.chips - 1))
        def _():
            self.emit(line.far_first(line.chips - 2))

    def produce(self, compute, after_first=None, between=None, hold_last=False):
        line = self.line
        chips, z = line.chips, line.z

        def step(s):
            d = line.far_first(s)
            compute(d)
            self.to_sibling(d).start()

            @pl.when(((z == 0) | (z == chips - 1)) & (s > 0) & (s < (chips - 1 if hold_last else chips)))
            def _():
                self.emit(line.far_first(s - 1))
                if after_first is not None:

                    @pl.when(s == 1)
                    def _():
                        after_first()

        if between is None:
            pl.loop(0, chips)(step)
        else:
            for s in range(chips):
                step(s)
                between(s)

    def duty(self, s, sides=(True, False)):
        chips, z, c = self.line.chips, self.line.z, self.line.c
        for near in sides:
            right = (2 * z < chips) if near else (2 * z >= chips)
            d = jnp.where(right, chips - 1 - s, s)
            active = jnp.where(right, (z > 0) & (d > z), (z < chips - 1) & (d < z))

            @pl.when(active)
            def _():
                self.to_sibling(d).wait_recv()
                for q in range(PARTS):
                    self.wait_line(d, q)
                    self.add(d, q, True)
                    slot = jnp.where(~right & (d == z - 1), chips, d)
                    self.along(d, slot, q, jnp.where(right, z + 1, z - 1)).start()

    def own_sum(self):
        chips, z, c = self.line.chips, self.line.z, self.line.c
        total, rx = self.total, self.rx
        self.to_sibling(z).wait_recv()
        for q in range(PARTS):

            @pl.when(z > 0)
            def _():
                self.wait_line(z, q)

            @pl.when(z < chips - 1)
            def _():
                self.wait_line(chips, q)

        def add_up(at):
            total[at, :] = self.part[self.rows_at(z, c, at.start, at.size), :].astype(F32) + self.sib[z, at, :].astype(F32)

            @pl.when(z > 0)
            def _():
                total[at, :] += rx[z, at, :].astype(F32)

            @pl.when(z < chips - 1)
            def _():
                total[at, :] += rx[chips, at, :].astype(F32)

        row_chunks(self.rows, add_up)

    def finish(self):
        z = self.line.z

        @pl.loop(0, self.line.chips)
        def _(d):
            self.to_sibling(d).wait_send()
            for q in range(PARTS):

                @pl.when(d > z)
                def _():
                    self.to_right(d, q).wait_send()

                @pl.when(d < z)
                def _():
                    self.to_left(d, q).wait_send()


class Gather:
    @staticmethod
    def scratch(n):
        return [DMA((3, n)), DMA((n,)), DMA(())]

    def __init__(self, line, own, buf, scratch):
        self.line, self.own, self.buf = line, own, buf
        self.send, self.recv, self.local_sem = scratch

    def copy(self, way, slot, mine=False):
        line, z, c = self.line, self.line.z, self.line.c
        src = self.own if mine else self.buf.at[slot]
        device = (line.dev(z, 1 - c), line.dev(z + 1, c), line.dev(z - 1, c))[way]
        return remote(src, self.buf.at[slot], self.send.at[way, slot], self.recv.at[slot], device)

    def local(self):
        return pltpu.make_async_copy(self.own, self.buf.at[self.line.me], self.local_sem)

    def along(self, at, mine=False):
        z, slot = self.line.z, 2 * at + self.line.c

        @pl.when((z < self.line.chips - 1) & (at <= z))
        def _():
            self.copy(1, slot, mine).start()

        @pl.when((z > 0) & (at >= z))
        def _():
            self.copy(2, slot, mine).start()

    def pass_on(self, at, mine=False):
        self.along(at, mine)
        self.copy(0, 2 * at + self.line.c, mine).start()

    def start(self, ends_later=False):
        line = self.line
        if ends_later:

            @pl.when((line.z > 0) & (line.z < line.chips - 1))
            def _():
                self.along(line.z, True)

            self.copy(0, line.me, True).start()
        else:
            self.pass_on(line.z, True)
        self.local().start()

    def start_ends(self):
        self.along(self.line.z, True)

    def arrive(self, t, sides=(True, False)):
        z, chips = self.line.z, self.line.chips
        for far in sides:
            at = jnp.where((2 * z < chips) == far, z + t, z - t)
            there = (at >= 0) & (at < chips)

            @pl.when(there)
            def _():
                self.copy(0, 2 * at + self.line.c).wait_recv()
                self.pass_on(at)

    def ready(self, j):
        at = self.line.near_first(j)
        if isinstance(j, int):
            if j == 0:
                self.local().wait()
        else:

            @pl.when(j == 0)
            def _():
                self.local().wait()

        self.copy(0, 2 * at + 1 - self.line.c).wait_recv()
        return at

    def finish(self):
        z = self.line.z

        @pl.loop(0, self.line.chips)
        def _(at):
            slot = 2 * at + self.line.c
            self.copy(0, slot).wait_send()

            @pl.when((z < self.line.chips - 1) & (at <= z))
            def _():
                self.copy(1, slot).wait_send()

            @pl.when((z > 0) & (at >= z))
            def _():
                self.copy(2, slot).wait_send()


def load(src, dst, sem):
    copy = pltpu.make_async_copy(src, dst, sem)
    copy.start()
    copy.wait()


def rows_of(z, rows):
    return pl.ds(pl.multiple_of(z * 2 * rows, 2 * rows), 2 * rows)


class Square:
    @staticmethod
    def scratch(units, tiles):
        return [DMA((units, 2, tiles)), DMA((units, 2, tiles)), DMA((units,)), DMA((units,)), DMA(())]

    def __init__(self, line, units, scratch):
        self.line, self.units = line, units
        self.send1, self.recv1, self.send2, self.recv2, self.sem = scratch
        self.tiles = self.send1.shape[2]

    def ways(self, u):
        line = self.line
        return (line.xn, line.yn) if self.units[u]["x_first"] else (line.yn, line.xn)

    def whole(self, u, block):
        unit = self.units[u]
        return unit["parts"].at[block, pl.ds(unit["row"], unit["rows"])]

    def first(self, u, slot, t):
        unit = self.units[u]
        one, _ = self.ways(u)
        block = one if slot == 0 else self.line.diag
        src, dst = self.whole(u, block), unit["land1"].at[slot]
        if self.tiles > 1:
            axis = unit["axis"]
            step = dst.shape[axis] // self.tiles
            at = (pl.ds(t * step, step),) if axis == 0 else (slice(None), pl.ds(t * step, step))
            src, dst = src.at[at], dst.at[at]
        return remote(src, dst, self.send1.at[u, slot, t], self.recv1.at[u, slot, t], (one, self.line.me))

    def start(self, u, t=0):
        for slot in range(2):
            self.first(u, slot, t).start()

    def add(self, u, slot, block, also=None):
        unit = self.units[u]
        for t in range(self.tiles):
            self.first(u, slot, t).wait_recv()
        land, tmp = unit["land1"], unit["tmp"].at[pl.ds(0, unit["rows"])]
        load(self.whole(u, block), tmp, self.sem)

        def one(at):
            value = land[slot, at, :].astype(F32) + tmp[at, :].astype(F32)
            if also is not None:
                value = value + also[at, :].astype(F32)
            land[slot, at, :] = value.astype(BF16)

        row_chunks(unit["rows"], one)

    def second(self, u):
        unit = self.units[u]
        _, two = self.ways(u)
        return remote(unit["land1"].at[1], unit["land2"], self.send2.at[u], self.recv2.at[u], (two, self.line.me))

    def fold(self, u):
        self.add(u, 1, self.ways(u)[1])
        self.second(u).start()

    def result(self, u):
        self.second(u).wait_recv()
        self.add(u, 0, self.line.replica, self.units[u]["land2"])

    def finish(self):
        for u in range(len(self.units)):
            self.second(u).wait_send()
            for slot in range(2):
                for t in range(self.tiles):
                    self.first(u, slot, t).wait_send()


def key_range(block, long_len):
    longs = long_len // QBLK
    return (0, block + 1, False) if block < longs else (longs, block + 1 - longs, True)


def score_mask(q_block, k_block, seg_row, seg_col, heads, compare):
    visible = None
    shape = (QBLK, QBLK)
    if q_block == k_block:
        visible = lax.broadcasted_iota(jnp.int32, shape, 0) <= lax.broadcasted_iota(jnp.int32, shape, 1)
    if compare:
        k_at, q_at = k_block * QBLK, q_block * QBLK
        same = seg_col[k_at : k_at + QBLK, :] == seg_row[:, q_at : q_at + QBLK]
        visible = same if visible is None else visible & same
    if visible is None:
        return None
    bias = jnp.where(visible, 0.0, MASKED)
    return jnp.concatenate([bias] * heads, 1)


def one_hot_rows(rank_row, start):
    group = rank_row.shape[1]
    places = start + lax.broadcasted_iota(jnp.int32, (QBLK, group), 0)
    return jnp.where(rank_row[...] == places, 1.0, 0.0).astype(BF16)


def one_hot_back(rank_col, start):
    group = rank_col.shape[0]
    places = lax.broadcasted_iota(jnp.int32, (QBLK, group), 1)
    return jnp.where(rank_col[pl.ds(start, QBLK), :] == places, 1.0, 0.0).astype(BF16)


def attention_kernel(heads, long_len, qkv, rank_row, rank_col, seg_row, seg_col, q_out, kv_out, lse, att_t, att, s_buf, v_t):
    group = qkv.shape[0]
    q_cols = heads * HD
    n_blocks = group // QBLK
    for b in range(n_blocks):
        ordered = dot(one_hot_rows(rank_row, b * QBLK), qkv[...])
        for h in range(heads):
            q_out[b, h * QBLK : (h + 1) * QBLK, :] = (ordered[:, h * HD : (h + 1) * HD] * 0.125).astype(BF16)
        kv_out[0, b * QBLK : (b + 1) * QBLK, :] = ordered[:, q_cols : q_cols + HD].astype(BF16)
        values = ordered[:, q_cols + HD :]
        kv_out[1, b * QBLK : (b + 1) * QBLK, :] = values.astype(BF16)
        v_t[:, b * QBLK : (b + 1) * QBLK] = values.T.astype(BF16)
    for b in range(n_blocks):
        first, count, compare = key_range(b, long_len)
        queries = q_out[b]
        top = None
        for i in range(count):
            k_at = (first + i) * QBLK
            scores = dot_t(kv_out[0, k_at : k_at + QBLK, :], queries)
            bias = score_mask(b, first + i, seg_row, seg_col, heads, compare)
            if bias is not None:
                scores = scores + bias
            s_buf[i] = scores
            high = jnp.max(scores, 0, keepdims=True)
            top = high if top is None else jnp.maximum(top, high)
        total, out = 0.0, 0.0
        for i in range(count):
            k_at = (first + i) * QBLK
            terms = jnp.exp(s_buf[i] - top)
            total = total + jnp.sum(terms, 0, keepdims=True)
            out = out + dot(v_t[:, k_at : k_at + QBLK], terms.astype(BF16))
        lse[b] = top + jnp.log(total)
        out = out / total
        for h in range(heads):
            att_t[h * HD : (h + 1) * HD, b * QBLK : (b + 1) * QBLK] = out[:, h * QBLK : (h + 1) * QBLK]
    low = att_t[...].astype(BF16)

    @pl.loop(0, n_blocks)
    def _(b):
        at = pl.multiple_of(b * QBLK, QBLK)
        att[pl.ds(at, QBLK), :] = dot_t(one_hot_back(rank_col, at), low).astype(BF16)


def attention_back_kernel(
    heads, long_len, q_in, kv, lse, att_t, grad_att, rank_row, rank_col, seg_row, seg_col, cos_t, sin_t, out,
    grad_kv, grad_t, k_t, go_rows, go_t, after_block,
):
    group = kv.shape[1]
    n_blocks = group // QBLK
    half = HD // 2
    q_cols = heads * HD
    for b in range(n_blocks):
        at = b * QBLK
        ordered = dot(one_hot_rows(rank_row, at), grad_att[...])
        for h in range(heads):
            go_rows[b, h * QBLK : (h + 1) * QBLK, :] = ordered[:, h * HD : (h + 1) * HD].astype(BF16)
        go_t[:, at : at + QBLK] = ordered.T
        k_t[:, at : at + QBLK] = kv[0, at : at + QBLK, :].astype(F32).T.astype(BF16)
    grad_kv[...] = jnp.zeros_like(grad_kv)
    for b in range(n_blocks):
        first, count, compare = key_range(b, long_len)
        q_at = b * QBLK
        queries, grad_rows = q_in[b], go_rows[b]
        centre = jnp.concatenate(
            [
                jnp.sum(
                    go_t[h * HD : (h + 1) * HD, q_at : q_at + QBLK] * att_t[h * HD : (h + 1) * HD, q_at : q_at + QBLK],
                    0,
                    keepdims=True,
                )
                for h in range(heads)
            ],
            1,
        )
        grad_q = 0.0
        for i in range(count):
            k_at = (first + i) * QBLK
            scores = dot_t(kv[0, k_at : k_at + QBLK, :], queries)
            bias = score_mask(b, first + i, seg_row, seg_col, heads, compare)
            if bias is not None:
                scores = scores + bias
            probs = jnp.exp(scores - lse[b])
            grad_probs = dot_t(kv[1, k_at : k_at + QBLK, :], grad_rows)
            grad_scores = (probs * (grad_probs - centre)).astype(BF16)
            grad_kv[0, k_at : k_at + QBLK, :] += dot(grad_scores, queries)
            grad_kv[1, k_at : k_at + QBLK, :] += dot(probs.astype(BF16), grad_rows)
            grad_q = grad_q + dot(k_t[:, k_at : k_at + QBLK], grad_scores)
        cos_b, sin_b = cos_t[:, q_at : q_at + QBLK], sin_t[:, q_at : q_at + QBLK]

        def turned(value):
            front, back = value[:half], value[half:]
            return jnp.concatenate([front * cos_b + back * sin_b, back * cos_b - front * sin_b], 0).astype(BF16)

        for h in range(heads):
            grad_t[h * HD : (h + 1) * HD, q_at : q_at + QBLK] = turned(grad_q[:, h * QBLK : (h + 1) * QBLK] * 0.125)
        after_block(b)
    for b in range(n_blocks):
        at = b * QBLK
        cos_b, sin_b = cos_t[:, at : at + QBLK], sin_t[:, at : at + QBLK]
        value = grad_kv[0, at : at + QBLK, :].T
        front, back = value[:half], value[half:]
        grad_t[q_cols : q_cols + half, at : at + QBLK] = (front * cos_b + back * sin_b).astype(BF16)
        grad_t[q_cols + half : q_cols + HD, at : at + QBLK] = (back * cos_b - front * sin_b).astype(BF16)
        grad_t[q_cols + HD :, at : at + QBLK] = grad_kv[1, at : at + QBLK, :].T.astype(BF16)

    @pl.loop(0, n_blocks)
    def _(b):
        at = pl.multiple_of(b * QBLK, QBLK)
        out[pl.ds(at, QBLK), :] = dot_t(one_hot_back(rank_col, at), grad_t[...]).astype(BF16)


def order_group(long_len, ids, ids_col, rank_row, rank_col, seg_row_out, seg_col_out, pos_out, key_col, acc):
    group = ids.shape[1]
    seg_row, pos_row = ids.at[0:1, :], ids.at[1:2, :]

    def chunks(fn):
        @pl.loop(0, group // QBLK)
        def _(i):
            fn(pl.multiple_of(i * QBLK, QBLK))

    def ones(mask):
        return jnp.where(mask, 1.0, 0.0)

    acc[...] = jnp.zeros_like(acc)

    def lengths(at):
        here = pl.ds(at, QBLK)
        same = ones(ids_col[here, 0:1] == seg_row[...])
        acc[0:1, :] += jnp.sum(same, 0, keepdims=True)
        first = jnp.sum(same, 1, keepdims=True) == float(long_len)
        key_col[here, :] = jnp.where(first, -1.0, ids_col[here, 0:1]) * float(group) + ids_col[here, 1:2]

    chunks(lengths)
    key_row = jnp.where(acc[0:1, :] == float(long_len), -1.0, seg_row[...]) * float(group)
    acc[1:2, :] = key_row + pos_row[...]

    def ranks(at):
        here = pl.ds(at, QBLK)
        mine, others = key_col[here, :], acc[1:2, :]
        rank_col[here, :] = jnp.sum(ones(others < mine), 1, keepdims=True).astype(jnp.int32)
        acc[2:3, :] += jnp.sum(ones(mine < others), 0, keepdims=True)

    chunks(ranks)
    rank_row[...] = acc[2:3, :].astype(jnp.int32)

    def ordered(at):
        here = pl.ds(at, QBLK)
        places = at + lax.broadcasted_iota(jnp.int32, (QBLK, group), 0)
        seg = jnp.sum(jnp.where(rank_row[...] == places, seg_row[...], 0.0), 1, keepdims=True)
        seg_col_out[here, :] = seg.astype(jnp.int32)
        moved = rank_col[here, :] == lax.broadcasted_iota(jnp.int32, (QBLK, group), 1)
        acc[3:4, :] += jnp.sum(jnp.where(moved, ids_col[here, 0:1], 0.0), 0, keepdims=True)
        acc[4:5, :] += jnp.sum(jnp.where(moved, ids_col[here, 1:2], 0.0), 0, keepdims=True)

    chunks(ordered)
    seg_row_out[...] = acc[3:4, :].astype(jnp.int32)
    pos_out[...] = acc[4:5, :]


def frequencies(index):
    return jnp.exp(-math.log(ROPE_BASE) * index.astype(F32) * (2.0 / HD))


def start_kernel(
    n, reps, spread, heads, long_len, tok, gain_a_in, gain_m_in, seg_in, pos_in, wk, wv_in, wq, wg, wu,
    q_out, kv_out, lse, att_t, att, rank_row, rank_col, seg_row_out, seg_col_out, cos_back, sin_back, gain_a, gain_m,
    normed, w_all, gu_own,
    gains, ids, wkv, gains_buf, own, wv, blk, qkv, cos, sin, ids_col, key_col, acc, pos_out, s_buf, v_t,
    g_send, g_recv, a_send, a_recv, r_send, r_recv, u_send, u_recv, local_sem, load_sem, *ag_scratch,
):
    line = Line(n)
    me, rep = line.me, line.replica
    rows, width = tok.shape
    w_rows = wq.shape[0]
    fb = gu_own.shape[-1]
    own_cols = fb * reps
    gains[...] = jnp.zeros_like(gains)
    gains[0:1, :] = gain_a_in[...].astype(F32)
    gains[1:2, :] = gain_m_in[...].astype(F32)
    ids[...] = jnp.zeros_like(ids)
    ids[0:1, :] = seg_in[...].astype(F32)
    ids[1:2, :] = pos_in[...].astype(F32)
    line.enter_all(reps)

    def gain_copy(i, to, slot):
        return remote(gains, gains_buf.at[slot], g_send.at[i], g_recv.at[slot], (rep, to))

    q_cols = heads * HD
    mine_at = pl.ds(rep * (w_rows // reps), w_rows // reps)

    def qkv_pieces(to, slot):
        return (
            (wq.at[mine_at, pl.ds(pl.multiple_of(to * q_cols, 128), q_cols)], w_all.at[slot, rep, :, pl.ds(0, q_cols)]),
            (wkv.at[to, mine_at], w_all.at[slot, rep, :, pl.ds(q_cols, 2 * HD)]),
        )

    def qkv_copy(k, i, to, slot):
        src, dst = qkv_pieces(to, slot)[k]
        return remote(src, dst, a_send.at[k, i], a_recv.at[k, slot], (rep, to))

    def gu_copy(k, to, slot):
        piece = (wg, wu)[k].at[:, pl.ds(pl.multiple_of(to * own_cols + rep * fb, 128), fb)]
        at = pl.ds(pl.multiple_of(slot * w_rows, 16), w_rows)
        return remote(piece, gu_own.at[k, at], u_send.at[k, to], u_recv.at[k, slot], (rep, to))

    def spread_weights(stage):
        if not spread:
            return
        if stage == 0:
            for k in range(2):
                gu_copy(k, 2 * line.z + 1 - line.c, me).start()
            return
        last = line.chips - 1

        @pl.loop(1, line.chips)
        def _(d):
            for to in (line.z + d, line.z - d):
                to_end = (to == 0) | (to == last)
                next_to_end = ((line.z == 0) | (line.z == last)) & (d == 1)
                now = (to_end, (~to_end) & next_to_end, (~to_end) & (~next_to_end))[stage % 3]

                @pl.when((to >= 0) & (to <= last) & now)
                def _():
                    for core in range(2):
                        for k in range(2):
                            gu_copy(k, 2 * to + core, me).start()

    for i in range(1, n):
        gain_copy(i, line.other(i), me).start()
    for i in range(1, n):
        qkv_copy(0, i, line.other(i), me).start()
    for i in range(n):
        at = i * KVH // n * HD
        wkv[i] = jnp.concatenate([wk[:, at : at + HD], wv_in[:, at : at + HD]], 1)
    for i in range(1, n):
        qkv_copy(1, i, line.other(i), me).start()
    own_pieces = qkv_pieces(me, me)
    mine = [
        pltpu.make_async_copy(*own_pieces[0], local_sem.at[0]),
        pltpu.make_async_copy(*own_pieces[1], local_sem.at[3]),
    ]
    if spread:
        for k in range(2):
            piece = (wg, wu)[k].at[:, pl.ds(pl.multiple_of(me * own_cols + rep * fb, 128), fb)]
            at = pl.ds(pl.multiple_of(me * w_rows, 16), w_rows)
            mine.append(pltpu.make_async_copy(piece, gu_own.at[k, at], local_sem.at[1 + k]))
    for copy in mine:
        copy.start()
    gains_buf[me] = gains[...]
    for i in range(1, n):
        gain_copy(i, me, line.other(i)).wait_recv()
    gain_a[...] = jnp.concatenate([gains_buf[i, 0:1, :] for i in range(n)], 1)
    gain_m[...] = jnp.concatenate([gains_buf[i, 1:2, :] for i in range(n)], 1)

    def norm(at):
        resid = tok[at, :].astype(F32)
        inverse = lax.rsqrt(jnp.mean(resid * resid, -1, keepdims=True) + EPSILON)
        own[at, :] = (resid * inverse * gain_a[...]).astype(BF16)

    row_chunks(rows, norm)
    gather = Gather(line, own, normed, ag_scratch)
    gather.start()
    spread_weights(0)
    for at in range(0, ids.shape[1], QBLK):
        ids_col[at : at + QBLK, :] = ids[:, at : at + QBLK].T
    order_group(long_len, ids, ids_col, rank_row, rank_col, seg_row_out, seg_col_out, pos_out, key_col, acc)
    for i in range(1, n):
        for k in range(2):
            qkv_copy(k, i, me, line.other(i)).wait_recv()
    for copy in mine[:2]:
        copy.wait()

    def share(i, to, slot):
        return remote(w_all.at[:, slot], w_all.at[:, slot], r_send.at[i], r_recv.at[slot], (to, me))

    for i in range(1, reps):
        share(i, lax.rem(rep + i, reps), rep).start()
    lanes = lax.broadcasted_iota(jnp.int32, (1, 128), 1)
    freq = frequencies(lax.rem(lanes, HD // 2))
    sign = jnp.where(lax.rem(lanes, HD) < HD // 2, -1.0, 1.0)

    def table(at):
        angles = ids_col[at, 1:2] * freq
        cos[at, :] = jnp.cos(angles)
        sin[at, :] = jnp.sin(angles) * sign

    row_chunks(ids_col.shape[0], table)
    gather.arrive(1)
    spread_weights(1)
    angles = frequencies(lax.broadcasted_iota(jnp.int32, (HD // 2, 1), 0)) * pos_out[...]
    cos_back[...] = jnp.cos(angles)
    sin_back[...] = jnp.sin(angles)
    for i in range(1, reps):
        share(i, rep, lax.rem(rep + i, reps)).wait_recv()
    load(w_all, wv, load_sem)
    cols = wv.shape[-1]
    lane = lax.broadcasted_iota(jnp.int32, (2 * rows, 128), 1)
    front = lax.rem(lane, HD) < HD // 2

    def project(j):
        z = gather.ready(j)
        load(normed.at[pl.ds(2 * z, 2)], blk, load_sem)
        at = rows_of(z, rows)
        raw = dot(blk[...].reshape(2 * rows, width), wv[...].reshape(width, cols))
        for t in range(0, cols, 128):
            part = raw[:, t : t + 128]
            cos_t, sin_t = cos[at, :], sin[at, :]
            if t == cols - 128:
                cos_t, sin_t = jnp.where(lane < HD, cos_t, 1.0), jnp.where(lane < HD, sin_t, 0.0)
            partner = jnp.where(front, pltpu.roll(part, 128 - HD // 2, 1), pltpu.roll(part, HD // 2, 1))
            qkv[at, t : t + 128] = (part * cos_t + partner * sin_t).astype(BF16)

    project(0)
    gather.arrive(2)
    spread_weights(2)

    is_end = (line.z == 0) | (line.z == line.chips - 1)

    @pl.loop(1, line.chips)
    def _(j):
        @pl.when(j + 2 < line.chips)
        def _():
            gather.arrive(j + 2)

        @pl.when(is_end & (j == max(1, line.chips - 3)))
        def _():
            spread_weights(3)

        project(j)

    @pl.when(~is_end)
    def _():
        spread_weights(3)

    attention_kernel(
        heads, long_len, qkv, rank_row, rank_col, seg_row_out, seg_col_out, q_out, kv_out, lse, att_t, att, s_buf, v_t
    )
    for i in range(1, n):
        gain_copy(i, line.other(i), me).wait_send()
        for k in range(2):
            qkv_copy(k, i, line.other(i), me).wait_send()
    for i in range(1, reps):
        share(i, lax.rem(rep + i, reps), rep).wait_send()
    if spread:
        for k in range(2):
            mine[2 + k].wait()
            for i in range(1, n):
                gu_copy(k, line.other(i), me).wait_send()
                gu_copy(k, me, line.other(i)).wait_recv()
    gather.finish()


def start_layer(n, reps, spread, heads, long_len, tok, gain_a, gain_m, seg, pos, wk, wv, wq, wg, wu):
    rows, width = tok.shape
    w_rows = wq.shape[0]
    cols = heads * HD + 2 * HD
    group = seg.shape[0]
    n_blocks = group // QBLK
    fb = wg.shape[1] // n // reps
    return pl.pallas_call(
        functools.partial(start_kernel, n, reps, spread, heads, long_len),
        name="start_layer",
        out_shape=(
            jax.ShapeDtypeStruct((n_blocks, heads * QBLK, HD), BF16),
            jax.ShapeDtypeStruct((2, group, HD), BF16),
            jax.ShapeDtypeStruct((n_blocks, 1, heads * QBLK), F32),
            jax.ShapeDtypeStruct((heads * HD, group), F32),
            jax.ShapeDtypeStruct((group, heads * HD), BF16),
            jax.ShapeDtypeStruct((1, group), jnp.int32),
            jax.ShapeDtypeStruct((group, 1), jnp.int32),
            jax.ShapeDtypeStruct((1, group), jnp.int32),
            jax.ShapeDtypeStruct((group, 1), jnp.int32),
            jax.ShapeDtypeStruct((HD // 2, group), F32),
            jax.ShapeDtypeStruct((HD // 2, group), F32),
            jax.ShapeDtypeStruct((1, width), F32),
            jax.ShapeDtypeStruct((1, width), F32),
            jax.ShapeDtypeStruct((n, rows, width), BF16),
            jax.ShapeDtypeStruct((n, reps, w_rows // reps, cols), BF16),
            jax.ShapeDtypeStruct((2, width, fb), BF16),
        ),
        in_specs=[VMEM] * 7 + [ANY] * 3,
        out_specs=(VMEM,) * 13 + (ANY,) * 3,
        scratch_shapes=[
            pltpu.VMEM((8, w_rows), F32),
            pltpu.VMEM((8, group), F32),
            pltpu.VMEM((n, w_rows, 2 * HD), BF16),
            pltpu.VMEM((n, 8, w_rows), F32),
            pltpu.VMEM((rows, width), BF16),
            pltpu.VMEM((n, reps, w_rows // reps, cols), BF16),
            pltpu.VMEM((2, rows, width), BF16),
            pltpu.VMEM((group, cols), BF16),
            pltpu.VMEM((group, 128), F32),
            pltpu.VMEM((group, 128), F32),
            pltpu.VMEM((group, 8), F32),
            pltpu.VMEM((group, 1), F32),
            pltpu.VMEM((8, group), F32),
            pltpu.VMEM((1, group), F32),
            pltpu.VMEM((long_len // QBLK, QBLK, heads * QBLK), F32),
            pltpu.VMEM((HD, group), BF16),
            DMA((n,)),
            DMA((n,)),
            DMA((2, n)),
            DMA((2, n)),
            DMA((reps,)),
            DMA((reps,)),
            DMA((2, n)),
            DMA((2, n)),
            DMA((4,)),
            DMA(()),
        ]
        + Gather.scratch(n),
        compiler_params=pltpu.CompilerParams(collective_id=4, has_side_effects=True, vmem_limit_bytes=VMEM_BYTES),
        cost_estimate=pl.CostEstimate(flops=2 * group * width * cols, bytes_accessed=300 * 2**20, transcendentals=0),
    )(tok, gain_a[None], gain_m[None], seg[None], pos[None], wk, wv, wq, wg, wu)


def weight_copies(gu, wbuf, w_sem):
    blocks, _, _, fb = gu.shape
    own = blocks * fb

    def copy(b, k):
        at = k * own + b * fb
        if not isinstance(at, int):
            at = pl.multiple_of(at, 128)
        return pltpu.make_async_copy(gu.at[b, k], wbuf.at[:, pl.ds(at, fb)], w_sem.at[k, b])

    return copy


def mlp_kernel(
    n, blocks, spread, att, wo, tok, gain, gu_in, cot, wd, normed, middle, hidden, grads, gu_out, cot_all, *scratch
):
    scatter_scratch, scratch = scratch[:8], scratch[8:]
    ag_scratch, cot_scratch, scratch = scratch[:3], scratch[3:6], scratch[6:]
    own_normed, blk, wbuf, wd_buf, grad_hid, hid_stage, grad_stage, w_sem, out_sem, load_sem, x_send, x_recv = scratch
    line = Line(n)
    rows, width = tok.shape
    fb = gu_in.shape[-1]
    own = blocks * fb
    rep = line.replica
    scatter = Scatter(line, scatter_scratch)
    cots = Gather(line, cot, cot_all, cot_scratch)
    gather = Gather(line, own_normed, normed, ag_scratch)
    wd_copy = pltpu.make_async_copy(wd, wd_buf, load_sem.at[1])
    wd_copy.start()
    line.enter(spread)
    cots.start(True)
    if spread:
        gu = gu_out

        def gu_copy(way, k, src, slot, device):
            return remote(src, gu.at[slot, k], x_send.at[way, k], x_recv.at[way, k], (device, line.me))

        firsts = [(0, 0, line.xn), (1, 1, line.yn), (0, 1, line.xn), (1, 0, line.yn)]
        for way, k, device in firsts[:2]:
            gu_copy(way, k, gu_in.at[k], rep, device).start()
        for k in range(2):
            pltpu.make_async_copy(gu_in.at[k], wbuf.at[:, pl.ds(pl.multiple_of(k * own + rep * fb, 128), fb)], w_sem.at[k, rep]).start()
            pltpu.make_async_copy(gu_in.at[k], gu.at[rep, k], load_sem.at[2 + k]).start()
    else:
        gu = gu_in
    weight_copy = weight_copies(gu, wbuf, w_sem)
    if not spread:
        for b in range(blocks):
            for k in range(2):
                weight_copy(b, k).start()

    def out_part(d):
        x = att[rows_of(d, rows), :]
        for t in range(0, width, 512):
            part = dot(x, wo[:, t : t + 512]).astype(BF16)
            scatter.part[rows_of(d, rows), t : t + 512] = part

    scatter.produce(out_part, cots.start_ends)
    wd_copy.wait()

    def grad_hidden(j):
        z = cots.ready(j)
        load(cot_all.at[pl.ds(2 * z, 2)], blk, load_sem.at[0])
        x = blk[...].reshape(2 * rows, width)
        tile = min(256, own)
        for t in range(0, own, tile):
            grad_hid[rows_of(z, rows), t : t + tile] = dot_t(x, wd_buf[t : t + tile, :]).astype(BF16)

    cots.arrive(1, (True,))
    if spread:
        for way, k, device in firsts[2:]:
            gu_copy(way, k, gu_in.at[k], rep, device).start()
    scatter.duty(0)
    cots.arrive(1, (False,))
    grad_hidden(0)
    if spread:
        for way, k, slot, device in ((0, 0, line.xn, line.yn), (1, 1, line.yn, line.xn)):
            gu_copy(way, k, gu.at[slot, k], slot, device).wait_recv()
            gu_copy(2 + way, k, gu.at[slot, k], slot, device).start()
            weight_copy(slot, k).start()

    @pl.loop(1, line.chips - 2)
    def _(s):
        scatter.duty(s)
        cots.arrive(s + 1)
        grad_hidden(s)

    scatter.duty(line.chips - 2)
    scatter.own_sum()

    def norm(at):
        mid = tok[at, :].astype(F32) + scatter.total[at, :]
        middle[at, :] = mid
        inverse = lax.rsqrt(jnp.mean(mid * mid, -1, keepdims=True) + EPSILON)
        own_normed[at, :] = (mid * inverse * gain[...]).astype(BF16)

    row_chunks(rows, norm)
    gather.start()
    cots.arrive(line.chips - 1)
    grad_hidden(line.chips - 2)
    grad_hidden(line.chips - 1)
    if spread:
        for way, k, slot in ((0, 1, line.xn), (1, 0, line.yn)):
            gu_copy(way, k, gu.at[slot, k], slot, line.xn).wait_recv()
            weight_copy(slot, k).start()
        for way, k, device in ((2, 0, line.yn), (3, 1, line.xn)):
            gu_copy(way, k, gu.at[line.diag, k], line.diag, device).wait_recv()
            weight_copy(line.diag, k).start()
    for b in range(blocks):
        for k in range(2):
            weight_copy(b, k).wait()

    def out_copies(z):
        at = rows_of(z, rows)
        return (
            pltpu.make_async_copy(hid_stage, hidden.at[at], out_sem.at[0]),
            pltpu.make_async_copy(grad_stage, grads.at[at], out_sem.at[1]),
        )

    @pl.loop(0, line.chips)
    def _(j):
        @pl.when(j > 0)
        def _():
            gather.arrive(j)

        z = gather.ready(j)
        load(normed.at[pl.ds(2 * z, 2)], blk, load_sem.at[0])

        @pl.when(j > 0)
        def _():
            for copy in out_copies(line.near_first(j - 1)):
                copy.wait()

        at = rows_of(z, rows)
        x = blk[...].reshape(2 * rows, width)
        tile = min(256, own)
        for t in range(0, own, tile):
            gate = dot(x, wbuf[:, t : t + tile])
            up = dot(x, wbuf[:, own + t : own + t + tile])
            sig = 1.0 / (1.0 + jnp.exp(-gate))
            gated = gate * sig
            gh = grad_hid[at, t : t + tile].astype(F32)
            hid_stage[:, t : t + tile] = (gated * up).astype(BF16)
            grad_stage[:, t : t + tile] = (gh * up * sig * (1.0 + gate * (1.0 - sig))).astype(BF16)
            grad_stage[:, own + t : own + t + tile] = (gh * gated).astype(BF16)
        for copy in out_copies(z):
            copy.start()

    for copy in out_copies(line.near_first(line.chips - 1)):
        copy.wait()
    if spread:
        for k in range(2):
            pltpu.make_async_copy(gu_in.at[k], gu.at[rep, k], load_sem.at[2 + k]).wait()
        for way, k, device in firsts:
            gu_copy(way, k, gu_in.at[k], rep, device).wait_send()
        for way, k, slot, device in ((2, 0, line.xn, line.yn), (3, 1, line.yn, line.xn)):
            gu_copy(way, k, gu.at[slot, k], slot, device).wait_send()
    scatter.finish()
    cots.finish()
    gather.finish()


def mlp_forward(n, reps, spread, att, wo, tok, gain, gu, cot, wd):
    rows, width = tok.shape
    group = att.shape[0]
    fb = gu.shape[-1]
    blocks = reps if spread else gu.shape[0]
    own = blocks * fb
    kept = (blocks, 2, width, fb) if spread else (1, 16, 128)
    return pl.pallas_call(
        functools.partial(mlp_kernel, n, blocks, spread),
        name="mlp_forward",
        out_shape=(
            jax.ShapeDtypeStruct((n, rows, width), BF16),
            jax.ShapeDtypeStruct((rows, width), F32),
            jax.ShapeDtypeStruct((group, own), BF16),
            jax.ShapeDtypeStruct((group, 2 * own), BF16),
            jax.ShapeDtypeStruct(kept, BF16),
            jax.ShapeDtypeStruct((n, rows, width), BF16),
        ),
        in_specs=[VMEM, VMEM, VMEM, VMEM, ANY, VMEM, ANY],
        out_specs=(ANY, VMEM, ANY, ANY, ANY, ANY),
        scratch_shapes=Scatter.scratch(n, rows, width)
        + Gather.scratch(n)
        + Gather.scratch(n)
        + [
            pltpu.VMEM((rows, width), BF16),
            pltpu.VMEM((2, rows, width), BF16),
            pltpu.VMEM((width, 2 * own), BF16),
            pltpu.VMEM((own, width), BF16),
            pltpu.VMEM((group, own), BF16),
            pltpu.VMEM((2 * rows, own), BF16),
            pltpu.VMEM((2 * rows, 2 * own), BF16),
            DMA((2, blocks)),
            DMA((2,)),
            DMA((4,)),
            DMA((4, 2)),
            DMA((4, 2)),
        ],
        compiler_params=pltpu.CompilerParams(collective_id=1, has_side_effects=True, vmem_limit_bytes=VMEM_BYTES),
        cost_estimate=pl.CostEstimate(flops=2 * group * width * own * 3, bytes_accessed=400 * 2**20, transcendentals=0),
    )(att, wo, tok, gain, gu, cot, wd)


def norm_back(grad_normed, resid, gain):
    inverse = lax.rsqrt(jnp.mean(resid * resid, -1, keepdims=True) + EPSILON)
    unit = resid * inverse
    scaled = grad_normed * gain
    return inverse * (scaled - unit * jnp.mean(scaled * unit, -1, keepdims=True)), grad_normed * unit


def middle_kernel(
    n, blocks, spread, grads_in, gu, mid_in, cot_in, gain, wo_in, normed, hidden, cot_all, wd,
    grad_mid, gml, grad_att, gain_sum, output,
    gate_parts, up_parts, down_parts, gate_q, up_q, down_q, down_out, *scratch,
):
    scatter_scratch, ag_scratch, scratch = scratch[:8], scratch[8:11], scratch[11:]
    mid, cot, wo, late_sem, *scratch = scratch
    late = [pltpu.make_async_copy(src, dst, late_sem.at[i]) for i, (src, dst) in enumerate(zip((mid_in, cot_in, wo_in), (mid, cot, wo)))]
    grads, own_low, blk, wbuf, w_sem, load_sem = scratch[:6]
    line = Line(n)
    rows, width = mid.shape
    group = grads.shape[0]
    fb = gu.shape[-1]
    own = blocks * fb
    scatter = Scatter(line, scatter_scratch)
    gather = Gather(line, own_low, gml, ag_scratch)
    grads_copy = pltpu.make_async_copy(grads_in, grads, load_sem)
    weight_copy = weight_copies(gu, wbuf, w_sem)

    def start_loads():
        grads_copy.start()
        for b in range(blocks):
            for k in range(2):
                weight_copy(b, k).start()
        for copy in late:
            copy.start()

    if not spread:
        start_loads()
    if not spread:
        line.enter(spread)

    def loaded():
        grads_copy.wait()
        for b in range(blocks):
            for k in range(2):
                weight_copy(b, k).wait()

    def normed_part(d):
        x = grads[rows_of(d, rows), :]
        for t in range(0, width, 512):
            part = dot_t(x, wbuf[t : t + 512, :]).astype(BF16)
            scatter.part[rows_of(d, rows), t : t + 512] = part

    if not spread:
        loaded()
        scatter.produce(normed_part)
    tiles = 4
    tile = width // tiles
    if spread:
        gate_land, up_land, down_land, gate_in, up_in, down_in, tmp, tmp_down, stage, part_sem, out_sem, hid_buf, tile_sem = scratch[6:19]
        half = fb // 2
        units = [
            dict(parts=gate_parts, row=0, rows=width, x_first=True, axis=0, land1=gate_land, land2=gate_in, tmp=tmp),
            dict(parts=up_parts, row=0, rows=width, x_first=False, axis=0, land1=up_land, land2=up_in, tmp=tmp),
        ]
        for i in range(2):
            units.append(
                dict(
                    parts=down_parts, row=i * half, rows=half, x_first=i == 0, axis=1,
                    land1=down_land.at[i], land2=down_in.at[i], tmp=tmp_down,
                )
            )
        square = Square(line, units, scratch[19:24])
        d_send, d_recv = scratch[24:26]
        rx, *sems = scratch[26:]
        output_sum = Scatter(line, (grads, scatter.sib, rx, scatter.total, *sems))
        slots = [hid_buf.at[:, pl.ds(own + i * tile, tile)] for i in range(2)]
        hid = hid_buf.at[:, pl.ds(0, own)]

        def column_copy(i):
            src = cot_all if i < tiles else normed
            return pltpu.make_async_copy(src.at[:, pl.ds(i % tiles * tile, tile)], slots[i % 2], tile_sem.at[i % 2])

        hid_copy = pltpu.make_async_copy(hidden, hid, tile_sem.at[2])
        hid_copy.start()
        column_copy(0).start()
        line.enter(spread)
        start_loads()

        def weight_tile(i):
            t = i % tiles
            column_copy(i).wait()
            if i + 1 < 2 * tiles:
                column_copy(i + 1).start()
            if i >= tiles:
                x = slots[i % 2][...]
                for k in range(2):
                    for b in range(blocks):
                        at = k * own + b * fb
                        stage[k, b] = tdot(x, grads[:, at : at + fb]).astype(BF16)
                copies = [
                    pltpu.make_async_copy(stage.at[k, b], parts.at[b, pl.ds(t * tile, tile)], part_sem.at[k, b])
                    for k, parts in enumerate((gate_parts, up_parts))
                    for b in range(blocks)
                ]
            else:
                if i == 0:
                    hid_copy.wait()
                x = slots[i % 2][...]
                for b in range(blocks):
                    part = tdot(hid[:, b * fb : (b + 1) * fb], x).astype(BF16)
                    for k in range(2):
                        stage[k, b, :fb, :] = part[:, k * fb : (k + 1) * fb]
                copies = [
                    pltpu.make_async_copy(
                        stage.at[k, b, pl.ds(0, fb)], down_parts.at[b, :, pl.ds(t * tile + k * fb, fb)], part_sem.at[k, b]
                    )
                    for k in range(2)
                    for b in range(blocks)
                ]
            for copy in copies:
                copy.start()
            for copy in copies:
                copy.wait()

        quarter = half // 2
        pieces = ((2, 0, quarter), (2, quarter, quarter), (3, 0, quarter // 2), (3, quarter // 2, quarter // 2))

        def place(i, replica):
            unit, row, count = pieces[i]
            at = replica * 3 * quarter + (unit - 2) * half + row
            return down_out.at[pl.ds(pl.multiple_of(at, 16), count)]

        def down_piece(i):
            unit, row, count = pieces[i]
            return units[unit]["land1"].at[0, pl.ds(row, count)]

        def down_send(way, i, src, replica, device):
            return remote(src, place(i, replica), d_send.at[way, i], d_recv.at[way, i], (device, line.me))

        def down_firsts(i):
            return [
                down_send(way, i, down_piece(i), line.replica, device) for way, device in enumerate((line.xn, line.yn))
            ]

        def down_second(i):
            replica, device = ((line.xn, line.yn), (line.yn, line.xn))[i % 2]
            return down_send(2 + i % 2, i, place(i, replica), replica, device)

        def down_local(i):
            return pltpu.make_async_copy(down_piece(i), place(i, line.replica), out_sem.at[3 + i])

        rest_copy = pltpu.make_async_copy(units[3]["land1"].at[0, pl.ds(quarter, quarter)], down_q, out_sem.at[2])

        def down_tile(i):
            if i < tiles:
                weight_tile(i)
                square.start(2, i)
                square.start(3, i)

        down_tile(0)
        loaded()
        scatter.produce(normed_part, None, lambda s: down_tile(s + 1))
        for i in range(line.chips + 1, tiles):
            down_tile(i)
        scatter.duty(0, (True,))
        for i in range(2):
            weight_tile(tiles + i)
            square.start(0, i)
            square.start(1, i)
        scatter.duty(0, (False,))
        square.fold(2)
        square.fold(3)
        scatter.duty(1)
        for i in range(2, 4):
            weight_tile(tiles + i)
            square.start(0, i)
            square.start(1, i)
        scatter.duty(2)
    else:
        for s in range(line.chips - 1):
            scatter.duty(s)
    scatter.own_sum()
    for copy in late:
        copy.wait()
    gain_sum[...] = jnp.zeros_like(gain_sum)

    def back(at):
        through, gain_term = norm_back(scatter.total[at, :], mid[at, :], gain[...])
        value = cot[at, :].astype(F32) + through
        grad_mid[at, :] = value
        own_low[at, :] = value.astype(BF16)
        gain_sum[...] += jnp.sum(gain_term, 0, keepdims=True)

    row_chunks(rows, back)
    gather.start()

    def attended_part(j, z=None):
        if z is None:
            z = gather.ready(j)
        load(gml.at[pl.ds(2 * z, 2)], blk, load_sem)
        grad_att[rows_of(z, rows), :] = dot_t(blk[...].reshape(2 * rows, width), wo[...]).astype(BF16)

    if spread:

        def down_copy(i):
            place = wbuf.at[pl.ds(0, own), pl.ds(i % 2 * tile, tile)]
            return pltpu.make_async_copy(wd.at[:, pl.ds(i * tile, tile)], place, w_sem.at[0, i % 2])

        down_copy(0).start()
        for i in range(tiles):
            down_copy(i).wait()
            if i + 1 < tiles:
                down_copy(i + 1).start()
            for d in range(line.chips):
                at = pl.ds(d * 2 * rows, 2 * rows)
                x = dot(hid[at, :], wbuf[:own, i % 2 * tile : (i % 2 + 1) * tile])
                grads[at, i * tile : (i + 1) * tile] = x.astype(BF16)
        here = gather.ready(0)
        output_sum.produce(lambda d: None)
        gather.arrive(1)
        attended_part(0, here)
        for u in (2, 3):
            square.result(u)
            for i in range(2 * u - 4, 2 * u - 2):
                for copy in down_firsts(i):
                    copy.start()
                down_local(i).start()
        rest_copy.start()
        square.fold(0)
        square.fold(1)
        gather.arrive(2)
        attended_part(1)
        output_sum.duty(0)
        gather.arrive(3)
        attended_part(2)
        attended_part(3)
        for i in range(4):
            replica = (line.xn, line.yn)[i % 2]
            down_send(i % 2, i, place(i, replica), replica, replica).wait_recv()
            down_second(i).start()
        output_sum.duty(1)
        output_sum.duty(2)
        copies = []
        for u, out in ((0, gate_q), (1, up_q)):
            square.result(u)
            copies.append(pltpu.make_async_copy(units[u]["land1"].at[0], out, out_sem.at[u]))
            copies[-1].start()
        output_sum.own_sum()

        def put(at):
            output[at, :] = (mid[at, :] + scatter.total[at, :]).astype(BF16)

        row_chunks(rows, put)
        output_sum.finish()
        rest_copy.wait()
        for i in range(4):
            for copy in down_firsts(i):
                copy.wait_send()
            down_second(i).wait_send()
            down_local(i).wait()
            replica, far = ((line.xn, line.yn), (line.yn, line.xn))[i % 2]
            down_send(2 + i % 2, i, place(i, line.diag), line.diag, replica).wait_recv()
            down_send(1 - i % 2, i, place(i, far), far, far).wait_recv()
        for copy in copies:
            copy.wait()
        square.finish()
    else:

        @pl.loop(0, line.chips)
        def _(j):
            @pl.when(j > 0)
            def _():
                gather.arrive(j)

            attended_part(j)

    scatter.finish()
    gather.finish()


def middle_backward(n, spread, grads, gu, mid, cot, gain, wo, normed, hidden, cot_all, wd):
    rows, width = mid.shape
    group = grads.shape[0]
    blocks, _, _, fb = gu.shape
    own = blocks * fb
    parts = [(4, width, fb), (4, width, fb), (4, fb, width), (width, fb), (width, fb), (fb // 4, width), (3 * fb, width)]
    if not spread:
        parts = [(16, 128)] * 7
    scratch = []
    if spread:
        scratch = [
            pltpu.VMEM((2, width, fb), BF16),
            pltpu.VMEM((2, width, fb), BF16),
            pltpu.VMEM((2, 2, fb // 2, width), BF16),
            pltpu.VMEM((width, fb), BF16),
            pltpu.VMEM((width, fb), BF16),
            pltpu.VMEM((2, fb // 2, width), BF16),
            pltpu.VMEM((width, fb), BF16),
            pltpu.VMEM((fb // 2, width), BF16),
            pltpu.VMEM((2, blocks, width // 4, fb), BF16),
            DMA((2, blocks)),
            DMA((7,)),
            pltpu.VMEM((group, own + width // 2), BF16),
            DMA((3,)),
        ] + Square.scratch(4, 4) + [DMA((4, 4)), DMA((4, 4))]
        again = Scatter.scratch(n, rows, width)
        scratch += again[2:3] + again[4:]
    return pl.pallas_call(
        functools.partial(middle_kernel, n, blocks, spread),
        name="middle_backward",
        out_shape=(
            jax.ShapeDtypeStruct((rows, width), F32),
            jax.ShapeDtypeStruct((n, rows, width), BF16),
            jax.ShapeDtypeStruct((group, wo.shape[0]), BF16),
            jax.ShapeDtypeStruct((1, width), F32),
            jax.ShapeDtypeStruct((rows, width) if spread else (16, 128), BF16),
            *[jax.ShapeDtypeStruct(shape, BF16) for shape in parts],
        ),
        in_specs=[ANY, ANY, ANY, ANY, VMEM, ANY, ANY, ANY, ANY, ANY],
        out_specs=(VMEM, ANY, VMEM, VMEM, VMEM) + (ANY,) * 7,
        scratch_shapes=Scatter.scratch(n, rows, width)
        + Gather.scratch(n)
        + [
            pltpu.VMEM(mid.shape, F32),
            pltpu.VMEM(cot.shape, BF16),
            pltpu.VMEM(wo.shape, BF16),
            DMA((3,)),
            pltpu.VMEM((group, 2 * own), BF16),
            pltpu.VMEM((rows, width), BF16),
            pltpu.VMEM((2, rows, width), BF16),
            pltpu.VMEM((width, 2 * own), BF16),
            DMA((2, blocks)),
            DMA(()),
        ]
        + scratch,
        compiler_params=pltpu.CompilerParams(collective_id=2, has_side_effects=True, vmem_limit_bytes=62 * 2**20),
        cost_estimate=pl.CostEstimate(flops=2 * group * width * own * 3, bytes_accessed=400 * 2**20, transcendentals=0),
    )(grads, gu, mid, cot, gain, wo, normed, hidden, cot_all, wd)


STAGED = 15


def end_kernel(
    n, reps, spread, heads, long_len, *refs,
):
    operands, refs = refs[:STAGED], refs[STAGED:]
    gain, gain_m_sum, gate_q, up_q, down_q, normed, gml, grad_tok, gain_grads, grads = refs[:10]
    gate_out, up_out, down_out, q_out, kv_out, out_out, *scratch = refs[10:]
    staged, stage_sem, scratch = scratch[:STAGED], scratch[STAGED], scratch[STAGED + 1 :]
    (
        q_in, kv, lse, att_t, grad_att, rank_row, rank_col, seg_row, seg_col, cos_t, sin_t, w, tok, grad_mid, attended,
    ) = staged
    stage_copies = [pltpu.make_async_copy(src, dst, stage_sem.at[i]) for i, (src, dst) in enumerate(zip(operands, staged))]
    for copy in stage_copies:
        copy.start()
    scatter_scratch, att_scratch, scratch = scratch[:8], scratch[8:13], scratch[13:]
    gain_sum, gain_src, gain_land, gain_all, g_send, g_recv = scratch[:6]
    line = Line(n)
    rows, width = tok.shape
    me, rep = line.me, line.replica
    scatter = Scatter(line, scatter_scratch)
    if spread:
        slots, slot_sem = scratch[19:21]
        fetches = [pltpu.make_async_copy(src, slots.at[i], slot_sem.at[i]) for i, src in enumerate((gml, normed))]
        for fetch in fetches:
            fetch.start()
    line.enter_all(reps)
    if spread:
        (
            a_send, a_recv, x_send, x_recv, local_sem, qkv_land, qkv_in, out_land, out_in, qkv_tmp, out_tmp,
            qkv_parts, out_parts, _, _,
        ) = scratch[6:21]
        fb = gate_q.shape[-1]
        own = 4 * fb
        quarters, outs = (gate_q, up_q), (gate_out, up_out)
        w_rows = gate_out.shape[0]
        down_rows = down_q.shape[0] // 2
        q_cols = heads * HD
        qkv_rows = w_rows // 4
        out_rows = out_parts.shape[1] // 2
        counts = (n, n, 2, n, 2, n)
        units = [
            dict(
                parts=qkv_parts, row=i * 4 * qkv_rows, rows=4 * qkv_rows, x_first=i == 0,
                land1=qkv_land.at[i], land2=qkv_in.at[i], tmp=qkv_tmp,
            )
            for i in range(2)
        ] + [
            dict(
                parts=out_parts, row=i * out_rows, rows=out_rows, x_first=i == 0,
                land1=out_land.at[i], land2=out_in.at[i], tmp=out_tmp,
            )
            for i in range(2)
        ]
        square = Square(line, units, scratch[21:])

        def place(k, f, replica):
            if k == 2:
                return down_out.at[pl.ds(pl.multiple_of(replica * 2 * down_rows + f * down_rows, 16), down_rows)]
            if k in (3, 5):
                at = pl.ds(pl.multiple_of(replica * qkv_rows, 16), qkv_rows)
                if k == 3:
                    return q_out.at[at, pl.ds(pl.multiple_of(f * q_cols, 128), q_cols)]
                return kv_out.at[at, pl.ds(pl.multiple_of(f * 2 * HD, 128), 2 * HD)]
            if k == 4:
                return out_out.at[pl.ds(pl.multiple_of(replica * 2 * out_rows + f * out_rows, 16), out_rows)]
            return outs[k].at[:, pl.ds(pl.multiple_of(f * own + replica * fb, 128), fb)]

        def block(k, f):
            if k in (3, 5):
                half, inner = lax.div(f, 4), lax.rem(f, 4)
                cols = pl.ds(0, q_cols) if k == 3 else pl.ds(q_cols, 2 * HD)
                return qkv_land.at[half, 0, pl.ds(pl.multiple_of(inner * qkv_rows, 16), qkv_rows), cols]
            return quarters[k].at[pl.ds(pl.multiple_of(f * w_rows, 16), w_rows)]

        def exchange(k, to, at):
            return remote(block(k, to), place(k, at, rep), a_send.at[k, to], a_recv.at[k, at], (rep, to))

        def exchange_at(d, kinds):
            if d == 0:
                for k in kinds:
                    exchange(k, 2 * line.z + 1 - line.c, me).start()
                return
            for to in (line.z + d, line.z - d):

                @pl.when((to >= 0) & (to < line.chips))
                def _():
                    for core in range(2):
                        for k in kinds:
                            exchange(k, 2 * to + core, me).start()

        def send(way, k, f, src, replica, device):
            return remote(src, place(k, f, replica), x_send.at[way, k, f], x_recv.at[way, k, f], (device, me))

        def share(k, f, src):
            send(0, k, f, src, rep, line.xn).start()
            send(1, k, f, src, rep, line.yn).start()

        def corner(core):
            return (0, line.xn, line.yn) if core % 2 == 0 else (1, line.yn, line.xn)

        def forward_all(z, kinds):
            for k in kinds:
                for core in range(2):
                    forward(k, 2 * z + core, core)

        def forward(k, f, core):
            way, replica, device = corner(core)
            src = place(k, f, replica)
            send(way, k, f, src, replica, replica).wait_recv()
            send(2 + way, k, f, src, replica, device).start()

        def local(i, src, dst):
            return pltpu.make_async_copy(src, dst, local_sem.at[i])

        def mine(k):
            return local(k, block(k, me), place(k, me, rep))

        def down_piece(i):
            return down_q.at[pl.ds(i * down_rows, down_rows)]

        def mine_down(i):
            return local((2, 4)[i], down_piece(i), place(2, i, rep))

        def mine_out(i):
            return local(6 + i, out_land.at[i, 0], place(4, i, rep))

        def stream(i, use):
            fetches[i].wait()
            for t in range(0, width, 512):
                use(t, slots[i, :, t : t + 512])

        def out_tile(at, x):
            part = tdot(attended[...], x).astype(BF16)
            for b in range(4):
                out_parts[b, :, at : at + x.shape[1]] = part[b * 2 * out_rows : (b + 1) * 2 * out_rows]

        def qkv_tile(at, x):
            part = tdot(x, grads[...]).astype(BF16)
            for i in range(x.shape[1] // w_rows):
                f = at // w_rows + i
                for b in range(4):
                    piece = part[i * w_rows + b * qkv_rows : i * w_rows + (b + 1) * qkv_rows]
                    qkv_parts[b, f * qkv_rows : (f + 1) * qkv_rows, :] = piece

        for k in range(2):
            share(k, me, block(k, me))
            mine(k).start()
        for i in range(2):
            share(2, i, down_piece(i))
            mine_down(i).start()
        exchange_at(0, (0, 1))
        exchange_at(1, (0, 1))
        for copy in stage_copies:
            copy.wait()
        stream(0, out_tile)
        square.start(2)
        square.start(3)

    def pass_on(z, kinds):
        for core in range(2):
            f = 2 * z + core

            @pl.when(f != me)
            def _():
                for k in kinds:
                    exchange(k, me, f).wait_recv()
                    share(k, f, place(k, f, rep))

    if not spread:
        for copy in stage_copies:
            copy.wait()

    def after_block(b):
        if not spread:
            return
        if b == 0:
            pass_on(line.near_first(0), (0, 1))
            exchange_at(2, (0, 1))
        if b == 2:
            for d in range(3, line.chips):
                exchange_at(d, (0, 1))

    attention_back_kernel(
        heads, long_len, q_in, kv, lse, att_t, grad_att, rank_row, rank_col, seg_row, seg_col, cos_t, sin_t, grads,
        *att_scratch, after_block,
    )
    if spread:
        stream(1, qkv_tile)
        square.start(0)
        square.start(1)
        pass_on(line.near_first(1), (0, 1))

    def normed_part(d):
        x = grads[rows_of(d, rows), :]
        for t in range(0, width, 512):
            part = dot_t(x, w[t : t + 512, :]).astype(BF16)
            scatter.part[rows_of(d, rows), t : t + 512] = part

    scatter.produce(normed_part, hold_last=spread)
    if spread:
        for u in range(4):
            square.fold(u)
        for i in range(2):
            forward(2, i, i)
        forward_all(line.near_first(0), (0, 1))
        square.result(0)
        square.result(1)
        for d in range(line.chips):
            exchange_at(d, (3, 5))
        for k in (3, 5):
            share(k, me, block(k, me))
            mine(k).start()
        scatter.emit_last()
        square.result(2)
        square.result(3)
        for i in range(2):
            share(4, i, out_land.at[i, 0])
            mine_out(i).start()
        pass_on(line.near_first(2), (0, 1))
        forward_all(line.near_first(1), (0, 1))
    for s in range(line.chips - 1):
        scatter.duty(s)
        if spread:
            if s == 0:
                pass_on(line.near_first(3), (0, 1))
            if s == 1:
                forward_all(line.near_first(2), (0, 1))
                for i in range(2):
                    forward(4, i, i)
            if s == 2:
                forward_all(line.near_first(3), (0, 1))
    scatter.own_sum()
    gain_sum[...] = jnp.zeros_like(gain_sum)

    def back(at):
        through, gain_term = norm_back(scatter.total[at, :], tok[at, :].astype(F32), gain[...])
        grad_tok[at, :] = grad_mid[at, :] + through
        gain_sum[...] += jnp.sum(gain_term, 0, keepdims=True)

    row_chunks(rows, back)

    g_rows = gain_grads.shape[1]
    gain_src[...] = jnp.zeros_like(gain_src)
    for f in range(n):
        gain_src[f, 0:1, :] = gain_sum[:, f * g_rows : (f + 1) * g_rows]
        gain_src[f, 1:2, :] = gain_m_sum[:, f * g_rows : (f + 1) * g_rows]

    def gain_copy(i, to, slot):
        return remote(gain_src.at[to], gain_land.at[slot], g_send.at[0, i], g_recv.at[0, slot], (rep, to))

    def gain_share(i, to, slot):
        return remote(gain_all.at[slot], gain_all.at[slot], g_send.at[1, i], g_recv.at[1, slot], (to, me))

    for i in range(1, n):
        gain_copy(i, line.other(i), me).start()
    gain_land[me] = gain_src[me]
    if spread:
        for j in range(line.chips):
            pass_on(line.near_first(j), (3, 5))
    for i in range(1, n):
        gain_copy(i, me, line.other(i)).wait_recv()
    gain_all[rep] = functools.reduce(lambda a, b: a + b, [gain_land[i] for i in range(n)])
    for i in range(1, reps):
        gain_share(i, lax.rem(rep + i, reps), rep).start()
    if spread:
        for j in range(line.chips):
            forward_all(line.near_first(j), (3, 5))
    for i in range(1, reps):
        gain_share(i, rep, lax.rem(rep + i, reps)).wait_recv()
    gain_grads[...] = functools.reduce(lambda a, b: a + b, [gain_all[i] for i in range(reps)])
    for i in range(1, n):
        gain_copy(i, line.other(i), me).wait_send()
    for i in range(1, reps):
        gain_share(i, lax.rem(rep + i, reps), rep).wait_send()
    if spread:
        for k in (0, 1, 3, 5):
            mine(k).wait()
        for i in range(2):
            mine_out(i).wait()
            mine_down(i).wait()
        for k in (0, 1, 3, 5):
            for i in range(1, n):
                exchange(k, line.other(i), me).wait_send()
        for k in range(6):
            for f in range(counts[k]):
                src = place(k, f, rep)
                send(0, k, f, src, rep, line.xn).wait_send()
                send(1, k, f, src, rep, line.yn).wait_send()
                way, replica, device = corner(f)
                send(2 + way, k, f, src, replica, device).wait_send()
                send(2 + way, k, f, src, line.diag, replica).wait_recv()
                far = (line.yn, line.xn)[way]
                send(1 - way, k, f, src, far, far).wait_recv()
        square.finish()
    scatter.finish()


def end_layer(
    n, reps, spread, heads, long_len, q_in, kv, lse, att_t, grad_att, ranks, cos_t, sin_t,
    w, tok, grad_mid, gain, gain_m_sum, attended, gate_q, up_q, down_q, normed, gml,
):
    rows, width = tok.shape
    group = attended.shape[0]
    n_blocks = group // QBLK
    cols = w.shape[1]
    w_rows = width // n
    shapes, scratch = [(16, 128)] * 6, []
    if spread:
        fb = gate_q.shape[-1]
        own = 4 * fb
        heads_rows = attended.shape[1] // 4
        q_rows = w_rows // 4
        shapes = [(w_rows, n * own)] * 2 + [(fb, width), (w_rows, n * heads * HD), (w_rows, n * 2 * HD), (4 * heads_rows, width)]
        scratch = [
            DMA((6, n)),
            DMA((6, n)),
            DMA((4, 6, n)),
            DMA((4, 6, n)),
            DMA((8,)),
            pltpu.VMEM((2, 2, 4 * q_rows, cols), BF16),
            pltpu.VMEM((2, 4 * q_rows, cols), BF16),
            pltpu.VMEM((2, 2, heads_rows // 2, width), BF16),
            pltpu.VMEM((2, heads_rows // 2, width), BF16),
            pltpu.VMEM((4 * q_rows, cols), BF16),
            pltpu.VMEM((heads_rows // 2, width), BF16),
            pltpu.VMEM((4, width // 4, cols), BF16),
            pltpu.VMEM((4, heads_rows, width), BF16),
            pltpu.VMEM((2, group, width), BF16),
            DMA((2,)),
        ] + Square.scratch(4, 1)
    operands = [q_in, kv, lse, att_t, grad_att, *ranks, cos_t, sin_t, w, tok, grad_mid, attended]
    return pl.pallas_call(
        functools.partial(end_kernel, n, reps, spread, heads, long_len),
        name="end_layer",
        out_shape=(
            jax.ShapeDtypeStruct((rows, width), F32),
            jax.ShapeDtypeStruct((8, w_rows), F32),
            jax.ShapeDtypeStruct((group, cols), BF16),
            *[jax.ShapeDtypeStruct(shape, BF16) for shape in shapes],
        ),
        in_specs=[ANY] * STAGED + [VMEM] * 2 + [ANY] * 5,
        out_specs=(VMEM, VMEM, VMEM) + (ANY,) * 6,
        scratch_shapes=[pltpu.VMEM(x.shape, x.dtype) for x in operands]
        + [DMA((STAGED,))]
        + Scatter.scratch(n, rows, width)
        + [
            pltpu.VMEM((2, group, HD), F32),
            pltpu.VMEM((cols, group), BF16),
            pltpu.VMEM((HD, group), BF16),
            pltpu.VMEM((n_blocks, heads * QBLK, HD), BF16),
            pltpu.VMEM((heads * HD, group), F32),
            pltpu.VMEM((1, width), F32),
            pltpu.VMEM((n, 8, w_rows), F32),
            pltpu.VMEM((n, 8, w_rows), F32),
            pltpu.VMEM((reps, 8, w_rows), F32),
            DMA((2, max(n, reps))),
            DMA((2, max(n, reps))),
        ]
        + scratch,
        compiler_params=pltpu.CompilerParams(collective_id=3, has_side_effects=True, vmem_limit_bytes=VMEM_BYTES),
        cost_estimate=pl.CostEstimate(flops=2 * group * width * cols, bytes_accessed=400 * 2**20, transcendentals=0),
    )(
        *operands, gain, gain_m_sum, gate_q, up_q, down_q, normed, gml,
    )


def body(
    tokens, segment, position, attn_gain, w_query, w_key, w_value, w_out, mlp_gain, w_gate, w_up, w_down, cotangent
):
    rows, width = tokens.shape
    group = segment.shape[0]
    long_len = group * 2 // 3
    n = lax.axis_size("fsdp")
    reps = lax.axis_size("replica")
    w_rows = w_query.shape[0]
    ff_own = w_gate.shape[1] // n
    ff_blk = ff_own // reps
    heads = H // n
    q_cols = heads * HD
    dup = n // KVH
    spread = reps == 4 and ff_blk % 128 == 0

    def swap(x):
        return lax.all_to_all(x, "fsdp", 0, 0, tiled=True)

    (
        q_in, kv, lse, att_t, attended, *ranks, cos_back, sin_back, gain_a, gain_m, normed_all, qkv_w, gu_own,
    ) = start_layer(
        n, reps, spread, heads, long_len, tokens, attn_gain, mlp_gain, segment, position, w_key, w_value, w_query, w_gate,
        w_up,
    )
    normed_all = normed_all.reshape(group, width)
    qkv_w = qkv_w.reshape(width, q_cols + 2 * HD)
    if not spread:
        gate_up = jnp.stack([w.reshape(w_rows, n, ff_own).transpose(1, 0, 2) for w in (w_gate, w_up)], 1)
        gu_own = swap(gate_up).transpose(1, 0, 2, 3).reshape(1, 2, width, ff_own)
    normed_mlp, middle, hidden, grads, gate_up, cot_all = mlp_forward(
        n, reps, spread, attended, w_out, tokens, gain_m, gu_own, cotangent, w_down
    )
    normed_mlp, cot_all = normed_mlp.reshape(group, width), cot_all.reshape(group, width)
    if not spread:
        gate_up = gu_own

    def over_replicas(x):
        return lax.psum_scatter(x, "replica", scatter_dimension=0, tiled=True)

    grad_mid, gml, grad_att, gain_m_sum, output, _, _, _, gate_q, up_q, down_q, down_first = middle_backward(
        n, spread, grads, gate_up, middle, cotangent, gain_m, w_out, normed_mlp, hidden, cot_all, w_down
    )
    gml = gml.reshape(group, width)
    if not spread:

        def column_blocks(first):
            grad = tdot(normed_mlp, grads[:, first : first + ff_own]).astype(BF16)
            return grad.reshape(width, reps, ff_blk).transpose(1, 0, 2).reshape(reps * width, ff_blk)

        gate_q, up_q = over_replicas(column_blocks(0)), over_replicas(column_blocks(ff_own))
        down_q = over_replicas(tdot(hidden, cot_all).astype(BF16))
        down = lax.psum_scatter(dot(hidden, w_down).astype(BF16), "fsdp", scatter_dimension=0, tiled=True)
        output = (middle + down.astype(F32)).astype(BF16)
    grad_tokens, gain_grads, grad_qkv, grad_gate, grad_up, down_second, grad_w_query, grad_kv, grad_out_w = end_layer(
        n, reps, spread, heads, long_len, q_in, kv, lse, att_t, grad_att, ranks, cos_back, sin_back,
        qkv_w, tokens, grad_mid, gain_a, gain_m_sum, attended, gate_q, up_q, down_q, normed_all, gml,
    )
    if spread:
        parts = [x.reshape(reps, -1, width) for x in (down_first, down_second)]
        grad_down = jnp.concatenate(parts, 1).reshape(ff_own, width)
    else:

        def by_rows(grad):
            grad = swap(grad.reshape(n, w_rows, -1))
            grad = lax.all_gather(grad, "replica", axis=0, tiled=False)
            return grad.transpose(2, 1, 0, 3).reshape(w_rows, -1)

        grad_gate, grad_up = by_rows(gate_q), by_rows(up_q)
        grad_down = lax.all_gather(down_q, "replica", axis=0, tiled=True)
        grad_w = tdot(normed_all, grad_qkv).astype(BF16)
        grad_w = grad_w.reshape(n, reps, w_rows // reps, -1).transpose(1, 0, 2, 3)
        grad_w = over_replicas(grad_w)[0]
        grad_w = lax.all_gather(swap(grad_w), "replica", axis=0, tiled=False)
        grad_w = grad_w.transpose(0, 2, 1, 3).reshape(w_rows, n, -1)
        grad_w_query, grad_kv = grad_w[:, :, :q_cols].reshape(w_rows, H * HD), grad_w[:, :, q_cols:]
        grad_out_w = lax.psum(tdot(attended, gml).astype(BF16), "replica")
    grad_kv = grad_kv.reshape(w_rows, KVH, dup, 2 * HD).astype(F32).sum(2)
    grad_w_key = grad_kv[:, :, :HD].reshape(w_rows, KVH * HD)
    grad_w_value = grad_kv[:, :, HD:].reshape(w_rows, KVH * HD)
    return (
        output,
        grad_tokens,
        gain_grads[0],
        grad_w_query.astype(F32),
        grad_w_key,
        grad_w_value,
        grad_out_w.astype(F32),
        gain_grads[1],
        grad_gate.astype(F32),
        grad_up.astype(F32),
        grad_down.astype(F32),
    )


def solution(mesh):
    both = P(("replica", "fsdp"), None)
    mat = P("fsdp", None)
    vec = P("fsdp")
    return jax.shard_map(
        body,
        mesh=mesh,
        in_specs=(both, P("replica"), P("replica"), vec, mat, mat, mat, mat, vec, mat, mat, mat, both),
        out_specs=(both, both, vec, mat, mat, mat, mat, vec, mat, mat, mat),
        check_vma=False,
    )
```
